32 devices in a mesh: batch: 4 (over y, x), seq: 8 (over z, core).
Axes of the slice: x: 2, y: 2, z: 4, core: 2. Of those that a mesh axis runs over, the one named last changes fastest.
Arguments:
- tokens: bfloat16 [32, 2048, 576], P('batch', 'seq'), may hold values from -6 to 6
- lengths: int32 [32], P('batch'), may hold values from 512 to 2048, as said below
- gain_attn: float32 [576], replicated, may hold values from 0.5 to 1.5
- w_query: bfloat16 [576, 576], replicated, may hold values from -0.25 to 0.25
- w_key: bfloat16 [576, 192], replicated, may hold values from -0.25 to 0.25
- w_value: bfloat16 [576, 192], replicated, may hold values from -0.25 to 0.25
- w_out: bfloat16 [576, 576], replicated, may hold values from -3 to 3
- gain_mlp: float32 [576], replicated, may hold values from 0.5 to 1.5
- w_gate: bfloat16 [576, 1536], replicated, may hold values from -0.25 to 0.25
- w_up: bfloat16 [576, 1536], replicated, may hold values from -0.25 to 0.25
- w_down: bfloat16 [1536, 576], replicated, may hold values from -0.15625 to 0.15625
- cotangent: bfloat16 [32, 2048, 576], P('batch', 'seq'), may hold values from -6 to 6
Outputs:
- layer_out: bfloat16 [32, 2048, 576], P('batch', 'seq')
- grad_tokens: bfloat16 [32, 2048, 576], P('batch', 'seq')
- grad_gain_attn: float32 [576], replicated
- grad_w_query: float32 [576, 576], replicated
- grad_w_key: float32 [576, 192], replicated
- grad_w_value: float32 [576, 192], replicated
- grad_w_out: float32 [576, 576], replicated
- grad_gain_mlp: float32 [576], replicated
- grad_w_gate: float32 [576, 1536], replicated
- grad_w_up: float32 [576, 1536], replicated
- grad_w_down: float32 [1536, 576], replicated
The draws below stay inside these ranges and needn't reach their ends.
Inputs may be any that keep to these rules, and one draw needn't show every extreme that they name: `lengths`: in each aligned block of 8 row slots one slot has length 2048 and another 2048 // 4.
All inputs are finite; a program needn't handle non-finite values.
Results may differ from the reference program's by a relative error of at most 0.015.
Values may be sent and summed in bfloat16 or wider, within the bound.
No kernel may reach another device: no remote copies, remote signals or barrier semaphores. Data moves between devices by JAX's collectives and lax.ppermute only.
A program may use at most 320 MiB of HBM per device.

```python
import jax
import jax.numpy as jnp
from jax import lax

D = 576
FF = 1536
H = 9
KVH = 3
HD = 64
L = 2048
ROWS_DEV = 8
ROWS = 32


def draw_lengths(key, part):
    key = jax.random.fold_in(key, 11)
    first_key, second_key = jax.random.split(key)
    block_count = ROWS // ROWS_DEV
    drawn = jax.random.randint(first_key, (block_count, ROWS_DEV), L // 4, L + 1)
    longest = jax.random.randint(second_key, (block_count, 1), 0, ROWS_DEV)
    slot_index = jnp.arange(ROWS_DEV)[None, :]
    drawn = jnp.where(slot_index == longest, L, drawn)
    drawn = jnp.where(slot_index == (longest + 1) % ROWS_DEV, L // 4, drawn)
    return drawn.reshape(ROWS).astype(jnp.int32)


def steps_of(own_key, extent, cuts, least, largest):
    factor_of = 1.0
    for dim, blocks in cuts:
        steps = jax.random.uniform(jax.random.fold_in(jax.random.fold_in(own_key, 6), dim), (blocks,), jnp.float32, least / len(cuts), largest / len(cuts))
        factor_of = factor_of * jnp.repeat(jnp.exp(steps), extent[dim] // blocks).reshape((-1,) + (1,) * (len(extent) - 1 - dim))
    return factor_of


def gaussian(key, dims, spread, bound, shards=(), kind=jnp.bfloat16):
    level = steps_of(key, dims, shards, -0.22, 0.18) if shards else 1.0
    values = jax.random.normal(key, dims, jnp.float32) * spread * level
    return jnp.minimum(jnp.maximum(values, -bound), bound).astype(kind)


def setup_inputs(seed: int = 0) -> dict:
    splits = jax.random.split(jax.random.key(seed), 13)
    return {
        "tokens": gaussian(splits[0], (ROWS, L, D), 1.0, 6.0, ((0, 4), (1, 8))),
        "lengths": draw_lengths(jax.random.fold_in(splits[12], 71), 0),
        "gain_attn": jnp.clip(1.0 + 0.1 * jax.random.normal(splits[2], (D,), jnp.float32), 0.5, 1.5),
        "w_query": gaussian(splits[3], (D, H * HD), D ** -0.5, 0.25),
        "w_key": gaussian(splits[4], (D, KVH * HD), D ** -0.5, 0.25),
        "w_value": gaussian(splits[5], (D, KVH * HD), D ** -0.5, 0.25),
        "w_out": gaussian(splits[6], (H * HD, D), (max(D * 16 // L, 1)) ** -0.5, 3.0),
        "gain_mlp": jnp.clip(1.0 + 0.1 * jax.random.normal(splits[7], (D,), jnp.float32), 0.5, 1.5),
        "w_gate": gaussian(splits[8], (D, FF), D ** -0.5, 0.25),
        "w_up": gaussian(splits[9], (D, FF), D ** -0.5, 0.25),
        "w_down": gaussian(splits[10], (FF, D), FF ** -0.5, 0.15625),
        "cotangent": gaussian(splits[11], (ROWS, L, D), 1.0, 6.0, ((0, 4), (1, 8))),
    }


EPSILON = 1e-05
ROPE_BASE = 10000.0
MASKED_SCORE = -1e+30
HIGHEST_PRECISION = lax.Precision.HIGHEST

@jax.custom_vjp
def low(v):
    return lax.optimization_barrier(v.astype(jnp.bfloat16)).astype(jnp.float32)

@jax.custom_vjp
def low_back(v):
    return v

def low_keep(v):
    return (low(v), None)

def low_pass(kept, grad):
    return (grad,)

def back_keep(v):
    return (v, None)

def back_low(kept, grad):
    return (low(grad),)
low.defvjp(low_keep, low_pass)
low_back.defvjp(back_keep, back_low)

def rope_tables(positions):
    freqs = ROPE_BASE ** (-(jnp.arange(HD // 2, dtype=jnp.float32) * 2.0) / HD)
    phases = positions[:, None] * freqs[None, :]
    phases = jnp.concatenate([phases, phases], axis=-1)
    return (jnp.cos(phases)[:, None, :], jnp.sin(phases)[:, None, :])

def rotate(vectors, cosine_table, sine_table):
    half_size = vectors.shape[-1] // 2
    turned = jnp.concatenate([-vectors[..., half_size:], vectors[..., :half_size]], axis=-1)
    return vectors * cosine_table + turned * sine_table

def rms_norm(vectors, gain):
    return vectors * lax.rsqrt(lax.optimization_barrier(jnp.mean(vectors * vectors, axis=-1, keepdims=True)) + EPSILON) * gain

def project(vectors, matrix):
    return jnp.einsum('rtd,de->rte', vectors, matrix, precision=HIGHEST_PRECISION)

def attend_row(pieces):
    queries, key_rows, value_rows, length = pieces
    positions = jnp.arange(L)
    allowed_keys = (positions[None, :] <= positions[:, None]) & (positions[None, :] < length)
    scores = jnp.einsum('qkgd,skd->kgqs', queries, key_rows, precision=HIGHEST_PRECISION) * HD ** (-0.5)
    scores = low_back(scores)
    scores = jnp.where(allowed_keys[None, None, :, :], scores, MASKED_SCORE)
    row_peak = lax.optimization_barrier(jnp.max(scores, axis=-1, keepdims=True))
    weights = jnp.exp(scores - row_peak)
    probs = weights / lax.optimization_barrier(jnp.sum(weights, axis=-1, keepdims=True))
    mixed = jnp.einsum('kgqs,skd->qkgd', low(probs), value_rows, precision=HIGHEST_PRECISION)
    return mixed.reshape(L, H * HD)

def layer_forward(inputs, gain_attn, w_query, w_key, w_value, w_out, gain_mlp, w_gate, w_up, w_down, lengths):
    row_count = inputs.shape[0]
    cosine_table, sine_table = rope_tables(jnp.arange(L).astype(jnp.float32))
    normed_attn = low(rms_norm(inputs, gain_attn))
    query_pre = low_back(project(normed_attn, w_query))
    key_pre = low_back(project(normed_attn, w_key))
    value_rows = low(low_back(project(normed_attn, w_value)))
    queries = low(rotate(query_pre.reshape(row_count, L, H, HD), cosine_table, sine_table))
    queries = queries.reshape(row_count, L, KVH, H // KVH, HD)
    key_rows = low(rotate(key_pre.reshape(row_count, L, KVH, HD), cosine_table, sine_table))
    value_rows = value_rows.reshape(row_count, L, KVH, HD)
    mixed = lax.map(jax.checkpoint(attend_row), (queries, key_rows, value_rows, lengths))
    mixed = low(low_back(mixed))
    resid = inputs + low_back(project(mixed, w_out))
    normed_mlp = low(rms_norm(resid, gain_mlp))
    gate_proj = low_back(project(normed_mlp, w_gate))
    up_proj = low_back(project(normed_mlp, w_up))
    hidden = low(jax.nn.silu(gate_proj) * up_proj)
    result = resid + project(hidden, w_down)
    valid = (jnp.arange(L)[None, :] < lengths[:, None]).astype(jnp.float32)[..., None]
    return result * valid

def reference(tokens, lengths, gain_attn, w_query, w_key, w_value, w_out, gain_mlp, w_gate, w_up, w_down, cotangent):
    params = (tokens.astype(jnp.float32), gain_attn.astype(jnp.float32), w_query.astype(jnp.float32), w_key.astype(jnp.float32), w_value.astype(jnp.float32), w_out.astype(jnp.float32), gain_mlp.astype(jnp.float32), w_gate.astype(jnp.float32), w_up.astype(jnp.float32), w_down.astype(jnp.float32))

    def forward_only(*values):
        return layer_forward(*values, lengths)
    result, pullback = jax.vjp(forward_only, *params)
    grads = pullback(cotangent.astype(jnp.float32))
    return (result.astype(jnp.bfloat16), grads[0].astype(jnp.bfloat16), grads[1], grads[2], grads[3], grads[4], grads[5], grads[6], grads[7], grads[8], grads[9])
```

```python
import functools

import jax
import jax.numpy as jnp
from jax import lax
from jax.experimental import pallas as pl
from jax.experimental.pallas import tpu as pltpu
from jax.sharding import PartitionSpec as P

H = 9
KVH = 3
HD = 64
GROUP = H // KVH

EPSILON = 1e-05
ROPE_BASE = 10000.0
MASKED_SCORE = -1e30
BF16 = jnp.bfloat16
F32 = jnp.float32
VMEM_LIMIT = 56 * 1024 * 1024


def dot(a, b, a_dim, b_dim):
    return lax.dot_general(a, b, (((a_dim,), (b_dim,)), ((), ())), preferred_element_type=F32)


def rope_tables(positions):
    freqs = ROPE_BASE ** (-(jnp.arange(HD // 2, dtype=F32) * 2.0) / HD)
    phases = freqs[:, None] * positions[None, :]
    return jnp.cos(phases), jnp.sin(phases)


def rms_scale(vectors):
    return lax.rsqrt(jnp.mean(vectors * vectors, axis=-1, keepdims=True) + EPSILON)


def norm_back(grad_normed, normed, inv_scale):
    return inv_scale * (
        grad_normed - normed * jnp.mean(grad_normed * normed, axis=-1, keepdims=True)
    )


def project(vectors, matrix):
    return jnp.einsum("rtd,de->rte", vectors, matrix, preferred_element_type=F32)


def project_back(gradient, matrix):
    return jnp.einsum("rte,de->rtd", gradient, matrix, preferred_element_type=F32)


def weight_grad(vectors, gradient):
    return jnp.einsum("rtd,rte->de", vectors, gradient, preferred_element_type=F32)


def qkv_kernel(info, x_ref, gain_ref, w_ref, cos_ref, sin_ref, q_ref, kv_ref, n_ref):
    used = info[0] < info[3 + pl.program_id(0)]

    @pl.when(used)
    def _():
        x = x_ref[0].astype(F32)
        normed = (x * rms_scale(x) * gain_ref[...]).astype(BF16)
        n_ref[0] = normed
        out = dot(w_ref[...], normed, 1, 1)
        cos, sin = cos_ref[...], sin_ref[...]

        def rope(block):
            u1, u2 = block[: HD // 2], block[HD // 2 :]
            return jnp.concatenate([u1 * cos - u2 * sin, u2 * cos + u1 * sin], axis=0)

        for h in range(H):
            rotated = rope(out[h * HD : (h + 1) * HD])
            q_ref[0, h * HD : (h + 1) * HD, :] = (rotated * HD**-0.5).astype(BF16)
        for k in range(KVH):
            base = H * HD + 2 * HD * k
            kv_ref[0, 2 * HD * k : 2 * HD * k + HD, :] = rope(out[base : base + HD]).astype(BF16)
            kv_ref[0, 2 * HD * k + HD : 2 * HD * (k + 1), :] = out[base + HD : base + 2 * HD].astype(
                BF16
            )

    @pl.when(jnp.logical_not(used))
    def _():
        q_ref[...] = jnp.zeros_like(q_ref)
        kv_ref[...] = jnp.zeros_like(kv_ref)
        n_ref[...] = jnp.zeros_like(n_ref)


def row_spec(shape):
    return pl.BlockSpec((1,) + shape, lambda r, info: (r, 0, 0))


def whole_spec(shape):
    return pl.BlockSpec(shape, lambda r, info: (0,) * len(shape))


def qkv_call(info, tokens, gain, weights, cos, sin):
    rows, length, width = tokens.shape
    return pl.pallas_call(
        qkv_kernel,
        grid_spec=pltpu.PrefetchScalarGridSpec(
            num_scalar_prefetch=1,
            grid=(rows,),
            in_specs=[
                row_spec((length, width)),
                whole_spec((1, width)),
                whole_spec(weights.shape),
                whole_spec(cos.shape),
                whole_spec(sin.shape),
            ],
            out_specs=[
                row_spec((H * HD, length)),
                row_spec((2 * KVH * HD, length)),
                row_spec((length, width)),
            ],
        ),
        out_shape=[
            jax.ShapeDtypeStruct((rows, H * HD, length), BF16),
            jax.ShapeDtypeStruct((rows, 2 * KVH * HD, length), BF16),
            jax.ShapeDtypeStruct((rows, length, width), BF16),
        ],
        compiler_params=pltpu.CompilerParams(vmem_limit_bytes=VMEM_LIMIT),
        name="qkv",
    )(info, tokens, gain, weights, cos, sin)


def heads_of(ref, k):
    return jnp.concatenate(
        [ref[0, (k * GROUP + g) * HD : (k * GROUP + g + 1) * HD, :] for g in range(GROUP)], axis=1
    )


def key_value(ref, k):
    return ref[0, 2 * HD * k : 2 * HD * k + HD, :], ref[0, 2 * HD * k + HD : 2 * HD * (k + 1), :]


def mask_diagonal(scores, start, length):
    size = scores.shape[0]
    key = lax.broadcasted_iota(jnp.int32, scores.shape, 0)
    query = lax.broadcasted_iota(jnp.int32, scores.shape, 1) % size
    allowed = jnp.logical_and(key <= query, start + key < length)
    return jnp.where(allowed, scores, MASKED_SCORE)


def visit_blocks(info, chips, kv_refs, visit):
    chip, core = info[1], info[2]

    @pl.when(core == 0)
    def _():
        visit([(0, True)], True)

    @pl.when(core == 1)
    def _():
        visit([(0, True), (1, False)], True)

    for d in range(1, chips):

        @pl.when(chip >= d)
        def _():
            visit([(2 * d, False), (2 * d + 1, False)], False)


def forward_kernel(chips, info, q_ref, *refs):
    kv_refs = refs[: 2 * chips]
    mixed_ref, lse_ref, peak_ref, total_ref, acc_ref = refs[2 * chips :]
    start, length = info[0], info[3 + pl.program_id(0)]
    used = start < length

    def visit(blocks, first):
        for k in range(KVH):
            queries = heads_of(q_ref, k)
            scores = []
            for b, diagonal in blocks:
                s = dot(key_value(kv_refs[b], k)[0], queries, 0, 0)
                scores.append(mask_diagonal(s, start, length) if diagonal else s)
            peak = scores[0].max(axis=0, keepdims=True)
            for s in scores[1:]:
                peak = jnp.maximum(peak, s.max(axis=0, keepdims=True))
            if not first:
                old = peak_ref[k]
                peak = jnp.maximum(peak, old)
                shrink = jnp.exp(old - peak)
            total, acc = 0.0, 0.0
            for (b, _), s in zip(blocks, scores):
                weights = jnp.exp(s - peak)
                total = total + weights.sum(axis=0, keepdims=True)
                acc = acc + dot(key_value(kv_refs[b], k)[1], weights.astype(BF16), 1, 0)
            if not first:
                total = total + total_ref[k] * shrink
                acc = acc + acc_ref[k] * shrink
            peak_ref[k], total_ref[k], acc_ref[k] = peak, total, acc

    @pl.when(used)
    def _():
        visit_blocks(info, chips, kv_refs, visit)
        size = q_ref.shape[2]
        parts = []
        for k in range(KVH):
            total = total_ref[k]
            out = acc_ref[k] / total
            lse = peak_ref[k] + jnp.log(total)
            for g in range(GROUP):
                lse_ref[0, k * GROUP + g : k * GROUP + g + 1, :] = lse[:, g * size : (g + 1) * size]
                parts.append(out[:, g * size : (g + 1) * size])
        mixed_ref[0] = jnp.concatenate(parts, axis=0).T.astype(BF16)

    @pl.when(jnp.logical_not(used))
    def _():
        mixed_ref[...] = jnp.zeros_like(mixed_ref)
        lse_ref[...] = jnp.zeros_like(lse_ref)


def forward_call(info, queries, kv_blocks):
    rows, _, length = queries.shape
    blocks = len(kv_blocks)
    return pl.pallas_call(
        functools.partial(forward_kernel, blocks // 2),
        grid_spec=pltpu.PrefetchScalarGridSpec(
            num_scalar_prefetch=1,
            grid=(rows,),
            in_specs=[row_spec((H * HD, length))] + [row_spec((2 * KVH * HD, length))] * blocks,
            out_specs=[row_spec((length, H * HD)), row_spec((H, length))],
            scratch_shapes=[
                pltpu.VMEM((KVH, 1, GROUP * length), F32),
                pltpu.VMEM((KVH, 1, GROUP * length), F32),
                pltpu.VMEM((KVH, HD, GROUP * length), F32),
            ],
        ),
        out_shape=[
            jax.ShapeDtypeStruct((rows, length, H * HD), BF16),
            jax.ShapeDtypeStruct((rows, H, length), F32),
        ],
        compiler_params=pltpu.CompilerParams(vmem_limit_bytes=VMEM_LIMIT),
        name="attention_forward",
    )(info, queries, *kv_blocks)


def backward_kernel(chips, info, q_ref, dmix_ref, mixed_ref, lse_ref, cos_ref, sin_ref, *refs):
    kv_refs = refs[: 2 * chips]
    dq_ref = refs[2 * chips]
    dkv_refs = refs[2 * chips + 1 : 4 * chips + 1]
    dmix_t_ref, inner_ref, dq_acc_ref = refs[4 * chips + 1 :]
    start, length = info[0], info[3 + pl.program_id(0)]
    chip, core = info[1], info[2]
    used = start < length
    size = q_ref.shape[2]

    def visit(blocks, first):
        for k in range(KVH):
            queries, dmix = heads_of(q_ref, k), heads_of(dmix_t_ref, k)
            lse = jnp.concatenate(
                [lse_ref[0, k * GROUP + g : k * GROUP + g + 1, :] for g in range(GROUP)], axis=1
            )
            inner = inner_ref[k]
            dq = None
            for b, diagonal in blocks:
                keys, values = key_value(kv_refs[b], k)
                s = dot(keys, queries, 0, 0)
                if diagonal:
                    s = mask_diagonal(s, start, length)
                probs = jnp.exp(s - lse)
                dprobs = dot(values, dmix, 0, 0)
                dscores = (probs * (dprobs - inner)).astype(BF16)
                part = dot(keys, dscores, 1, 0)
                dq = part if dq is None else dq + part
                dk = dot(dscores, queries, 1, 1)
                dv = dot(probs.astype(BF16), dmix, 1, 1)
                dkv_refs[b][0, :, 2 * HD * k : 2 * HD * (k + 1)] = jnp.concatenate(
                    [dk, dv], axis=1
                ).astype(BF16)
            if first:
                dq_acc_ref[k] = dq
            else:
                dq_acc_ref[k] += dq

    def clear(ref):
        ref[...] = jnp.zeros_like(ref)

    @pl.when(used)
    def _():
        dmix_t = dmix_ref[0].astype(F32).T
        mixed_t = mixed_ref[0].astype(F32).T
        dmix_t_ref[0] = dmix_t.astype(BF16)
        product = dmix_t * mixed_t
        for k in range(KVH):
            inner_ref[k] = jnp.concatenate(
                [
                    product[(k * GROUP + g) * HD : (k * GROUP + g + 1) * HD].sum(axis=0, keepdims=True)
                    for g in range(GROUP)
                ],
                axis=1,
            )
        visit_blocks(info, chips, kv_refs, visit)
        cos, sin = cos_ref[...], sin_ref[...]
        parts = []
        for k in range(KVH):
            dq = dq_acc_ref[k] * HD**-0.5
            for g in range(GROUP):
                head = dq[:, g * size : (g + 1) * size]
                u1, u2 = head[: HD // 2], head[HD // 2 :]
                parts += [u1 * cos + u2 * sin, u2 * cos - u1 * sin]
        dq_ref[0] = jnp.concatenate(parts, axis=0).T.astype(BF16)

    @pl.when(jnp.logical_not(used))
    def _():
        clear(dq_ref)
        clear(dkv_refs[0])

    @pl.when(jnp.logical_or(jnp.logical_not(used), core == 0))
    def _():
        clear(dkv_refs[1])

    for d in range(1, chips):

        @pl.when(jnp.logical_or(jnp.logical_not(used), chip < d))
        def _():
            clear(dkv_refs[2 * d])
            clear(dkv_refs[2 * d + 1])


def backward_call(info, queries, dmix, mixed, lse, cos, sin, kv_blocks):
    rows, _, length = queries.shape
    blocks = len(kv_blocks)
    return pl.pallas_call(
        functools.partial(backward_kernel, blocks // 2),
        grid_spec=pltpu.PrefetchScalarGridSpec(
            num_scalar_prefetch=1,
            grid=(rows,),
            in_specs=[
                row_spec((H * HD, length)),
                row_spec((length, H * HD)),
                row_spec((length, H * HD)),
                row_spec((H, length)),
                whole_spec(cos.shape),
                whole_spec(sin.shape),
            ]
            + [row_spec((2 * KVH * HD, length))] * blocks,
            out_specs=[row_spec((length, H * HD))] + [row_spec((length, 2 * KVH * HD))] * blocks,
            scratch_shapes=[
                pltpu.VMEM((1, H * HD, length), BF16),
                pltpu.VMEM((KVH, 1, GROUP * length), F32),
                pltpu.VMEM((KVH, HD, GROUP * length), F32),
            ],
        ),
        out_shape=[jax.ShapeDtypeStruct((rows, length, H * HD), BF16)]
        + [jax.ShapeDtypeStruct((rows, length, 2 * KVH * HD), BF16)] * blocks,
        compiler_params=pltpu.CompilerParams(vmem_limit_bytes=VMEM_LIMIT),
        name="attention_backward",
    )(info, queries, dmix, mixed, lse, cos, sin, *kv_blocks)


def interleave(keys, values):
    shape = keys.shape[:-1]
    pair = jnp.stack([keys.reshape(shape + (KVH, HD)), values.reshape(shape + (KVH, HD))], axis=-2)
    return pair.reshape(shape + (2 * KVH * HD,))


def separate(pairs):
    shape = pairs.shape[:-1]
    split = pairs.reshape(shape + (KVH, 2, HD))
    return (
        split[..., 0, :].reshape(shape + (KVH * HD,)),
        split[..., 1, :].reshape(shape + (KVH * HD,)),
    )


def body(
    tokens,
    lengths,
    gain_attn,
    w_query,
    w_key,
    w_value,
    w_out,
    gain_mlp,
    w_gate,
    w_up,
    w_down,
    cotangent,
):
    rows, local_len, width = tokens.shape
    seq = lax.axis_size("seq")
    chips = seq // 2
    place = lax.axis_index("seq")
    start = place * local_len
    swap = [(i, i ^ 1) for i in range(seq)]
    onward = [(i, i + 2) for i in range(seq - 2)]
    backward = [(i + 2, i) for i in range(seq - 2)]
    positions = start + jnp.arange(local_len, dtype=jnp.int32)
    cos, sin = rope_tables(positions.astype(F32))
    valid = (positions[None, :] < lengths[:, None]).astype(F32)[..., None]
    info = jnp.concatenate(
        [jnp.stack([start, place // 2, place % 2]).astype(jnp.int32), lengths]
    )
    w_kv = interleave(w_key, w_value)
    w_qkv_t = jnp.concatenate([w_query, w_kv], axis=1).T

    queries, kv_own, attn_in = qkv_call(info, tokens, gain_attn[None, :], w_qkv_t, cos, sin)
    kv_blocks = []
    moving = kv_own
    for d in range(chips):
        if d:
            moving = lax.ppermute(moving, "seq", onward)
        kv_blocks += [moving, lax.ppermute(moving, "seq", swap)]
    mixed, lse = forward_call(info, queries, kv_blocks)

    inputs = tokens.astype(F32)
    resid = inputs + project(mixed, w_out)
    mlp_scale = rms_scale(resid)
    normed_mlp = resid * mlp_scale
    mlp_in = (normed_mlp * gain_mlp).astype(BF16)
    gate_proj = project(mlp_in, w_gate)
    up_proj = project(mlp_in, w_up)
    sigmoid_gate = jax.nn.sigmoid(gate_proj)
    activated = gate_proj * sigmoid_gate
    hidden = (activated * up_proj).astype(BF16)
    layer_out = ((resid + project(hidden, w_down)) * valid).astype(BF16)
    grad_out = cotangent.astype(F32) * valid
    grad_out_low = grad_out.astype(BF16)
    grad_down = weight_grad(grad_out_low, hidden)
    grad_hidden = project_back(grad_out_low, w_down)
    grad_gate_pre = (
        grad_hidden * up_proj * sigmoid_gate * (1.0 + gate_proj * (1.0 - sigmoid_gate))
    ).astype(BF16)
    grad_up_pre = (grad_hidden * activated).astype(BF16)
    grad_gate = weight_grad(mlp_in, grad_gate_pre)
    grad_up = weight_grad(mlp_in, grad_up_pre)
    grad_mlp_in = project_back(grad_gate_pre, w_gate) + project_back(grad_up_pre, w_up)
    grad_gain_mlp = jnp.sum(grad_mlp_in * normed_mlp, axis=(0, 1))
    grad_resid = grad_out + norm_back(grad_mlp_in * gain_mlp, normed_mlp, mlp_scale)
    grad_attn = grad_resid.astype(BF16)
    grad_out_proj = weight_grad(mixed, grad_attn)
    grad_mixed = project_back(grad_attn, w_out).astype(BF16)

    grad_query_pre, *dkv_blocks = backward_call(
        info, queries, grad_mixed, mixed, lse, cos, sin, kv_blocks
    )
    total = None
    for d in reversed(range(chips)):
        own = dkv_blocks[2 * d].astype(F32) + lax.ppermute(
            dkv_blocks[2 * d + 1], "seq", swap
        ).astype(F32)
        if total is not None:
            own = own + lax.ppermute(total, "seq", backward).astype(F32)
        total = own.astype(BF16)
    grad_key, grad_value_pre = separate(total)
    keys = grad_key.astype(F32).reshape(rows, local_len, KVH, HD)
    k1, k2 = keys[..., : HD // 2], keys[..., HD // 2 :]
    cos_n, sin_n = cos.T[:, None, :], sin.T[:, None, :]
    grad_key_pre = (
        jnp.concatenate([k1 * cos_n + k2 * sin_n, k2 * cos_n - k1 * sin_n], axis=-1)
        .astype(BF16)
        .reshape(rows, local_len, KVH * HD)
    )
    attn_scale = rms_scale(inputs)
    normed_attn = inputs * attn_scale
    grad_query_w = weight_grad(attn_in, grad_query_pre)
    grad_key_w = weight_grad(attn_in, grad_key_pre)
    grad_value_w = weight_grad(attn_in, grad_value_pre)
    grad_attn_in = (
        project_back(grad_query_pre, w_query)
        + project_back(grad_key_pre, w_key)
        + project_back(grad_value_pre, w_value)
    )
    grad_gain_attn = jnp.sum(grad_attn_in * normed_attn, axis=(0, 1))
    grad_tokens = (
        grad_resid + norm_back(grad_attn_in * gain_attn, normed_attn, attn_scale)
    ).astype(BF16)

    both = ("batch", "seq")
    mlp_grads = lax.psum(
        jnp.concatenate([grad_gate, grad_up, grad_down], axis=1).astype(BF16), both
    ).astype(F32)
    attn_grads = lax.psum(
        jnp.concatenate([grad_query_w, grad_key_w, grad_value_w, grad_out_proj], axis=1).astype(
            BF16
        ),
        both,
    ).astype(F32)
    gains = lax.psum(jnp.stack([grad_gain_attn, grad_gain_mlp]), both)
    hidden_width = w_gate.shape[1]
    q_end, k_end, v_end = H * HD, (H + KVH) * HD, (H + 2 * KVH) * HD
    return (
        layer_out,
        grad_tokens,
        gains[0],
        attn_grads[:, :q_end],
        attn_grads[:, q_end:k_end],
        attn_grads[:, k_end:v_end],
        attn_grads[:, v_end:],
        gains[1],
        mlp_grads[:, :hidden_width],
        mlp_grads[:, hidden_width : 2 * hidden_width],
        mlp_grads[:, 2 * hidden_width :].T,
    )


def solution(mesh):
    split, copied = P("batch", "seq", None), P()
    in_specs = (split, P("batch")) + (copied,) * 9 + (split,)
    out_specs = (split, split) + (copied,) * 9
    return jax.shard_map(body, mesh=mesh, in_specs=in_specs, out_specs=out_specs, check_vma=False)
```

```python
import functools

import jax
import jax.numpy as jnp
from jax import lax
from jax.experimental import pallas as pl
from jax.experimental.pallas import tpu as pltpu
from jax.sharding import PartitionSpec as P

H = 9
KVH = 3
HD = 64
GROUP = H // KVH
Q_WIDTH = H * HD
KV_WIDTH = 2 * KVH * HD

EPSILON = 1e-05
ROPE_BASE = 10000.0
MASKED_SCORE = -1e30
BF16 = jnp.bfloat16
F32 = jnp.float32
VMEM_LIMIT = 56 * 1024 * 1024
LANES = 128

START, CHIP, CORE, BATCH, LENGTHS = 0, 1, 2, 3, 4


def dot(a, b, a_dim=1, b_dim=0):
    return lax.dot_general(a, b, (((a_dim,), (b_dim,)), ((), ())), preferred_element_type=F32)


def rope_tables(positions):
    freqs = ROPE_BASE ** (-(jnp.arange(HD // 2, dtype=F32) * 2.0) / HD)
    phases = freqs[:, None] * positions[None, :]
    return jnp.cos(phases), jnp.sin(phases)


def rope(block, cos, sin):
    u1, u2 = block[: HD // 2], block[HD // 2 :]
    return jnp.concatenate([u1 * cos - u2 * sin, u2 * cos + u1 * sin], axis=0)


def rope_back(block, cos, sin):
    u1, u2 = block[: HD // 2], block[HD // 2 :]
    return jnp.concatenate([u1 * cos + u2 * sin, u2 * cos - u1 * sin], axis=0)


def rms_scale(vectors):
    return lax.rsqrt(jnp.mean(vectors * vectors, axis=0, keepdims=True) + EPSILON)


def norm_back(grad_normed, normed, inv_scale):
    return inv_scale * (
        grad_normed - normed * jnp.mean(grad_normed * normed, axis=0, keepdims=True)
    )


def clear(ref):
    ref[...] = jnp.zeros_like(ref)


def row_spec(shape, first=0):
    return pl.BlockSpec((1,) + shape, lambda r, info: (first + r, 0, 0))


def slot_spec(shape, rows, first=0):
    return pl.BlockSpec((1,) + shape, lambda r, info: (info[LENGTHS + rows + first + r], 0, 0))


def whole_spec(shape):
    return pl.BlockSpec(
        shape, lambda r, info: (0,) * len(shape), pipeline_mode=pl.Buffered(buffer_count=1)
    )


def shape_of(shape, dtype=BF16):
    return jax.ShapeDtypeStruct(shape, dtype)


def cost_of(microseconds):
    return pl.CostEstimate(
        flops=int(microseconds * 8e8), bytes_accessed=int(microseconds * 1e6), transcendentals=0
    )


def row_kernel_call(
    kernel, name, rows, in_specs, out_specs, out_shape, scratch=(), cost=None, aliases=None
):
    return pl.pallas_call(
        kernel,
        grid_spec=pltpu.PrefetchScalarGridSpec(
            num_scalar_prefetch=1,
            grid=(rows,),
            in_specs=in_specs,
            out_specs=out_specs,
            scratch_shapes=scratch,
        ),
        out_shape=out_shape,
        compiler_params=pltpu.CompilerParams(vmem_limit_bytes=VMEM_LIMIT),
        cost_estimate=cost,
        input_output_aliases=aliases or {},
        name=name,
    )


def row_used(info, first=0):
    length = info[LENGTHS + first + pl.program_id(0)]
    return length, info[START] < length


def qkv_kernel(first, info, x_ref, gain_ref, w_ref, cos_ref, sin_ref, q_ref, kv_ref):
    _, used = row_used(info, first)

    @pl.when(used)
    def _():
        x = x_ref[0].astype(F32)
        normed = (x * rms_scale(x) * gain_ref[...]).astype(BF16)
        out = dot(w_ref[...], normed)
        cos, sin = cos_ref[...], sin_ref[...]
        for h in range(H):
            rotated = rope(out[h * HD : (h + 1) * HD], cos, sin)
            q_ref[0, h * HD : (h + 1) * HD, :] = (rotated * HD**-0.5).astype(BF16)
        for k in range(KVH):
            base, at = Q_WIDTH + 2 * HD * k, 2 * HD * k
            kv_ref[0, at : at + HD, :] = rope(out[base : base + HD], cos, sin).astype(BF16)
            kv_ref[0, at + HD : at + 2 * HD, :] = out[base + HD : base + 2 * HD].astype(BF16)

    @pl.when(jnp.logical_not(used))
    def _():
        clear(q_ref)
        clear(kv_ref)


def qkv_call(info, tokens, gain, weights, cos, sin, first=0, count=None):
    rows, width, length = tokens.shape
    count = count or rows
    return row_kernel_call(
        functools.partial(qkv_kernel, first),
        "qkv",
        count,
        [
            slot_spec((width, length), rows, first),
            whole_spec(gain.shape),
            whole_spec(weights.shape),
            whole_spec(cos.shape),
            whole_spec(sin.shape),
        ],
        [row_spec((Q_WIDTH, length)), row_spec((KV_WIDTH, length))],
        [shape_of((count, Q_WIDTH, length)), shape_of((count, KV_WIDTH, length))],
        cost=cost_of(1.2 * count),
    )(info, tokens, gain, weights, cos, sin)


def heads_of(ref, k):
    return jnp.concatenate(
        [ref[0, (k * GROUP + g) * HD : (k * GROUP + g + 1) * HD, :] for g in range(GROUP)], axis=1
    )


def key_value(kv_refs, block, k):
    ref, at = kv_refs[block], 2 * HD * k
    return ref[0, at : at + HD, :], ref[0, at + HD : at + 2 * HD, :]


def stack_spec(reach, length):
    return pl.BlockSpec((reach + 1, 1, KV_WIDTH, length), lambda r, info: (0, r, 0, 0))


def mask_diagonal(scores, start, length):
    size = scores.shape[0]
    key = lax.broadcasted_iota(jnp.int32, scores.shape, 0)
    query = lax.broadcasted_iota(jnp.int32, scores.shape, 1) % size
    allowed = jnp.logical_and(key <= query, start + key < length)
    return jnp.where(allowed, scores, MASKED_SCORE)


def visit_blocks(info, chips, visit):
    chip, core = info[CHIP], info[CORE]

    @pl.when(core == 0)
    def _():
        visit([(0, True)], True)

    @pl.when(core == 1)
    def _():
        visit([(0, True), (1, False)], True)

    for d in range(1, chips):

        @pl.when(chip >= d)
        def _():
            visit([(2 * d, False), (2 * d + 1, False)], False)


def forward_kernel(chunk, info, q_ref, *refs):
    first_row, _, reach = chunk
    kv_refs = refs[: 2 * reach + 2]
    mixed_ref, lse_ref, peak_ref, total_ref, acc_ref = refs[-5:]
    length, used = row_used(info, first_row)
    start = info[START]

    def visit(blocks, first):
        for k in range(KVH):
            queries = heads_of(q_ref, k)
            scores = []
            for b, diagonal in blocks:
                s = dot(key_value(kv_refs, b, k)[0], queries, 0, 0)
                scores.append(mask_diagonal(s, start, length) if diagonal else s)
            peak = scores[0].max(axis=0, keepdims=True)
            for s in scores[1:]:
                peak = jnp.maximum(peak, s.max(axis=0, keepdims=True))
            if not first:
                old = peak_ref[k]
                peak = jnp.maximum(peak, old)
                shrink = jnp.exp(old - peak)
            total, acc = 0.0, 0.0
            for (b, _), s in zip(blocks, scores):
                weights = jnp.exp(s - peak)
                total = total + weights.sum(axis=0, keepdims=True)
                acc = acc + dot(key_value(kv_refs, b, k)[1], weights.astype(BF16))
            if not first:
                total = total + total_ref[k] * shrink
                acc = acc + acc_ref[k] * shrink
            peak_ref[k], total_ref[k], acc_ref[k] = peak, total, acc

    @pl.when(used)
    def _():
        visit_blocks(info, reach + 1, visit)
        size = q_ref.shape[2]
        for k in range(KVH):
            total = total_ref[k]
            out = (acc_ref[k] / total).astype(BF16)
            lse = peak_ref[k] + jnp.log(total)
            for g in range(GROUP):
                h = k * GROUP + g
                lse_ref[0, h : h + 1, :] = lse[:, g * size : (g + 1) * size]
                mixed_ref[0, h * HD : (h + 1) * HD, :] = out[:, g * size : (g + 1) * size]

    @pl.when(jnp.logical_not(used))
    def _():
        clear(mixed_ref)
        clear(lse_ref)


def forward_call(chunk, rows, info, queries, kv, mixed):
    first, count, reach = chunk
    length = queries.shape[2]
    earlier = [] if mixed is None else [mixed]
    return row_kernel_call(
        functools.partial(forward_kernel, chunk),
        "attention_forward",
        count,
        [row_spec((Q_WIDTH, length), first)]
        + [row_spec((KV_WIDTH, length))] * len(kv)
        + [pl.BlockSpec(memory_space=pl.ANY)] * len(earlier),
        [row_spec((Q_WIDTH, length), first), row_spec((H, length))],
        [shape_of((rows, Q_WIDTH, length)), shape_of((count, H, length), F32)],
        [
            pltpu.VMEM((KVH, 1, GROUP * length), F32),
            pltpu.VMEM((KVH, 1, GROUP * length), F32),
            pltpu.VMEM((KVH, HD, GROUP * length), F32),
        ],
        aliases={2 + len(kv): 0} if earlier else None,
        cost=cost_of(2.5 * count),
    )(info, queries, *kv, *earlier)


def backward_kernel(chunk, info, q_ref, dmix_ref, mixed_ref, lse_ref, cos_ref, sin_ref, *refs):
    first_row, _, reach = chunk
    kv_refs = refs[: 2 * reach + 2]
    dq_ref, *dkv_refs = refs[-5:-2]
    inner_ref, dq_acc_ref = refs[-2:]
    length, used = row_used(info, first_row)
    start, chip, core = info[START], info[CHIP], info[CORE]
    size = q_ref.shape[2]

    def visit(blocks, first):
        for k in range(KVH):
            queries, dmix = heads_of(q_ref, k), heads_of(dmix_ref, k)
            lse = jnp.concatenate(
                [lse_ref[0, k * GROUP + g : k * GROUP + g + 1, :] for g in range(GROUP)], axis=1
            )
            inner = inner_ref[k]
            dq = None
            for b, diagonal in blocks:
                keys, values = key_value(kv_refs, b, k)
                s = dot(keys, queries, 0, 0)
                if diagonal:
                    s = mask_diagonal(s, start, length)
                probs = jnp.exp(s - lse)
                dprobs = dot(values, dmix, 0, 0)
                dscores = (probs * (dprobs - inner)).astype(BF16)
                part = dot(keys, dscores)
                dq = part if dq is None else dq + part
                dk = dot(dscores, queries, 1, 1)
                dv = dot(probs.astype(BF16), dmix, 1, 1)
                dkv_refs[b % 2][b // 2, 0, 2 * HD * k : 2 * HD * (k + 1), :] = (
                    jnp.concatenate([dk, dv], axis=1).T.astype(BF16)
                )
            if first:
                dq_acc_ref[k] = dq
            else:
                dq_acc_ref[k] += dq

    @pl.when(used)
    def _():
        for k in range(KVH):
            parts = []
            for g in range(GROUP):
                at = slice((k * GROUP + g) * HD, (k * GROUP + g + 1) * HD)
                product = dmix_ref[0, at, :].astype(F32) * mixed_ref[0, at, :].astype(F32)
                parts.append(product.sum(axis=0, keepdims=True))
            inner_ref[k] = jnp.concatenate(parts, axis=1)
        visit_blocks(info, reach + 1, visit)
        cos, sin = cos_ref[...], sin_ref[...]
        for k in range(KVH):
            dq = dq_acc_ref[k] * HD**-0.5
            for g in range(GROUP):
                h = k * GROUP + g
                dq_ref[0, h * HD : (h + 1) * HD, :] = rope_back(
                    dq[:, g * size : (g + 1) * size], cos, sin
                ).astype(BF16)

    unused = jnp.logical_not(used)

    def clear_block(b):
        dkv_refs[b % 2][b // 2] = jnp.zeros(dkv_refs[b % 2].shape[1:], BF16)

    @pl.when(unused)
    def _():
        clear(dq_ref)
        clear_block(0)

    @pl.when(jnp.logical_or(unused, core == 0))
    def _():
        clear_block(1)

    for d in range(1, reach + 1):

        @pl.when(jnp.logical_or(unused, chip < d))
        def _():
            clear_block(2 * d)
            clear_block(2 * d + 1)


def backward_call(chunk, info, queries, dmix, mixed, lse, cos, sin, kv):
    first, count, reach = chunk
    length = dmix.shape[2]
    return row_kernel_call(
        functools.partial(backward_kernel, chunk),
        "attention_backward",
        count,
        [
            row_spec((Q_WIDTH, length), first),
            row_spec((Q_WIDTH, length), first),
            row_spec((Q_WIDTH, length), first),
            row_spec((H, length)),
            whole_spec(cos.shape),
            whole_spec(sin.shape),
        ]
        + [row_spec((KV_WIDTH, length))] * len(kv),
        [row_spec((Q_WIDTH, length))] + [stack_spec(reach, length)] * 2,
        [shape_of((count, Q_WIDTH, length))]
        + [shape_of((reach + 1, count, KV_WIDTH, length))] * 2,
        [
            pltpu.VMEM((KVH, 1, GROUP * length), F32),
            pltpu.VMEM((KVH, HD, GROUP * length), F32),
        ],
        cost=cost_of(4 * count),
    )(info, queries, dmix, mixed, lse, cos, sin, *kv)


def write_halves(info, acc_refs, keep_ref, send_ref):
    at = 0
    for acc_ref in acc_refs:
        half, width = acc_ref.shape[0] // 2, acc_ref.shape[1]
        mine = pl.multiple_of(info[CORE] * half, 8)
        other = pl.multiple_of((1 - info[CORE]) * half, 8)
        keep_ref[:, at : at + width] = acc_ref[pl.ds(mine, half), :].astype(BF16)
        send_ref[:, at : at + width] = acc_ref[pl.ds(other, half), :].astype(BF16)
        at += width


def mlp_kernel(
    info,
    x_ref,
    mixed_ref,
    dy_ref,
    gain_ref,
    w_out_t_ref,
    w_out_ref,
    w_gate_t_ref,
    w_gate_ref,
    w_up_t_ref,
    w_up_ref,
    w_down_ref,
    w_down_t_ref,
    out_ref,
    da_ref,
    dmix_ref,
    keep_ref,
    send_ref,
    grad_gain_ref,
    acc_ref,
    acc_out_ref,
    acc_gain_ref,
):
    length, used = row_used(info)
    row = pl.program_id(0)
    width, size = x_ref.shape[1:]
    hidden_width = w_gate_ref.shape[1]
    step = 512 if hidden_width % 512 == 0 else hidden_width

    @pl.when(row == 0)
    def _():
        clear(acc_ref)
        clear(acc_out_ref)
        clear(acc_gain_ref)

    @pl.when(used)
    def _():
        mixed = mixed_ref[0]
        resid = x_ref[0].astype(F32) + dot(w_out_t_ref[...], mixed)
        scale = rms_scale(resid)
        normed = resid * scale
        mlp_in = (normed * gain_ref[...]).astype(BF16)
        position = info[START] + lax.broadcasted_iota(jnp.int32, (1, size), 1)
        valid = (position < length).astype(F32)
        dy_wide = dy_ref[0].astype(F32) * valid
        dy = dy_wide.astype(BF16)
        out, grad_in = resid, None
        for at in range(0, hidden_width, step):
            part = slice(at, at + step)
            gate = dot(w_gate_t_ref[part, :], mlp_in)
            up = dot(w_up_t_ref[part, :], mlp_in)
            dhidden = dot(w_down_ref[part, :], dy)
            sigmoid = 1.0 / (1.0 + jnp.exp(-gate))
            activated = gate * sigmoid
            hidden = (activated * up).astype(BF16)
            dgate = (dhidden * up * sigmoid * (1.0 + gate * (1.0 - sigmoid))).astype(BF16)
            dup = (dhidden * activated).astype(BF16)
            out = out + dot(w_down_t_ref[:, part], hidden)
            piece = dot(w_gate_ref[:, part], dgate) + dot(w_up_ref[:, part], dup)
            grad_in = piece if grad_in is None else grad_in + piece
            acc_ref[:, at : at + step] += dot(mlp_in, dgate, 1, 1)
            acc_ref[:, hidden_width + at : hidden_width + at + step] += dot(mlp_in, dup, 1, 1)
            acc_ref[:, 2 * hidden_width + at : 2 * hidden_width + at + step] += dot(
                dy, hidden, 1, 1
            )
        out_ref[0] = (out * valid).astype(BF16)
        acc_gain_ref[...] += grad_in * normed
        dresid = dy_wide + norm_back(grad_in * gain_ref[...], normed, scale)
        da = dresid.astype(BF16)
        da_ref[0] = da
        dmix_ref[0] = dot(w_out_ref[...], da).astype(BF16)
        acc_out_ref[...] += dot(mixed, da, 1, 1)

    @pl.when(jnp.logical_not(used))
    def _():
        clear(out_ref)
        clear(da_ref)
        clear(dmix_ref)

    @pl.when(row == pl.num_programs(0) - 1)
    def _():
        write_halves(info, [acc_ref, acc_out_ref], keep_ref, send_ref)
        grad_gain_ref[...] = jnp.broadcast_to(
            acc_gain_ref[...].sum(axis=1, keepdims=True), grad_gain_ref.shape
        )


def mlp_call(info, tokens, mixed, cotangent, gain, weights):
    rows, width, length = tokens.shape
    total = 3 * weights[2].shape[0]
    return row_kernel_call(
        mlp_kernel,
        "feed_forward",
        rows,
        [
            slot_spec((width, length), rows),
            row_spec((Q_WIDTH, length)),
            slot_spec((width, length), rows),
            whole_spec(gain.shape),
        ]
        + [whole_spec(w.shape) for w in weights],
        [
            slot_spec((width, length), rows),
            row_spec((width, length)),
            row_spec((Q_WIDTH, length)),
            whole_spec((width // 2, total + width)),
            whole_spec((width // 2, total + width)),
            whole_spec((width, LANES)),
        ],
        [
            shape_of((rows, width, length)),
            shape_of((rows, width, length)),
            shape_of((rows, Q_WIDTH, length)),
            shape_of((width // 2, total + width)),
            shape_of((width // 2, total + width)),
            shape_of((width, LANES), F32),
        ],
        [
            pltpu.VMEM((width, total), F32),
            pltpu.VMEM((Q_WIDTH, width), F32),
            pltpu.VMEM((width, length), F32),
        ],
        cost=cost_of(60),
    )(info, tokens, mixed, cotangent, gain, *weights)


def qkv_back_kernel(
    info,
    x_ref,
    da_ref,
    dq_ref,
    dkv_ref,
    gain_ref,
    w_ref,
    cos_ref,
    sin_ref,
    grad_gain_mlp_ref,
    dx_ref,
    keep_ref,
    send_ref,
    acc_ref,
    acc_gain_ref,
):
    _, used = row_used(info)
    row = pl.program_id(0)
    width = x_ref.shape[1]
    inner = Q_WIDTH + KV_WIDTH

    @pl.when(row == 0)
    def _():
        clear(acc_ref)
        clear(acc_gain_ref)

    @pl.when(used)
    def _():
        x = x_ref[0].astype(F32)
        scale = rms_scale(x)
        normed = x * scale
        attn_in = (normed * gain_ref[...]).astype(BF16)
        cos, sin = cos_ref[...], sin_ref[...]
        parts = [dq_ref[0]]
        for k in range(KVH):
            at = 2 * HD * k
            parts.append(rope_back(dkv_ref[0, at : at + HD, :].astype(F32), cos, sin).astype(BF16))
            parts.append(dkv_ref[0, at + HD : at + 2 * HD, :])
        grads = jnp.concatenate(parts, axis=0)
        dn = dot(w_ref[...], grads)
        acc_ref[:, :inner] += dot(attn_in, grads, 1, 1)
        acc_gain_ref[...] += dn * normed
        dx_ref[0] = (
            da_ref[0].astype(F32) + norm_back(dn * gain_ref[...], normed, scale)
        ).astype(BF16)

    @pl.when(jnp.logical_not(used))
    def _():
        clear(dx_ref)

    @pl.when(row == pl.num_programs(0) - 1)
    def _():
        lane = lax.broadcasted_iota(jnp.int32, (width, LANES), 1)
        acc_ref[:, inner:] = jnp.where(
            lane < LANES // 2,
            acc_gain_ref[...].sum(axis=1, keepdims=True),
            grad_gain_mlp_ref[...],
        )
        write_halves(info, [acc_ref], keep_ref, send_ref)


def qkv_back_call(info, tokens, da, dq, dkv, gain, weights, cos, sin, grad_gain_mlp):
    rows, width, length = tokens.shape
    total = Q_WIDTH + KV_WIDTH + LANES
    return row_kernel_call(
        qkv_back_kernel,
        "qkv_backward",
        rows,
        [
            slot_spec((width, length), rows),
            row_spec((width, length)),
            row_spec((Q_WIDTH, length)),
            row_spec((KV_WIDTH, length)),
        ]
        + [whole_spec(a.shape) for a in (gain, weights, cos, sin, grad_gain_mlp)],
        [
            slot_spec((width, length), rows),
            whole_spec((width // 2, total)),
            whole_spec((width // 2, total)),
        ],
        [
            shape_of((rows, width, length)),
            shape_of((width // 2, total)),
            shape_of((width // 2, total)),
        ],
        [pltpu.VMEM((width, total), F32), pltpu.VMEM((width, length), F32)],
        cost=cost_of(14),
    )(info, tokens, da, dq, dkv, gain, weights, cos, sin, grad_gain_mlp)


def exchange(array, axis, bits, low=1):
    size = lax.axis_size(axis)
    return lax.ppermute(array, axis, [(i, i ^ (bits * low)) for i in range(size)])


def add(*arrays):
    total = arrays[0].astype(F32)
    for array in arrays[1:]:
        total = total + array.astype(F32)
    return total.astype(BF16)


def place_of(axis, low):
    return lax.axis_index(axis) // low, lax.axis_size(axis) // low


def after(value, *others):
    return lax.optimization_barrier((value, others))[0]


class Sum:
    def __init__(self, keep, send, divided):
        self.keep, self.send, self.divided = keep, send, divided
        self.share = divided // (lax.axis_size("seq") // 2)
        self.steps = iter(
            [self.halve, self.over_batch, self.over_chips]
            + ([self.back_chips] if divided else [])
            + [self.back_batch, self.back_halves]
        )

    def begin(self):
        next(self.steps)()

    def end(self, *others):
        self.local = after(self.local, *others)
        self.array = self.finish(self.local, self.received)
        return self.array

    def added(self, local, received):
        return add(local, *received)

    def halve(self):
        self.local, self.received = self.keep, [exchange(self.send, "seq", 1)]
        self.finish = self.added

    def over_batch(self):
        me, count = place_of("batch", 1)
        share = self.array.shape[0] // count

        def part(index):
            return lax.dynamic_slice_in_dim(self.array, index * share, share, 0)

        self.received = [exchange(part(me ^ k), "batch", k) for k in range(1, count)]
        self.local, self.finish = part(me), self.added

    def over_chips(self):
        me, count = place_of("seq", 2)

        def part(index):
            if not self.divided:
                return self.array
            left = lax.dynamic_slice_in_dim(self.array, index * self.share, self.share, 1)
            return jnp.concatenate([left, self.array[:, self.divided :]], axis=1)

        self.received = [exchange(part(me ^ k), "seq", k, 2) for k in range(1, count)]
        self.local, self.finish = part(me), self.added

    def back_chips(self):
        _, count = place_of("seq", 2)
        left, right = self.array[:, : self.share], self.array[:, self.share :]
        self.received = [exchange(left, "seq", k, 2) for k in range(1, count)]
        self.local = left
        self.finish = lambda local, received: jnp.concatenate([local, *received, right], axis=1)

    def back_batch(self):
        _, count = place_of("batch", 1)
        self.received = [exchange(self.array, "batch", k) for k in range(1, count)]
        self.local = self.array
        self.finish = lambda local, received: jnp.stack([local, *received])

    def back_halves(self):
        self.local, self.received = self.array, exchange(self.array, "seq", 1)
        self.finish = lambda local, received: (local, received)


def select_core(info, mine_ref, other_ref, write):
    shares = pl.num_programs(0) // 2
    upper = (pl.program_id(0) >= shares).astype(jnp.int32)

    @pl.when(upper == info[CORE])
    def _():
        write(mine_ref)

    @pl.when(upper != info[CORE])
    def _():
        write(other_ref)


def share_specs(shape):
    shares = shape[0]
    rest = (0,) * (len(shape) - 1)

    def index(core, i, info):
        step = i - core * shares
        return (jnp.clip(step, 0, shares - 1) ^ info[BATCH],) + rest

    block = (1,) + tuple(shape[1:])
    return [
        pl.BlockSpec(block, lambda i, info: index(info[CORE], i, info)),
        pl.BlockSpec(block, lambda i, info: index(1 - info[CORE], i, info)),
    ]


def divided_kernel(chips, info, mine_ref, other_ref, *out_refs):
    out_width, rest = out_refs[0].shape[2], out_refs[-1].shape[2]
    width = (mine_ref.shape[2] - rest) // chips

    def write(ref):
        for q in range(chips):
            begin = pl.multiple_of((info[CHIP] ^ q) * width, LANES)
            share = ref[0, :, pl.ds(begin, width)].astype(F32)
            at = q * width
            while at < (q + 1) * width:
                out, column = divmod(at, out_width)
                size = min((q + 1) * width - at, out_width - column)
                begin = at - q * width
                out_refs[out][0, :, column : column + size] = share[:, begin : begin + size]
                at += size
        out_refs[-1][0] = ref[0, :, chips * width :].astype(F32)

    select_core(info, mine_ref, other_ref, write)


def divided_call(info, mine, other, chips, divided, count):
    shares, height, total = mine.shape
    widths = [divided // count] * count + [total - divided]
    out = row_kernel_call(
        functools.partial(divided_kernel, chips),
        "assemble_divided",
        2 * shares,
        share_specs(mine.shape),
        [pl.BlockSpec((1, height, w), lambda i, info: (i, 0, 0)) for w in widths],
        [shape_of((2 * shares, height, w), F32) for w in widths],
        cost=cost_of(8),
    )(info, mine, other)
    return [o.reshape(2 * shares * height, w) for o, w in zip(out, widths)]


def whole_kernel(info, mine_ref, other_ref, out_ref):
    def write(ref):
        out_ref[...] = ref[...].astype(F32)

    select_core(info, mine_ref, other_ref, write)


def whole_call(info, mine, other):
    shares, height, width = mine.shape
    out = row_kernel_call(
        whole_kernel,
        "assemble_whole",
        2 * shares,
        share_specs(mine.shape),
        pl.BlockSpec((1, height, width), lambda i, info: (i, 0, 0)),
        shape_of((2 * shares, height, width), F32),
        cost=cost_of(3),
    )(info, mine, other)
    return out.reshape(2 * shares * height, width)


def assemble_kernel(info, mine_ref, other_ref, query_ref, key_ref, value_ref, gain_ref, whole_ref):
    shares, height, _ = mine_ref.shape
    batch = info[BATCH]

    def write(half, ref):
        for j in range(shares):
            at = (half * shares + j) * height
            whole_ref[at : at + height, :] = ref[j ^ batch].astype(F32)

    @pl.when(info[CORE] == 0)
    def _():
        write(0, mine_ref)
        write(1, other_ref)

    @pl.when(info[CORE] == 1)
    def _():
        write(0, other_ref)
        write(1, mine_ref)

    query_ref[...] = whole_ref[:, :Q_WIDTH]
    rest = whole_ref[:, Q_WIDTH:].T
    for k in range(KVH):
        at = 2 * HD * k
        key_ref[k * HD : (k + 1) * HD, :] = rest[at : at + HD]
        value_ref[k * HD : (k + 1) * HD, :] = rest[at + HD : at + 2 * HD]
    gain_ref[0:1, :] = rest[KV_WIDTH : KV_WIDTH + 1]
    gain_ref[1:2, :] = rest[KV_WIDTH + LANES // 2 : KV_WIDTH + LANES // 2 + 1]


def assemble_call(info, mine, other):
    shares, height, total = mine.shape
    width = 2 * shares * height
    shapes = [(width, Q_WIDTH), (KVH * HD, width), (KVH * HD, width), (2, width)]
    return row_kernel_call(
        assemble_kernel,
        "assemble",
        1,
        [whole_spec(mine.shape)] * 2,
        [whole_spec(shape) for shape in shapes],
        [shape_of(shape, F32) for shape in shapes],
        [pltpu.VMEM((width, total), F32)],
        cost=cost_of(5),
    )(info, mine, other)


def interleave(keys, values):
    shape = keys.shape[:-1]
    pair = jnp.stack([keys.reshape(shape + (KVH, HD)), values.reshape(shape + (KVH, HD))], axis=-2)
    return pair.reshape(shape + (KV_WIDTH,))


def separate(pairs):
    shape = pairs.shape[:-1]
    split = pairs.reshape(shape + (KVH, 2, HD))
    return (
        split[..., 0, :].reshape(shape + (KVH * HD,)),
        split[..., 1, :].reshape(shape + (KVH * HD,)),
    )


def describe(lengths, start, place):
    rows = lengths.shape[0]
    index = jnp.arange(rows)
    ahead = (lengths[None, :] > lengths[:, None]) | (
        (lengths[None, :] == lengths[:, None]) & (index[None, :] < index[:, None])
    )
    rank = ahead.sum(axis=1)
    chosen = rank[None, :] == index[:, None]
    ordered = jnp.where(chosen, lengths[None, :], 0).sum(axis=1)
    slots = jnp.where(chosen, index[None, :], 0).sum(axis=1)
    return jnp.concatenate(
        [jnp.stack([start, place // 2, place % 2, lax.axis_index("batch")]), ordered, slots]
    ).astype(jnp.int32)


PLANS = ((4, 4, 3, 2), (4, 4, 4, 3), (4, 4, 4, 4))


def plan_of(rows, chips, quarters):
    size = rows // len(quarters)
    return [(i * size, size, -(-chips * q // 4) - 1) for i, q in enumerate(quarters)]


def plan_index(ordered, span):
    rows, chunks = ordered.shape[0], len(PLANS[0])
    needed = -(-ordered[:: rows // chunks] * 4 // span)
    _, count = place_of("batch", 1)
    for other in [exchange(needed, "batch", k) for k in range(1, count)]:
        needed = jnp.maximum(needed, other)
    index = len(PLANS) - 1
    for i in reversed(range(len(PLANS) - 1)):
        index = jnp.where(jnp.all(needed <= jnp.array(PLANS[i], jnp.int32)), i, index)
    return index


def hops(low, high, way):
    return [(2 * c + k, 2 * (c + way) + k) for c in range(low, high + 1) for k in range(2)]


def layer(quarters, info, x, dy, tables, gain_columns, queries, keys, w_qkv, weights):
    rows = x.shape[0]
    w_out, w_gate, w_up, w_down = weights
    mlp_weights = [w_out.T, w_out, w_gate.T, w_gate, w_up.T, w_up, w_down, w_down.T]
    seq = lax.axis_size("seq")
    chips = seq // 2
    cos, sin = tables
    gain_column, gain_mlp_column = gain_columns
    plan = plan_of(rows, chips, quarters)

    moving = [keys[first : first + count] for first, count, _ in plan]
    moving = lax.optimization_barrier(moving)
    kv = [[own, exchange(own, "seq", 1)] for own in moving]

    def hop(i, d):
        if d <= plan[i][2]:
            moving[i] = lax.ppermute(moving[i], "seq", hops(d - 1, plan[i][2] - 1, 1))
            kv[i].extend([moving[i], exchange(moving[i], "seq", 1)])

    for d in range(1, chips):
        hop(0, d)
        hop(1, d)
        hop(2, d)
        hop(3, d)
        if d == 2:
            moving[0] = after(moving[0], kv[2][:4], kv[3][:4])
            moving[1] = after(moving[1], mlp_weights)

    def forward(i, mixed, *others):
        q = after(queries, *others) if others else queries
        return forward_call(plan[i], rows, info, q, kv[i], mixed)

    lse = [None] * len(plan)
    mixed, lse[3] = forward(3, None)
    mixed, lse[2] = forward(2, mixed)
    mixed, lse[0] = forward(0, mixed)
    mixed, lse[1] = forward(1, mixed)

    layer_out, da, dmix, keep, send, grad_gain_mlp = mlp_call(
        info, x, mixed, dy, gain_mlp_column, mlp_weights
    )

    hidden_width = mlp_weights[3].shape[1]
    divided = 3 * hidden_width
    if divided % (chips * LANES):
        divided = 0
    sums = Sum(keep, send, divided)
    swaps, parts, flights, totals, dq = {}, {}, {}, {}, {}

    def backward(i, *others):
        l = after(lse[i], *others)
        dq[i], own, sibling = backward_call(plan[i], info, queries, dmix, mixed, l, cos, sin, kv[i])
        swaps[i] = (own, exchange(sibling, "seq", 1))
        return own

    def joined(i, *others):
        own, received = swaps.pop(i)
        parts[i] = add(after(own, *others), received)
        reach = plan[i][2]
        totals[i] = (reach, parts[i][reach])
        return parts[i]

    def send_back(i):
        d, total = totals[i]
        if d:
            flights[i] = lax.ppermute(total, "seq", hops(d, plan[i][2], -1))

    def received(i, *others):
        if i in flights:
            d, _ = totals[i]
            total = add(after(parts[i][d - 1], *others), flights.pop(i))
            totals[i] = (d - 1, total)
            return total
        return totals[i][1]

    sums.begin()
    now = backward(0)
    now = sums.end(now)
    sums.begin()
    now = backward(1, now)
    now = joined(0, now)
    send_back(0)
    now = sums.end(now)
    sums.begin()
    now = backward(2, now)
    now = received(0, now)
    send_back(0)
    now = joined(1, now)
    send_back(1)
    if divided:
        now = sums.end(now)
        sums.begin()
    now = backward(3, now)
    now = received(0, now)
    send_back(0)
    now = received(1, now)
    send_back(1)
    now = joined(2, now)
    now = joined(3, now)
    send_back(2)
    send_back(3)
    now = sums.end(now)
    sums.begin()
    while any(d for d, _ in totals.values()):
        for i in range(len(plan)):
            now = received(i, now)
            send_back(i)
    late_dq = jnp.concatenate([dq[i] for i in range(len(plan))], axis=0)
    late_dkv = jnp.concatenate([totals[i][1] for i in range(len(plan))], axis=0)
    dx, keep, send = qkv_back_call(
        info, x, da, late_dq, late_dkv, gain_column, w_qkv, cos, sin, grad_gain_mlp
    )
    late = Sum(keep, send, 0)
    late.begin()
    now = late.end()
    late.begin()
    now = sums.end(now)
    sums.begin()
    now = late.end(now)
    late.begin()
    pair = sums.end(now)
    if divided:
        grads = divided_call(info, *pair, chips, divided, 3)
    else:
        ends = [hidden_width, 2 * hidden_width, 3 * hidden_width]
        grads = jnp.split(whole_call(info, *pair), ends, axis=1)
    late.end(*grads)
    late.begin()
    late.end()
    late.begin()
    grad_gate, grad_up, grad_down, grad_out = grads
    grad_query, grad_key, grad_value, gains = assemble_call(info, *late.end())

    return (
        layer_out,
        dx,
        gains[0],
        grad_query,
        grad_key.T,
        grad_value.T,
        grad_out,
        gains[1],
        grad_gate,
        grad_up,
        grad_down.T,
    )


def body(
    tokens,
    lengths,
    gain_attn,
    w_query,
    w_key,
    w_value,
    w_out,
    gain_mlp,
    w_gate,
    w_up,
    w_down,
    cotangent,
):
    rows, local_len, _ = tokens.shape
    seq = lax.axis_size("seq")
    place = lax.axis_index("seq")
    start = place * local_len
    tables = rope_tables((start + jnp.arange(local_len, dtype=jnp.int32)).astype(F32))
    info = describe(lengths, start, place)
    w_qkv = jnp.concatenate([w_query, interleave(w_key, w_value)], axis=1)
    x = jnp.swapaxes(tokens, 1, 2)
    dy = jnp.swapaxes(cotangent, 1, 2)
    gains = gain_attn[:, None], gain_mlp[:, None]
    index = plan_index(info[LENGTHS : LENGTHS + rows], seq * local_len)
    queries, keys = qkv_call(info, x, gains[0], w_qkv.T, *tables)
    layer_out, dx, *grads = lax.switch(
        index,
        [functools.partial(layer, plan) for plan in PLANS],
        info,
        x,
        dy,
        tables,
        gains,
        queries,
        keys,
        w_qkv,
        [w_out, w_gate, w_up, w_down],
    )
    return jnp.swapaxes(layer_out, 1, 2), jnp.swapaxes(dx, 1, 2), *grads


def solution(mesh):
    split, copied = P("batch", "seq", None), P()
    in_specs = (split, P("batch")) + (copied,) * 9 + (split,)
    out_specs = (split, split) + (copied,) * 9
    return jax.shard_map(body, mesh=mesh, in_specs=in_specs, out_specs=out_specs, check_vma=False)
```

```python
import functools

import jax
import jax.numpy as jnp
from jax import lax
from jax.experimental import pallas as pl
from jax.experimental.pallas import tpu as pltpu
from jax.sharding import PartitionSpec as P

H = 9
KVH = 3
HD = 64
GROUP = H // KVH
Q_WIDTH = H * HD
KV_WIDTH = 2 * KVH * HD

EPSILON = 1e-05
ROPE_BASE = 10000.0
MASKED_SCORE = -1e30
BF16 = jnp.bfloat16
F32 = jnp.float32
VMEM_LIMIT = 56 * 1024 * 1024
LANES = 128

START, CHIP, CORE, BATCH, LENGTHS = 0, 1, 2, 3, 4


def dot(a, b, a_dim=1, b_dim=0):
    return lax.dot_general(a, b, (((a_dim,), (b_dim,)), ((), ())), preferred_element_type=F32)


def rope_tables(positions):
    freqs = ROPE_BASE ** (-(jnp.arange(HD // 2, dtype=F32) * 2.0) / HD)
    phases = freqs[:, None] * positions[None, :]
    return jnp.cos(phases), jnp.sin(phases)


def rope(block, cos, sin):
    u1, u2 = block[: HD // 2], block[HD // 2 :]
    return jnp.concatenate([u1 * cos - u2 * sin, u2 * cos + u1 * sin], axis=0)


def rope_back(block, cos, sin):
    u1, u2 = block[: HD // 2], block[HD // 2 :]
    return jnp.concatenate([u1 * cos + u2 * sin, u2 * cos - u1 * sin], axis=0)


def rms_scale(vectors):
    return lax.rsqrt(jnp.mean(vectors * vectors, axis=0, keepdims=True) + EPSILON)


def norm_back(grad_normed, normed, inv_scale):
    return inv_scale * (
        grad_normed - normed * jnp.mean(grad_normed * normed, axis=0, keepdims=True)
    )


def clear(ref):
    ref[...] = jnp.zeros_like(ref)


def row_spec(shape, first=0):
    return pl.BlockSpec((1,) + shape, lambda r, info: (first + r, 0, 0))


def slot_spec(shape, rows, first=0):
    return pl.BlockSpec((1,) + shape, lambda r, info: (info[LENGTHS + rows + first + r], 0, 0))


def whole_spec(shape):
    return pl.BlockSpec(
        shape, lambda r, info: (0,) * len(shape), pipeline_mode=pl.Buffered(buffer_count=1)
    )


def shape_of(shape, dtype=BF16):
    return jax.ShapeDtypeStruct(shape, dtype)


def cost_of(microseconds):
    return pl.CostEstimate(
        flops=int(microseconds * 8e8), bytes_accessed=int(microseconds * 1e6), transcendentals=0
    )


def row_kernel_call(
    kernel, name, rows, in_specs, out_specs, out_shape, scratch=(), cost=None, aliases=None
):
    return pl.pallas_call(
        kernel,
        grid_spec=pltpu.PrefetchScalarGridSpec(
            num_scalar_prefetch=1,
            grid=(rows,),
            in_specs=in_specs,
            out_specs=out_specs,
            scratch_shapes=scratch,
        ),
        out_shape=out_shape,
        compiler_params=pltpu.CompilerParams(vmem_limit_bytes=VMEM_LIMIT),
        cost_estimate=cost,
        input_output_aliases=aliases or {},
        name=name,
    )


def row_used(info, first=0):
    length = info[LENGTHS + first + pl.program_id(0)]
    return length, info[START] < length


def qkv_kernel(first, info, x_ref, gain_ref, w_query_ref, w_key_t_ref, w_value_t_ref, cos_ref, sin_ref, q_ref, kv_ref):
    _, used = row_used(info, first)

    @pl.when(used)
    def _():
        x = x_ref[0].astype(F32)
        normed = (x * rms_scale(x) * gain_ref[...]).astype(BF16)
        out = dot(w_query_ref[...], normed, 0, 0)
        cos, sin = cos_ref[...], sin_ref[...]
        for h in range(H):
            rotated = rope(out[h * HD : (h + 1) * HD], cos, sin)
            q_ref[0, h * HD : (h + 1) * HD, :] = (rotated * HD**-0.5).astype(BF16)
        out_key, out_value = dot(w_key_t_ref[...], normed), dot(w_value_t_ref[...], normed)
        for k in range(KVH):
            head, at = slice(k * HD, (k + 1) * HD), 2 * HD * k
            kv_ref[0, at : at + HD, :] = rope(out_key[head], cos, sin).astype(BF16)
            kv_ref[0, at + HD : at + 2 * HD, :] = out_value[head].astype(BF16)

    @pl.when(jnp.logical_not(used))
    def _():
        clear(q_ref)
        clear(kv_ref)


def qkv_call(info, tokens, gain, weights, cos, sin, first=0, count=None):
    rows, width, length = tokens.shape
    count = count or rows
    return row_kernel_call(
        functools.partial(qkv_kernel, first),
        "qkv",
        count,
        [
            slot_spec((width, length), rows, first),
            whole_spec(gain.shape),
        ]
        + [whole_spec(a.shape) for a in (*weights, cos, sin)],
        [row_spec((Q_WIDTH, length)), row_spec((KV_WIDTH, length))],
        [shape_of((count, Q_WIDTH, length)), shape_of((count, KV_WIDTH, length))],
        cost=cost_of(1.2 * count),
    )(info, tokens, gain, *weights, cos, sin)


def heads_of(ref, k):
    return jnp.concatenate(
        [ref[0, (k * GROUP + g) * HD : (k * GROUP + g + 1) * HD, :] for g in range(GROUP)], axis=1
    )


def key_value(kv_refs, block, k):
    ref, at = kv_refs[block], 2 * HD * k
    return ref[0, at : at + HD, :], ref[0, at + HD : at + 2 * HD, :]


def stack_spec(reach, length):
    return pl.BlockSpec((reach + 1, 1, KV_WIDTH, length), lambda r, info: (0, r, 0, 0))


def mask_diagonal(scores, start, length):
    size = scores.shape[0]
    key = lax.broadcasted_iota(jnp.int32, scores.shape, 0)
    query = lax.broadcasted_iota(jnp.int32, scores.shape, 1) % size
    allowed = jnp.logical_and(key <= query, start + key < length)
    return jnp.where(allowed, scores, MASKED_SCORE)


def visit_blocks(info, chips, visit):
    chip, core = info[CHIP], info[CORE]

    @pl.when(core == 0)
    def _():
        visit([(0, True)], True)

    @pl.when(core == 1)
    def _():
        visit([(0, True), (1, False)], True)

    for d in range(1, chips, 2):
        near = [(2 * d, False), (2 * d + 1, False)]

        if d + 1 < chips:

            @pl.when(chip > d)
            def _():
                visit(near + [(2 * d + 2, False), (2 * d + 3, False)], False)

        @pl.when((chip == d) if d + 1 < chips else (chip >= d))
        def _():
            visit(near, False)


def forward_kernel(chunk, info, q_ref, *refs):
    first_row, _, reach = chunk
    kv_refs = refs[: 2 * reach + 2]
    mixed_ref, lse_ref, peak_ref, total_ref, acc_ref = refs[-5:]
    length, used = row_used(info, first_row)
    start = info[START]

    def visit(blocks, first):
        def scores_of(k):
            queries = heads_of(q_ref, k)
            scores = []
            for b, diagonal in blocks:
                s = dot(key_value(kv_refs, b, k)[0], queries, 0, 0)
                scores.append(mask_diagonal(s, start, length) if diagonal else s)
            return scores

        ahead = [scores_of(k) for k in range(1)]
        for k in range(KVH):
            scores = ahead.pop(0)
            if k + 1 < KVH:
                ahead.append(scores_of(k + 1))
            peak = scores[0].max(axis=0, keepdims=True)
            for s in scores[1:]:
                peak = jnp.maximum(peak, s.max(axis=0, keepdims=True))
            if not first:
                old = peak_ref[k]
                peak = jnp.maximum(peak, old)
                shrink = jnp.exp(old - peak)
            total, acc = 0.0, 0.0
            for (b, _), s in zip(blocks, scores):
                weights = jnp.exp(s - peak)
                total = total + weights.sum(axis=0, keepdims=True)
                acc = acc + dot(key_value(kv_refs, b, k)[1], weights.astype(BF16))
            if not first:
                total = total + total_ref[k] * shrink
                acc = acc + acc_ref[k] * shrink
            peak_ref[k], total_ref[k], acc_ref[k] = peak, total, acc

    @pl.when(used)
    def _():
        visit_blocks(info, reach + 1, visit)
        size = q_ref.shape[2]
        for k in range(KVH):
            total = total_ref[k]
            out = (acc_ref[k] / total).astype(BF16)
            lse = peak_ref[k] + jnp.log(total)
            for g in range(GROUP):
                h = k * GROUP + g
                lse_ref[0, h : h + 1, :] = lse[:, g * size : (g + 1) * size]
                mixed_ref[0, h * HD : (h + 1) * HD, :] = out[:, g * size : (g + 1) * size]

    @pl.when(jnp.logical_not(used))
    def _():
        clear(mixed_ref)
        clear(lse_ref)


def forward_call(chunk, rows, info, queries, kv, mixed):
    first, count, reach = chunk
    length = queries.shape[2]
    earlier = [] if mixed is None else [mixed]
    return row_kernel_call(
        functools.partial(forward_kernel, chunk),
        "attention_forward",
        count,
        [row_spec((Q_WIDTH, length), first)]
        + [row_spec((KV_WIDTH, length))] * len(kv)
        + [pl.BlockSpec(memory_space=pl.ANY)] * len(earlier),
        [row_spec((Q_WIDTH, length), first), row_spec((H, length))],
        [shape_of((rows, Q_WIDTH, length)), shape_of((count, H, length), F32)],
        [
            pltpu.VMEM((KVH, 1, GROUP * length), F32),
            pltpu.VMEM((KVH, 1, GROUP * length), F32),
            pltpu.VMEM((KVH, HD, GROUP * length), F32),
        ],
        aliases={2 + len(kv): 0} if earlier else None,
        cost=cost_of(2.5 * count),
    )(info, queries, *kv, *earlier)


def backward_kernel(chunk, info, q_ref, dmix_ref, mixed_ref, lse_ref, cos_ref, sin_ref, *refs):
    first_row, _, reach = chunk
    kv_refs = refs[: 2 * reach + 2]
    dq_ref, *dkv_refs = refs[-5:-2]
    inner_ref, dq_acc_ref = refs[-2:]
    length, used = row_used(info, first_row)
    start, chip, core = info[START], info[CHIP], info[CORE]
    size = q_ref.shape[2]

    def visit(blocks, first):
        def products(k, b, diagonal):
            keys, values = key_value(kv_refs, b, k)
            s = dot(keys, heads_of(q_ref, k), 0, 0)
            if diagonal:
                s = mask_diagonal(s, start, length)
            return s, dot(values, heads_of(dmix_ref, k), 0, 0)

        work = [(k, b, diagonal) for k in range(KVH) for b, diagonal in blocks]
        ahead = products(*work[0])
        for n, (k, b, _) in enumerate(work):
            (s, dprobs), ahead = ahead, products(*work[n + 1]) if n + 1 < len(work) else None
            queries, dmix = heads_of(q_ref, k), heads_of(dmix_ref, k)
            lse = jnp.concatenate(
                [lse_ref[0, k * GROUP + g : k * GROUP + g + 1, :] for g in range(GROUP)], axis=1
            )
            probs = jnp.exp(s - lse)
            dscores = (probs * (dprobs - inner_ref[k])).astype(BF16)
            dq = dot(key_value(kv_refs, b, k)[0], dscores)
            if first and b == blocks[0][0]:
                dq_acc_ref[k] = dq
            else:
                dq_acc_ref[k] += dq
            at, out = 2 * HD * k, dkv_refs[b % 2]
            out[b // 2, 0, at : at + HD, :] = dot(queries, dscores, 1, 1).astype(BF16)
            out[b // 2, 0, at + HD : at + 2 * HD, :] = dot(dmix, probs.astype(BF16), 1, 1).astype(
                BF16
            )

    @pl.when(used)
    def _():
        for k in range(KVH):
            parts = []
            for g in range(GROUP):
                at = slice((k * GROUP + g) * HD, (k * GROUP + g + 1) * HD)
                product = dmix_ref[0, at, :].astype(F32) * mixed_ref[0, at, :].astype(F32)
                parts.append(product.sum(axis=0, keepdims=True))
            inner_ref[k] = jnp.concatenate(parts, axis=1)
        visit_blocks(info, reach + 1, visit)
        cos, sin = cos_ref[...], sin_ref[...]
        for k in range(KVH):
            dq = dq_acc_ref[k] * HD**-0.5
            for g in range(GROUP):
                h = k * GROUP + g
                dq_ref[0, h * HD : (h + 1) * HD, :] = rope_back(
                    dq[:, g * size : (g + 1) * size], cos, sin
                ).astype(BF16)

    unused = jnp.logical_not(used)

    def clear_block(b):
        dkv_refs[b % 2][b // 2] = jnp.zeros(dkv_refs[b % 2].shape[1:], BF16)

    @pl.when(unused)
    def _():
        clear(dq_ref)
        clear_block(0)

    @pl.when(jnp.logical_or(unused, core == 0))
    def _():
        clear_block(1)

    for d in range(1, reach + 1):

        @pl.when(jnp.logical_or(unused, chip < d))
        def _():
            clear_block(2 * d)
            clear_block(2 * d + 1)


def backward_call(chunk, info, queries, dmix, mixed, lse, cos, sin, kv):
    first, count, reach = chunk
    length = dmix.shape[2]
    return row_kernel_call(
        functools.partial(backward_kernel, chunk),
        "attention_backward",
        count,
        [
            row_spec((Q_WIDTH, length), first),
            row_spec((Q_WIDTH, length), first),
            row_spec((Q_WIDTH, length), first),
            row_spec((H, length)),
            whole_spec(cos.shape),
            whole_spec(sin.shape),
        ]
        + [row_spec((KV_WIDTH, length))] * len(kv),
        [row_spec((Q_WIDTH, length))] + [stack_spec(reach, length)] * 2,
        [shape_of((count, Q_WIDTH, length))]
        + [shape_of((reach + 1, count, KV_WIDTH, length))] * 2,
        [
            pltpu.VMEM((KVH, 1, GROUP * length), F32),
            pltpu.VMEM((KVH, HD, GROUP * length), F32),
        ],
        cost=cost_of(4 * count),
    )(info, queries, dmix, mixed, lse, cos, sin, *kv)


def write_halves(info, acc_refs, keep_ref, send_ref):
    at = 0
    for acc_ref in acc_refs:
        half, width = acc_ref.shape[0] // 2, acc_ref.shape[1]
        mine = pl.multiple_of(info[CORE] * half, 8)
        other = pl.multiple_of((1 - info[CORE]) * half, 8)
        keep_ref[:, at : at + width] = acc_ref[pl.ds(mine, half), :].astype(BF16)
        send_ref[:, at : at + width] = acc_ref[pl.ds(other, half), :].astype(BF16)
        at += width


def mlp_kernel(
    info,
    x_ref,
    mixed_ref,
    dy_ref,
    gain_ref,
    w_out_ref,
    w_gate_ref,
    w_up_ref,
    w_down_t_ref,
    out_ref,
    da_ref,
    dmix_ref,
    keep_ref,
    send_ref,
    grad_gain_ref,
    acc_ref,
    acc_out_ref,
    acc_gain_ref,
):
    length, used = row_used(info)
    row = pl.program_id(0)
    width, size = x_ref.shape[1:]
    hidden_width = w_gate_ref.shape[1]
    step = hidden_width // 2 if hidden_width % (2 * LANES) == 0 else hidden_width

    @pl.when(row == 0)
    def _():
        clear(acc_ref)
        clear(acc_out_ref)
        clear(acc_gain_ref)

    @pl.when(used)
    def _():
        mixed = mixed_ref[0]
        resid = x_ref[0].astype(F32) + dot(w_out_ref[...], mixed, 0, 0)
        scale = rms_scale(resid)
        normed = resid * scale
        mlp_in = (normed * gain_ref[...]).astype(BF16)
        position = info[START] + lax.broadcasted_iota(jnp.int32, (1, size), 1)
        valid = (position < length).astype(F32)
        dy_wide = dy_ref[0].astype(F32) * valid
        dy = dy_wide.astype(BF16)
        def products(at):
            part = slice(at, at + step)
            return (
                dot(w_gate_ref[:, part], mlp_in, 0, 0),
                dot(w_up_ref[:, part], mlp_in, 0, 0),
                dot(w_down_t_ref[:, part], dy, 0, 0),
            )

        out, grad_in = resid, None
        ahead = products(0)
        for at in range(0, hidden_width, step):
            part = slice(at, at + step)
            (gate, up, dhidden), ahead = ahead, None
            if at + step < hidden_width:
                ahead = products(at + step)
            sigmoid = 0.5 + 0.5 * jnp.tanh(0.5 * gate)
            activated = gate * sigmoid
            hidden = (activated * up).astype(BF16)
            dgate = (dhidden * up * (sigmoid + activated * (1.0 - sigmoid))).astype(BF16)
            dup = (dhidden * activated).astype(BF16)
            out = out + dot(w_down_t_ref[:, part], hidden)
            piece = dot(w_gate_ref[:, part], dgate) + dot(w_up_ref[:, part], dup)
            grad_in = piece if grad_in is None else grad_in + piece
            acc_ref[:, at : at + step] += dot(mlp_in, dgate, 1, 1)
            acc_ref[:, hidden_width + at : hidden_width + at + step] += dot(mlp_in, dup, 1, 1)
            acc_ref[:, 2 * hidden_width + at : 2 * hidden_width + at + step] += dot(
                dy, hidden, 1, 1
            )
        out_ref[0] = (out * valid).astype(BF16)
        acc_gain_ref[...] += grad_in * normed
        dresid = dy_wide + norm_back(grad_in * gain_ref[...], normed, scale)
        da = dresid.astype(BF16)
        da_ref[0] = da
        dmix_ref[0] = dot(w_out_ref[...], da).astype(BF16)
        acc_out_ref[...] += dot(mixed, da, 1, 1)

    @pl.when(jnp.logical_not(used))
    def _():
        clear(out_ref)
        clear(da_ref)
        clear(dmix_ref)

    @pl.when(row == pl.num_programs(0) - 1)
    def _():
        write_halves(info, [acc_ref, acc_out_ref], keep_ref, send_ref)
        grad_gain_ref[...] = jnp.broadcast_to(
            acc_gain_ref[...].sum(axis=1, keepdims=True), grad_gain_ref.shape
        )


def mlp_call(info, tokens, mixed, cotangent, gain, weights):
    rows, width, length = tokens.shape
    total = 3 * weights[1].shape[1]
    return row_kernel_call(
        mlp_kernel,
        "feed_forward",
        rows,
        [
            slot_spec((width, length), rows),
            row_spec((Q_WIDTH, length)),
            slot_spec((width, length), rows),
            whole_spec(gain.shape),
        ]
        + [whole_spec(w.shape) for w in weights],
        [
            slot_spec((width, length), rows),
            row_spec((width, length)),
            row_spec((Q_WIDTH, length)),
            whole_spec((width // 2, total + width)),
            whole_spec((width // 2, total + width)),
            whole_spec((width, LANES)),
        ],
        [
            shape_of((rows, width, length)),
            shape_of((rows, width, length)),
            shape_of((rows, Q_WIDTH, length)),
            shape_of((width // 2, total + width)),
            shape_of((width // 2, total + width)),
            shape_of((width, LANES), F32),
        ],
        [
            pltpu.VMEM((width, total), F32),
            pltpu.VMEM((Q_WIDTH, width), F32),
            pltpu.VMEM((width, length), F32),
        ],
        cost=cost_of(60),
    )(info, tokens, mixed, cotangent, gain, *weights)


def qkv_back_kernel(
    info,
    x_ref,
    da_ref,
    dq_ref,
    dkv_ref,
    gain_ref,
    w_query_ref,
    w_key_t_ref,
    w_value_t_ref,
    cos_ref,
    sin_ref,
    grad_gain_mlp_ref,
    dx_ref,
    keep_ref,
    send_ref,
    acc_ref,
    acc_gain_ref,
):
    _, used = row_used(info)
    row = pl.program_id(0)
    width = x_ref.shape[1]
    inner = Q_WIDTH + KV_WIDTH

    @pl.when(row == 0)
    def _():
        clear(acc_ref)
        clear(acc_gain_ref)

    @pl.when(used)
    def _():
        x = x_ref[0].astype(F32)
        scale = rms_scale(x)
        normed = x * scale
        attn_in = (normed * gain_ref[...]).astype(BF16)
        cos, sin = cos_ref[...], sin_ref[...]
        dq, dk, dv = dq_ref[0], [], []
        for k in range(KVH):
            at = 2 * HD * k
            dk.append(rope_back(dkv_ref[0, at : at + HD, :].astype(F32), cos, sin).astype(BF16))
            dv.append(dkv_ref[0, at + HD : at + 2 * HD, :])
        dk, dv = jnp.concatenate(dk, axis=0), jnp.concatenate(dv, axis=0)
        dn = dot(w_query_ref[...], dq)
        dn += dot(w_key_t_ref[...], dk, 0, 0) + dot(w_value_t_ref[...], dv, 0, 0)
        acc_ref[:, :Q_WIDTH] += dot(attn_in, dq, 1, 1)
        acc_ref[:, Q_WIDTH:inner] += dot(attn_in, jnp.concatenate([dk, dv], axis=0), 1, 1)
        acc_gain_ref[...] += dn * normed
        dx_ref[0] = (
            da_ref[0].astype(F32) + norm_back(dn * gain_ref[...], normed, scale)
        ).astype(BF16)

    @pl.when(jnp.logical_not(used))
    def _():
        clear(dx_ref)

    @pl.when(row == pl.num_programs(0) - 1)
    def _():
        lane = lax.broadcasted_iota(jnp.int32, (width, LANES), 1)
        acc_ref[:, inner:] = jnp.where(
            lane < LANES // 2,
            acc_gain_ref[...].sum(axis=1, keepdims=True),
            grad_gain_mlp_ref[...],
        )
        write_halves(info, [acc_ref], keep_ref, send_ref)


def qkv_back_call(info, tokens, da, dq, dkv, gain, weights, cos, sin, grad_gain_mlp):
    rows, width, length = tokens.shape
    total = Q_WIDTH + KV_WIDTH + LANES
    return row_kernel_call(
        qkv_back_kernel,
        "qkv_backward",
        rows,
        [
            slot_spec((width, length), rows),
            row_spec((width, length)),
            row_spec((Q_WIDTH, length)),
            row_spec((KV_WIDTH, length)),
        ]
        + [whole_spec(a.shape) for a in (gain, *weights, cos, sin, grad_gain_mlp)],
        [
            slot_spec((width, length), rows),
            whole_spec((width // 2, total)),
            whole_spec((width // 2, total)),
        ],
        [
            shape_of((rows, width, length)),
            shape_of((width // 2, total)),
            shape_of((width // 2, total)),
        ],
        [pltpu.VMEM((width, total), F32), pltpu.VMEM((width, length), F32)],
        cost=cost_of(14),
    )(info, tokens, da, dq, dkv, gain, *weights, cos, sin, grad_gain_mlp)


def exchange(array, axis, bits, low=1):
    size = lax.axis_size(axis)
    return lax.ppermute(array, axis, [(i, i ^ (bits * low)) for i in range(size)])


def add(*arrays):
    total = arrays[0].astype(F32)
    for array in arrays[1:]:
        total = total + array.astype(F32)
    return total.astype(BF16)


def place_of(axis, low):
    return lax.axis_index(axis) // low, lax.axis_size(axis) // low


def after(value, *others):
    return lax.optimization_barrier((value, others))[0]


class Sum:
    def __init__(self, keep, send, divided):
        self.keep, self.send, self.divided = keep, send, divided
        self.share = divided // (lax.axis_size("seq") // 2)
        self.steps = iter(
            [self.halve, self.over_batch, self.over_chips]
            + ([self.back_chips] if divided else [])
            + [self.back_batch, self.back_halves]
        )

    def begin(self):
        next(self.steps)()

    def end(self, *others):
        self.local = after(self.local, *others)
        self.array = self.finish(self.local, self.received)
        return self.array

    def arrived(self, number, *others):
        return after(self.received[number], *others)

    def added(self, local, received):
        return add(local, *received)

    def halve(self):
        self.local, self.received = self.keep, [exchange(self.send, "seq", 1)]
        self.finish = self.added

    def over_batch(self):
        me, count = place_of("batch", 1)
        share = self.array.shape[0] // count

        def part(index):
            return lax.dynamic_slice_in_dim(self.array, index * share, share, 0)

        self.received = [exchange(part(me ^ k), "batch", k) for k in range(1, count)]
        self.local, self.finish = part(me), self.added

    def over_chips(self):
        me, count = place_of("seq", 2)

        def part(index):
            if not self.divided:
                return self.array
            left = lax.dynamic_slice_in_dim(self.array, index * self.share, self.share, 1)
            return jnp.concatenate([left, self.array[:, self.divided :]], axis=1)

        self.received = [exchange(part(me ^ k), "seq", k, 2) for k in range(1, count)]
        self.local, self.finish = part(me), self.added

    def back_chips(self):
        _, count = place_of("seq", 2)
        left, right = self.array[:, : self.share], self.array[:, self.share :]
        self.received = [exchange(left, "seq", k, 2) for k in range(1, count)]
        self.local = left
        self.finish = lambda local, received: jnp.concatenate([local, *received, right], axis=1)

    def back_batch(self):
        _, count = place_of("batch", 1)
        self.received = [exchange(self.array, "batch", k) for k in range(1, count)]
        self.local = self.array
        self.finish = lambda local, received: jnp.stack([local, *received])

    def back_halves(self):
        self.local, self.received = self.array, exchange(self.array, "seq", 1)
        self.finish = lambda local, received: (local, received)


def select_core(info, mine_ref, other_ref, write):
    shares = pl.num_programs(0) // 2
    upper = (pl.program_id(0) >= shares).astype(jnp.int32)

    @pl.when(upper == info[CORE])
    def _():
        write(mine_ref)

    @pl.when(upper != info[CORE])
    def _():
        write(other_ref)


def share_specs(shape):
    shares = shape[0]
    rest = (0,) * (len(shape) - 1)

    def index(core, i, info):
        step = i - core * shares
        return (jnp.clip(step, 0, shares - 1) ^ info[BATCH],) + rest

    block = (1,) + tuple(shape[1:])
    return [
        pl.BlockSpec(block, lambda i, info: index(info[CORE], i, info)),
        pl.BlockSpec(block, lambda i, info: index(1 - info[CORE], i, info)),
    ]


def divided_kernel(chips, info, mine_ref, other_ref, *out_refs):
    out_width, rest = out_refs[0].shape[2], out_refs[-1].shape[2]
    width = (mine_ref.shape[2] - rest) // chips

    def write(ref):
        for q in range(chips):
            begin = pl.multiple_of((info[CHIP] ^ q) * width, LANES)
            share = ref[0, :, pl.ds(begin, width)].astype(F32)
            at = q * width
            while at < (q + 1) * width:
                out, column = divmod(at, out_width)
                size = min((q + 1) * width - at, out_width - column)
                begin = at - q * width
                out_refs[out][0, :, column : column + size] = share[:, begin : begin + size]
                at += size
        out_refs[-1][0] = ref[0, :, chips * width :].astype(F32)

    select_core(info, mine_ref, other_ref, write)


def divided_call(info, mine, other, chips, divided, count):
    shares, height, total = mine.shape
    widths = [divided // count] * count + [total - divided]
    out = row_kernel_call(
        functools.partial(divided_kernel, chips),
        "assemble_divided",
        2 * shares,
        share_specs(mine.shape),
        [pl.BlockSpec((1, height, w), lambda i, info: (i, 0, 0)) for w in widths],
        [shape_of((2 * shares, height, w), F32) for w in widths],
        cost=cost_of(8),
    )(info, mine, other)
    return [o.reshape(2 * shares * height, w) for o, w in zip(out, widths)]


def whole_kernel(info, mine_ref, other_ref, out_ref):
    def write(ref):
        out_ref[...] = ref[...].astype(F32)

    select_core(info, mine_ref, other_ref, write)


def whole_call(info, mine, other):
    shares, height, width = mine.shape
    out = row_kernel_call(
        whole_kernel,
        "assemble_whole",
        2 * shares,
        share_specs(mine.shape),
        pl.BlockSpec((1, height, width), lambda i, info: (i, 0, 0)),
        shape_of((2 * shares, height, width), F32),
        cost=cost_of(3),
    )(info, mine, other)
    return out.reshape(2 * shares * height, width)


def assemble_kernel(info, mine_ref, other_ref, query_ref, key_ref, value_ref, gain_ref, whole_ref):
    shares, height, _ = mine_ref.shape
    batch = info[BATCH]

    def write(half, ref):
        for j in range(shares):
            at = (half * shares + j) * height
            whole_ref[at : at + height, :] = ref[j ^ batch].astype(F32)

    @pl.when(info[CORE] == 0)
    def _():
        write(0, mine_ref)
        write(1, other_ref)

    @pl.when(info[CORE] == 1)
    def _():
        write(0, other_ref)
        write(1, mine_ref)

    query_ref[...] = whole_ref[:, :Q_WIDTH]
    rest = whole_ref[:, Q_WIDTH:].T
    key_ref[...] = rest[: KV_WIDTH // 2]
    value_ref[...] = rest[KV_WIDTH // 2 : KV_WIDTH]
    gain_ref[0:1, :] = rest[KV_WIDTH : KV_WIDTH + 1]
    gain_ref[1:2, :] = rest[KV_WIDTH + LANES // 2 : KV_WIDTH + LANES // 2 + 1]


def assemble_call(info, mine, other):
    shares, height, total = mine.shape
    width = 2 * shares * height
    shapes = [(width, Q_WIDTH), (KVH * HD, width), (KVH * HD, width), (2, width)]
    return row_kernel_call(
        assemble_kernel,
        "assemble",
        1,
        [whole_spec(mine.shape)] * 2,
        [whole_spec(shape) for shape in shapes],
        [shape_of(shape, F32) for shape in shapes],
        [pltpu.VMEM((width, total), F32)],
        cost=cost_of(5),
    )(info, mine, other)


def describe(lengths, start, place):
    rows = lengths.shape[0]
    index = jnp.arange(rows)
    ahead = (lengths[None, :] > lengths[:, None]) | (
        (lengths[None, :] == lengths[:, None]) & (index[None, :] < index[:, None])
    )
    rank = ahead.sum(axis=1)
    chosen = rank[None, :] == index[:, None]
    ordered = jnp.where(chosen, lengths[None, :], 0).sum(axis=1)
    slots = jnp.where(chosen, index[None, :], 0).sum(axis=1)
    return jnp.concatenate(
        [jnp.stack([start, place // 2, place % 2, lax.axis_index("batch")]), ordered, slots]
    ).astype(jnp.int32)


PLANS = ((4, 4, 3, 2), (4, 4, 4, 3), (4, 4, 4, 4))


def plan_of(rows, chips, quarters):
    size = rows // len(quarters)
    return [(i * size, size, -(-chips * q // 4) - 1) for i, q in enumerate(quarters)]


def plan_index(ordered, span):
    rows, chunks = ordered.shape[0], len(PLANS[0])
    needed = -(-ordered[:: rows // chunks] * 4 // span)
    _, count = place_of("batch", 1)
    for other in [exchange(needed, "batch", k) for k in range(1, count)]:
        needed = jnp.maximum(needed, other)
    index = len(PLANS) - 1
    for i in reversed(range(len(PLANS) - 1)):
        index = jnp.where(jnp.all(needed <= jnp.array(PLANS[i], jnp.int32)), i, index)
    return index


def hops(low, high, way):
    return [(2 * c + k, 2 * (c + way) + k) for c in range(low, high + 1) for k in range(2)]


def layer(quarters, info, x, dy, tables, gain_columns, queries, keys, qkv_weights, mlp_weights):
    rows = x.shape[0]
    seq = lax.axis_size("seq")
    chips = seq // 2
    cos, sin = tables
    gain_column, gain_mlp_column = gain_columns
    plan = plan_of(rows, chips, quarters)

    moving = [keys[first : first + count] for first, count, _ in plan]
    moving = lax.optimization_barrier(moving)
    kv = [[own, exchange(own, "seq", 1)] for own in moving]

    def hop(i, d):
        if d <= plan[i][2]:
            moving[i] = lax.ppermute(moving[i], "seq", hops(d - 1, plan[i][2] - 1, 1))
            kv[i].append(moving[i])
            if (i, d) != (1, chips - 1):
                kv[i].append(exchange(moving[i], "seq", 1))

    for d in range(1, chips):
        hop(0, d)
        hop(1, d)
        if d == 1:
            moving[2:] = after(moving[2:], moving[1])
        hop(2, d)
        hop(3, d)
        if d == 2:
            moving[0] = after(moving[0], kv[2][:4], kv[3][:4])

    def forward(i, mixed, *others):
        q = after(queries, *others) if others else queries
        return forward_call(plan[i], rows, info, q, kv[i], mixed)

    lse = [None] * len(plan)
    mixed, lse[3] = forward(3, None)
    mixed, lse[0] = forward(0, mixed)
    moving[1] = after(moving[1], lse[0])
    kv[1][2 * chips - 2 :] = [moving[1], exchange(moving[1], "seq", 1)]
    mixed, lse[2] = forward(2, mixed)
    mixed, lse[1] = forward(1, mixed)

    layer_out, da, dmix, keep, send, grad_gain_mlp = mlp_call(
        info, x, mixed, dy, gain_mlp_column, mlp_weights
    )

    hidden_width = mlp_weights[1].shape[1]
    divided = 3 * hidden_width
    if divided % (chips * LANES):
        divided = 0
    sums = Sum(keep, send, divided)
    swaps, parts, flights, totals, dq = {}, {}, {}, {}, {}

    def backward(i, *others):
        l = after(lse[i], *others)
        dq[i], own, sibling = backward_call(plan[i], info, queries, dmix, mixed, l, cos, sin, kv[i])
        swaps[i] = (own, exchange(sibling, "seq", 1))
        return own

    def joined(i, *others):
        own, received = swaps.pop(i)
        parts[i] = add(after(own, *others), received)
        reach = plan[i][2]
        totals[i] = (reach, parts[i][reach])
        return parts[i]

    def send_back(i):
        d, total = totals[i]
        if d:
            flights[i] = lax.ppermute(total, "seq", hops(d, plan[i][2], -1))

    def received(i, *others):
        if i in flights:
            d, _ = totals[i]
            total = add(after(parts[i][d - 1], *others), flights.pop(i))
            totals[i] = (d - 1, total)
            return total
        return totals[i][1]

    sums.begin()
    now = backward(0)
    now = sums.end(now)
    sums.begin()
    now = backward(1, now)
    now = joined(0, now)
    send_back(0)
    now = sums.end(now)
    sums.begin()
    now = backward(2, now)
    now = joined(1, now)
    now = received(0, now)
    send_back(0)
    send_back(1)
    now = sums.end(now)
    if divided:
        sums.begin()
    now = backward(3, now)
    now = received(0, now)
    now = received(1, now)
    send_back(0)
    send_back(1)
    now = joined(2, now)
    now = joined(3, now)
    if divided:
        now = sums.end(now)
    sums.begin()
    send_back(2)
    send_back(3)
    while any(d for d, _ in totals.values()):
        for i in range(len(plan)):
            now = received(i, now)
            send_back(i)
    late_dq = jnp.concatenate([dq[i] for i in range(len(plan))], axis=0)
    late_dkv = jnp.concatenate([totals[i][1] for i in range(len(plan))], axis=0)
    now = sums.end(late_dkv)
    sums.begin()
    late_dkv = after(late_dkv, now)
    dx, keep, send = qkv_back_call(
        info, x, da, late_dq, late_dkv, gain_column, qkv_weights, cos, sin, grad_gain_mlp
    )
    late = Sum(keep, send, 0)
    late.begin()
    now = late.end()
    pair = sums.end(now)
    late.begin()
    if divided:
        grads = divided_call(info, *pair, chips, divided, 3)
    else:
        ends = [hidden_width, 2 * hidden_width, 3 * hidden_width]
        grads = jnp.split(whole_call(info, *pair), ends, axis=1)
    late.end(*grads)
    late.begin()
    late.end()
    late.begin()
    late.end()
    late.begin()
    grad_gate, grad_up, grad_down, grad_out = grads
    grad_query, grad_key, grad_value, gains = assemble_call(info, *late.end())

    return (
        layer_out,
        dx,
        gains[0],
        grad_query,
        grad_key.T,
        grad_value.T,
        grad_out,
        gains[1],
        grad_gate,
        grad_up,
        grad_down.T,
    )


def body(
    tokens,
    lengths,
    gain_attn,
    w_query,
    w_key,
    w_value,
    w_out,
    gain_mlp,
    w_gate,
    w_up,
    w_down,
    cotangent,
):
    rows, local_len, _ = tokens.shape
    seq = lax.axis_size("seq")
    place = lax.axis_index("seq")
    start = place * local_len
    tables = rope_tables((start + jnp.arange(local_len, dtype=jnp.int32)).astype(F32))
    info = describe(lengths, start, place)
    qkv_weights = [w_query, w_key.T, w_value.T]
    x = jnp.swapaxes(tokens, 1, 2)
    dy = jnp.swapaxes(cotangent, 1, 2)
    gains = gain_attn[:, None], gain_mlp[:, None]
    index = plan_index(info[LENGTHS : LENGTHS + rows], seq * local_len)
    queries, keys = qkv_call(info, x, gains[0], qkv_weights, *tables)
    layer_out, dx, *grads = lax.switch(
        index,
        [functools.partial(layer, plan) for plan in PLANS],
        info,
        x,
        dy,
        tables,
        gains,
        queries,
        keys,
        qkv_weights,
        [w_out, w_gate, w_up, w_down.T],
    )
    return jnp.swapaxes(layer_out, 1, 2), jnp.swapaxes(dx, 1, 2), *grads


def solution(mesh):
    split, copied = P("batch", "seq", None), P()
    in_specs = (split, P("batch")) + (copied,) * 9 + (split,)
    out_specs = (split, split) + (copied,) * 9
    return jax.shard_map(body, mesh=mesh, in_specs=in_specs, out_specs=out_specs, check_vma=False)
```

```python
import functools

import jax
import jax.numpy as jnp
from jax import lax
from jax.experimental import pallas as pl
from jax.experimental.pallas import tpu as pltpu
from jax.sharding import PartitionSpec as P

H = 9
KVH = 3
HD = 64
GROUP = H // KVH
Q_WIDTH = H * HD
KV_WIDTH = 2 * KVH * HD

EPSILON = 1e-05
ROPE_BASE = 10000.0
MASKED_SCORE = -1e30
BF16 = jnp.bfloat16
F32 = jnp.float32
VMEM_LIMIT = 56 * 1024 * 1024
LANES = 128

START, CHIP, CORE, BATCH, LENGTHS = 0, 1, 2, 3, 4


def dot(a, b, a_dim=1, b_dim=0):
    return lax.dot_general(a, b, (((a_dim,), (b_dim,)), ((), ())), preferred_element_type=F32)


def rope_tables(positions):
    freqs = ROPE_BASE ** (-(jnp.arange(HD // 2, dtype=F32) * 2.0) / HD)
    phases = freqs[:, None] * positions[None, :]
    return jnp.cos(phases), jnp.sin(phases)


def rope(block, cos, sin):
    u1, u2 = block[: HD // 2], block[HD // 2 :]
    return jnp.concatenate([u1 * cos - u2 * sin, u2 * cos + u1 * sin], axis=0)


def rope_back(block, cos, sin):
    u1, u2 = block[: HD // 2], block[HD // 2 :]
    return jnp.concatenate([u1 * cos + u2 * sin, u2 * cos - u1 * sin], axis=0)


def rms_scale(vectors):
    return lax.rsqrt(jnp.mean(vectors * vectors, axis=0, keepdims=True) + EPSILON)


def norm_back(grad_normed, normed, inv_scale):
    return inv_scale * (
        grad_normed - normed * jnp.mean(grad_normed * normed, axis=0, keepdims=True)
    )


def clear(ref):
    ref[...] = jnp.zeros_like(ref)


def row_spec(shape, first=0):
    return pl.BlockSpec((1,) + shape, lambda r, info: (first + r, 0, 0))


def kv_spec(array):
    return pl.BlockSpec(
        (1,) + array.shape[1:], lambda r, info: (jnp.minimum(r, array.shape[0] - 1), 0, 0)
    )


def slot_spec(shape, rows, first=0):
    return pl.BlockSpec((1,) + shape, lambda r, info: (info[LENGTHS + rows + first + r], 0, 0))


def whole_spec(shape):
    return pl.BlockSpec(
        shape, lambda r, info: (0,) * len(shape), pipeline_mode=pl.Buffered(buffer_count=1)
    )


def shape_of(shape, dtype=BF16):
    return jax.ShapeDtypeStruct(shape, dtype)


def cost_of(microseconds):
    return pl.CostEstimate(
        flops=int(microseconds * 8e8), bytes_accessed=int(microseconds * 1e6), transcendentals=0
    )


def row_kernel_call(
    kernel, name, rows, in_specs, out_specs, out_shape, scratch=(), cost=None, aliases=None
):
    return pl.pallas_call(
        kernel,
        grid_spec=pltpu.PrefetchScalarGridSpec(
            num_scalar_prefetch=1,
            grid=(rows,),
            in_specs=in_specs,
            out_specs=out_specs,
            scratch_shapes=scratch,
        ),
        out_shape=out_shape,
        compiler_params=pltpu.CompilerParams(vmem_limit_bytes=VMEM_LIMIT),
        cost_estimate=cost,
        input_output_aliases=aliases or {},
        name=name,
    )


def row_used(info, first=0):
    length = info[LENGTHS + first + pl.program_id(0)]
    return length, info[START] < length


def qkv_kernel(first, info, x_ref, gain_ref, w_query_ref, w_key_t_ref, w_value_t_ref, cos_ref, sin_ref, q_ref, kv_ref):
    _, used = row_used(info, first)

    @pl.when(used)
    def _():
        x = x_ref[0].astype(F32)
        normed = (x * rms_scale(x) * gain_ref[...]).astype(BF16)
        out = dot(w_query_ref[...], normed, 0, 0)
        cos, sin = cos_ref[...], sin_ref[...]
        for h in range(H):
            rotated = rope(out[h * HD : (h + 1) * HD], cos, sin)
            q_ref[0, h * HD : (h + 1) * HD, :] = (rotated * HD**-0.5).astype(BF16)
        out_key, out_value = dot(w_key_t_ref[...], normed), dot(w_value_t_ref[...], normed)
        for k in range(KVH):
            head, at = slice(k * HD, (k + 1) * HD), 2 * HD * k
            kv_ref[0, at : at + HD, :] = rope(out_key[head], cos, sin).astype(BF16)
            kv_ref[0, at + HD : at + 2 * HD, :] = out_value[head].astype(BF16)

    @pl.when(jnp.logical_not(used))
    def _():
        clear(q_ref)
        clear(kv_ref)


def qkv_call(info, tokens, gain, weights, cos, sin, first=0, count=None):
    rows, width, length = tokens.shape
    count = count or rows
    return row_kernel_call(
        functools.partial(qkv_kernel, first),
        "qkv",
        count,
        [
            slot_spec((width, length), rows, first),
            whole_spec(gain.shape),
        ]
        + [whole_spec(a.shape) for a in (*weights, cos, sin)],
        [row_spec((Q_WIDTH, length)), row_spec((KV_WIDTH, length))],
        [shape_of((count, Q_WIDTH, length)), shape_of((count, KV_WIDTH, length))],
        cost=cost_of(1.2 * count),
    )(info, tokens, gain, *weights, cos, sin)


def heads_of(ref, k):
    return jnp.concatenate(
        [ref[0, (k * GROUP + g) * HD : (k * GROUP + g + 1) * HD, :] for g in range(GROUP)], axis=1
    )


def key_value(kv_refs, block, k):
    ref, at = kv_refs[block], 2 * HD * k
    return ref[0, at : at + HD, :], ref[0, at + HD : at + 2 * HD, :]


def stack_spec(reach, length):
    return pl.BlockSpec((reach + 1, 1, KV_WIDTH, length), lambda r, info: (0, r, 0, 0))


def mask_diagonal(scores, start, length):
    size = scores.shape[0]
    key = lax.broadcasted_iota(jnp.int32, scores.shape, 0)
    query = lax.broadcasted_iota(jnp.int32, scores.shape, 1) % size
    allowed = jnp.logical_and(key <= query, start + key < length)
    return jnp.where(allowed, scores, MASKED_SCORE)


def visit_blocks(info, chips, visit):
    chip, core = info[CHIP], info[CORE]

    @pl.when(core == 0)
    def _():
        visit([(0, True)], True)

    @pl.when(core == 1)
    def _():
        visit([(0, True), (1, False)], True)

    for d in range(1, chips, 2):
        near = [(2 * d, False), (2 * d + 1, False)]

        if d + 1 < chips:

            @pl.when(chip > d)
            def _():
                visit(near + [(2 * d + 2, False), (2 * d + 3, False)], False)

        @pl.when((chip == d) if d + 1 < chips else (chip >= d))
        def _():
            visit(near, False)


def forward_kernel(chunk, info, q_ref, *refs):
    first_row, _, reach = chunk
    kv_refs = refs[: 2 * reach + 2]
    mixed_ref, lse_ref, peak_ref, total_ref, acc_ref = refs[-5:]
    length, used = row_used(info, first_row)
    start = info[START]

    def visit(blocks, first):
        def scores_of(k):
            queries = heads_of(q_ref, k)
            scores = []
            for b, diagonal in blocks:
                s = dot(key_value(kv_refs, b, k)[0], queries, 0, 0)
                scores.append(mask_diagonal(s, start, length) if diagonal else s)
            return scores

        ahead = [scores_of(k) for k in range(1)]
        for k in range(KVH):
            scores = ahead.pop(0)
            if k + 1 < KVH:
                ahead.append(scores_of(k + 1))
            peak = scores[0].max(axis=0, keepdims=True)
            for s in scores[1:]:
                peak = jnp.maximum(peak, s.max(axis=0, keepdims=True))
            if not first:
                old = peak_ref[k]
                peak = jnp.maximum(peak, old)
                shrink = jnp.exp(old - peak)
            total, acc = 0.0, 0.0
            for (b, _), s in zip(blocks, scores):
                weights = jnp.exp(s - peak)
                total = total + weights.sum(axis=0, keepdims=True)
                acc = acc + dot(key_value(kv_refs, b, k)[1], weights.astype(BF16))
            if not first:
                total = total + total_ref[k] * shrink
                acc = acc + acc_ref[k] * shrink
            peak_ref[k], total_ref[k], acc_ref[k] = peak, total, acc

    @pl.when(used)
    def _():
        visit_blocks(info, reach + 1, visit)
        size = q_ref.shape[2]
        for k in range(KVH):
            total = total_ref[k]
            out = (acc_ref[k] / total).astype(BF16)
            lse = peak_ref[k] + jnp.log(total)
            for g in range(GROUP):
                h = k * GROUP + g
                lse_ref[0, h : h + 1, :] = lse[:, g * size : (g + 1) * size]
                mixed_ref[0, h * HD : (h + 1) * HD, :] = out[:, g * size : (g + 1) * size]

    @pl.when(jnp.logical_not(used))
    def _():
        clear(mixed_ref)
        clear(lse_ref)


def forward_call(chunk, rows, info, queries, kv, mixed):
    first, count, reach = chunk
    length = queries.shape[2]
    earlier = [] if mixed is None else [mixed]
    return row_kernel_call(
        functools.partial(forward_kernel, chunk),
        "attention_forward",
        count,
        [row_spec((Q_WIDTH, length), first)]
        + [kv_spec(a) for a in kv]
        + [pl.BlockSpec(memory_space=pl.ANY)] * len(earlier),
        [row_spec((Q_WIDTH, length), first), row_spec((H, length))],
        [shape_of((rows, Q_WIDTH, length)), shape_of((count, H, length), F32)],
        [
            pltpu.VMEM((KVH, 1, GROUP * length), F32),
            pltpu.VMEM((KVH, 1, GROUP * length), F32),
            pltpu.VMEM((KVH, HD, GROUP * length), F32),
        ],
        aliases={2 + len(kv): 0} if earlier else None,
        cost=cost_of(2.5 * count),
    )(info, queries, *kv, *earlier)


def backward_kernel(chunk, info, q_ref, dmix_ref, mixed_ref, lse_ref, cos_ref, sin_ref, *refs):
    first_row, _, reach = chunk
    kv_refs = refs[: 2 * reach + 2]
    dq_ref, *dkv_refs = refs[-5:-2]
    inner_ref, dq_acc_ref = refs[-2:]
    length, used = row_used(info, first_row)
    start, chip, core = info[START], info[CHIP], info[CORE]
    size = q_ref.shape[2]

    def visit(blocks, first):
        def products(k, b, diagonal):
            keys, values = key_value(kv_refs, b, k)
            s = dot(keys, heads_of(q_ref, k), 0, 0)
            if diagonal:
                s = mask_diagonal(s, start, length)
            return s, dot(values, heads_of(dmix_ref, k), 0, 0)

        work = [(k, b, diagonal) for k in range(KVH) for b, diagonal in blocks]
        ahead = products(*work[0])
        for n, (k, b, _) in enumerate(work):
            (s, dprobs), ahead = ahead, products(*work[n + 1]) if n + 1 < len(work) else None
            queries, dmix = heads_of(q_ref, k), heads_of(dmix_ref, k)
            lse = jnp.concatenate(
                [lse_ref[0, k * GROUP + g : k * GROUP + g + 1, :] for g in range(GROUP)], axis=1
            )
            probs = jnp.exp(s - lse)
            dscores = (probs * (dprobs - inner_ref[k])).astype(BF16)
            dq = dot(key_value(kv_refs, b, k)[0], dscores)
            if first and b == blocks[0][0]:
                dq_acc_ref[k] = dq
            else:
                dq_acc_ref[k] += dq
            at, out = 2 * HD * k, dkv_refs[b % 2]
            out[b // 2, 0, at : at + HD, :] = dot(queries, dscores, 1, 1).astype(BF16)
            out[b // 2, 0, at + HD : at + 2 * HD, :] = dot(dmix, probs.astype(BF16), 1, 1).astype(
                BF16
            )

    @pl.when(used)
    def _():
        for k in range(KVH):
            parts = []
            for g in range(GROUP):
                at = slice((k * GROUP + g) * HD, (k * GROUP + g + 1) * HD)
                product = dmix_ref[0, at, :].astype(F32) * mixed_ref[0, at, :].astype(F32)
                parts.append(product.sum(axis=0, keepdims=True))
            inner_ref[k] = jnp.concatenate(parts, axis=1)
        visit_blocks(info, reach + 1, visit)
        cos, sin = cos_ref[...], sin_ref[...]
        for k in range(KVH):
            dq = dq_acc_ref[k] * HD**-0.5
            for g in range(GROUP):
                h = k * GROUP + g
                dq_ref[0, h * HD : (h + 1) * HD, :] = rope_back(
                    dq[:, g * size : (g + 1) * size], cos, sin
                ).astype(BF16)

    unused = jnp.logical_not(used)

    def clear_block(b):
        dkv_refs[b % 2][b // 2] = jnp.zeros(dkv_refs[b % 2].shape[1:], BF16)

    @pl.when(unused)
    def _():
        clear(dq_ref)
        clear_block(0)

    @pl.when(jnp.logical_or(unused, core == 0))
    def _():
        clear_block(1)

    for d in range(1, reach + 1):

        @pl.when(jnp.logical_or(unused, chip < d))
        def _():
            clear_block(2 * d)
            clear_block(2 * d + 1)


def backward_call(chunk, info, queries, dmix, mixed, lse, cos, sin, kv):
    first, count, reach = chunk
    length = dmix.shape[2]
    return row_kernel_call(
        functools.partial(backward_kernel, chunk),
        "attention_backward",
        count,
        [
            row_spec((Q_WIDTH, length), first),
            row_spec((Q_WIDTH, length), first),
            row_spec((Q_WIDTH, length), first),
            row_spec((H, length)),
            whole_spec(cos.shape),
            whole_spec(sin.shape),
        ]
        + [kv_spec(a) for a in kv],
        [row_spec((Q_WIDTH, length))] + [stack_spec(reach, length)] * 2,
        [shape_of((count, Q_WIDTH, length))]
        + [shape_of((reach + 1, count, KV_WIDTH, length))] * 2,
        [
            pltpu.VMEM((KVH, 1, GROUP * length), F32),
            pltpu.VMEM((KVH, HD, GROUP * length), F32),
        ],
        cost=cost_of(4 * count),
    )(info, queries, dmix, mixed, lse, cos, sin, *kv)


def write_halves(info, acc_refs, keep_ref, send_ref):
    at = 0
    for acc_ref in acc_refs:
        half, width = acc_ref.shape[0] // 2, acc_ref.shape[1]
        mine = pl.multiple_of(info[CORE] * half, 8)
        other = pl.multiple_of((1 - info[CORE]) * half, 8)
        keep_ref[:, at : at + width] = acc_ref[pl.ds(mine, half), :].astype(BF16)
        send_ref[:, at : at + width] = acc_ref[pl.ds(other, half), :].astype(BF16)
        at += width


def mlp_kernel(
    info,
    x_ref,
    mixed_ref,
    dy_ref,
    gain_ref,
    w_out_ref,
    w_gate_ref,
    w_up_ref,
    w_down_t_ref,
    out_ref,
    da_ref,
    dmix_ref,
    keep_ref,
    send_ref,
    grad_gain_ref,
    acc_ref,
    acc_out_ref,
    acc_gain_ref,
):
    length, used = row_used(info)
    row = pl.program_id(0)
    width, size = x_ref.shape[1:]
    hidden_width = w_gate_ref.shape[1]
    step = hidden_width // 2 if hidden_width % (2 * LANES) == 0 else hidden_width

    @pl.when(row == 0)
    def _():
        clear(acc_ref)
        clear(acc_out_ref)
        clear(acc_gain_ref)

    @pl.when(used)
    def _():
        mixed = mixed_ref[0]
        resid = x_ref[0].astype(F32) + dot(w_out_ref[...], mixed, 0, 0)
        scale = rms_scale(resid)
        normed = resid * scale
        mlp_in = (normed * gain_ref[...]).astype(BF16)
        position = info[START] + lax.broadcasted_iota(jnp.int32, (1, size), 1)
        valid = (position < length).astype(F32)
        dy_wide = dy_ref[0].astype(F32) * valid
        dy = dy_wide.astype(BF16)
        def products(at):
            part = slice(at, at + step)
            return (
                dot(w_gate_ref[:, part], mlp_in, 0, 0),
                dot(w_up_ref[:, part], mlp_in, 0, 0),
                dot(w_down_t_ref[:, part], dy, 0, 0),
            )

        out, grad_in = resid, None
        ahead = products(0)
        for at in range(0, hidden_width, step):
            part = slice(at, at + step)
            (gate, up, dhidden), ahead = ahead, None
            if at + step < hidden_width:
                ahead = products(at + step)
            sigmoid = 0.5 + 0.5 * jnp.tanh(0.5 * gate)
            activated = gate * sigmoid
            hidden = (activated * up).astype(BF16)
            dgate = (dhidden * up * (sigmoid + activated * (1.0 - sigmoid))).astype(BF16)
            dup = (dhidden * activated).astype(BF16)
            out = out + dot(w_down_t_ref[:, part], hidden)
            piece = dot(w_gate_ref[:, part], dgate) + dot(w_up_ref[:, part], dup)
            grad_in = piece if grad_in is None else grad_in + piece
            acc_ref[:, at : at + step] += dot(mlp_in, dgate, 1, 1)
            acc_ref[:, hidden_width + at : hidden_width + at + step] += dot(mlp_in, dup, 1, 1)
            acc_ref[:, 2 * hidden_width + at : 2 * hidden_width + at + step] += dot(
                dy, hidden, 1, 1
            )
        out_ref[0] = (out * valid).astype(BF16)
        acc_gain_ref[...] += grad_in * normed
        dresid = dy_wide + norm_back(grad_in * gain_ref[...], normed, scale)
        da = dresid.astype(BF16)
        da_ref[0] = da
        dmix_ref[0] = dot(w_out_ref[...], da).astype(BF16)
        acc_out_ref[...] += dot(mixed, da, 1, 1)

    @pl.when(jnp.logical_not(used))
    def _():
        clear(out_ref)
        clear(da_ref)
        clear(dmix_ref)

    @pl.when(row == pl.num_programs(0) - 1)
    def _():
        write_halves(info, [acc_ref, acc_out_ref], keep_ref, send_ref)
        grad_gain_ref[...] = jnp.broadcast_to(
            acc_gain_ref[...].sum(axis=1, keepdims=True), grad_gain_ref.shape
        )


def mlp_call(info, tokens, mixed, cotangent, gain, weights):
    rows, width, length = tokens.shape
    total = 3 * weights[1].shape[1]
    return row_kernel_call(
        mlp_kernel,
        "feed_forward",
        rows,
        [
            slot_spec((width, length), rows),
            row_spec((Q_WIDTH, length)),
            slot_spec((width, length), rows),
            whole_spec(gain.shape),
        ]
        + [whole_spec(w.shape) for w in weights],
        [
            slot_spec((width, length), rows),
            row_spec((width, length)),
            row_spec((Q_WIDTH, length)),
            whole_spec((width // 2, total + width)),
            whole_spec((width // 2, total + width)),
            whole_spec((width, LANES)),
        ],
        [
            shape_of((rows, width, length)),
            shape_of((rows, width, length)),
            shape_of((rows, Q_WIDTH, length)),
            shape_of((width // 2, total + width)),
            shape_of((width // 2, total + width)),
            shape_of((width, LANES), F32),
        ],
        [
            pltpu.VMEM((width, total), F32),
            pltpu.VMEM((Q_WIDTH, width), F32),
            pltpu.VMEM((width, length), F32),
        ],
        cost=cost_of(60),
    )(info, tokens, mixed, cotangent, gain, *weights)


def qkv_back_kernel(
    info,
    x_ref,
    da_ref,
    dq_ref,
    dkv_ref,
    gain_ref,
    w_query_ref,
    w_key_t_ref,
    w_value_t_ref,
    cos_ref,
    sin_ref,
    grad_gain_mlp_ref,
    dx_ref,
    keep_ref,
    send_ref,
    acc_ref,
    acc_gain_ref,
):
    _, used = row_used(info)
    row = pl.program_id(0)
    width = x_ref.shape[1]
    inner = Q_WIDTH + KV_WIDTH

    @pl.when(row == 0)
    def _():
        clear(acc_ref)
        clear(acc_gain_ref)

    @pl.when(used)
    def _():
        x = x_ref[0].astype(F32)
        scale = rms_scale(x)
        normed = x * scale
        attn_in = (normed * gain_ref[...]).astype(BF16)
        cos, sin = cos_ref[...], sin_ref[...]
        dq, dk, dv = dq_ref[0], [], []
        for k in range(KVH):
            at = 2 * HD * k
            dk.append(rope_back(dkv_ref[0, at : at + HD, :].astype(F32), cos, sin).astype(BF16))
            dv.append(dkv_ref[0, at + HD : at + 2 * HD, :])
        dk, dv = jnp.concatenate(dk, axis=0), jnp.concatenate(dv, axis=0)
        dn = dot(w_query_ref[...], dq)
        dn += dot(w_key_t_ref[...], dk, 0, 0) + dot(w_value_t_ref[...], dv, 0, 0)
        acc_ref[:, :Q_WIDTH] += dot(attn_in, dq, 1, 1)
        acc_ref[:, Q_WIDTH:inner] += dot(attn_in, jnp.concatenate([dk, dv], axis=0), 1, 1)
        acc_gain_ref[...] += dn * normed
        dx_ref[0] = (
            da_ref[0].astype(F32) + norm_back(dn * gain_ref[...], normed, scale)
        ).astype(BF16)

    @pl.when(jnp.logical_not(used))
    def _():
        clear(dx_ref)

    @pl.when(row == pl.num_programs(0) - 1)
    def _():
        lane = lax.broadcasted_iota(jnp.int32, (width, LANES), 1)
        acc_ref[:, inner:] = jnp.where(
            lane < LANES // 2,
            acc_gain_ref[...].sum(axis=1, keepdims=True),
            grad_gain_mlp_ref[...],
        )
        write_halves(info, [acc_ref], keep_ref, send_ref)


def qkv_back_call(info, tokens, da, dq, dkv, gain, weights, cos, sin, grad_gain_mlp):
    rows, width, length = tokens.shape
    total = Q_WIDTH + KV_WIDTH + LANES
    return row_kernel_call(
        qkv_back_kernel,
        "qkv_backward",
        rows,
        [
            slot_spec((width, length), rows),
            row_spec((width, length)),
            row_spec((Q_WIDTH, length)),
            row_spec((KV_WIDTH, length)),
        ]
        + [whole_spec(a.shape) for a in (gain, *weights, cos, sin, grad_gain_mlp)],
        [
            slot_spec((width, length), rows),
            whole_spec((width // 2, total)),
            whole_spec((width // 2, total)),
        ],
        [
            shape_of((rows, width, length)),
            shape_of((width // 2, total)),
            shape_of((width // 2, total)),
        ],
        [pltpu.VMEM((width, total), F32), pltpu.VMEM((width, length), F32)],
        cost=cost_of(14),
    )(info, tokens, da, dq, dkv, gain, *weights, cos, sin, grad_gain_mlp)


def exchange(array, axis, bits, low=1):
    size = lax.axis_size(axis)
    return lax.ppermute(array, axis, [(i, i ^ (bits * low)) for i in range(size)])


def add(*arrays):
    total = arrays[0].astype(F32)
    for array in arrays[1:]:
        total = total + array.astype(F32)
    return total.astype(BF16)


def place_of(axis, low):
    return lax.axis_index(axis) // low, lax.axis_size(axis) // low


def after(value, *others):
    return lax.optimization_barrier((value, others))[0]


class Sum:
    def __init__(self, keep, send, divided):
        self.keep, self.send, self.divided = keep, send, divided
        self.share = divided // (lax.axis_size("seq") // 2)
        self.steps = iter(
            [self.halve, self.over_batch, self.over_chips]
            + ([self.back_chips] if divided else [])
            + [self.back_batch, self.back_halves]
        )

    def begin(self):
        next(self.steps)()

    def end(self, *others):
        self.local = after(self.local, *others)
        self.array = self.finish(self.local, self.received)
        return self.array

    def arrived(self, number, *others):
        return after(self.received[number], *others)

    def added(self, local, received):
        return add(local, *received)

    def halve(self):
        self.local, self.received = self.keep, [exchange(self.send, "seq", 1)]
        self.finish = self.added

    def over_batch(self):
        me, count = place_of("batch", 1)
        share = self.array.shape[0] // count

        def part(index):
            return lax.dynamic_slice_in_dim(self.array, index * share, share, 0)

        self.received = [exchange(part(me ^ k), "batch", k) for k in range(1, count)]
        self.local, self.finish = part(me), self.added

    def over_chips(self):
        me, count = place_of("seq", 2)

        def part(index):
            if not self.divided:
                return self.array
            left = lax.dynamic_slice_in_dim(self.array, index * self.share, self.share, 1)
            return jnp.concatenate([left, self.array[:, self.divided :]], axis=1)

        self.received = [exchange(part(me ^ k), "seq", k, 2) for k in range(1, count)]
        self.local, self.finish = part(me), self.added

    def back_chips(self):
        _, count = place_of("seq", 2)
        left, right = self.array[:, : self.share], self.array[:, self.share :]
        self.received = [exchange(left, "seq", k, 2) for k in range(1, count)]
        self.local = left
        self.finish = lambda local, received: jnp.concatenate([local, *received, right], axis=1)

    def back_batch(self):
        _, count = place_of("batch", 1)
        self.received = [exchange(self.array, "batch", k) for k in range(1, count)]
        self.local = self.array
        self.finish = lambda local, received: jnp.stack([local, *received])

    def back_halves(self):
        self.local, self.received = self.array, exchange(self.array, "seq", 1)
        self.finish = lambda local, received: (local, received)


def select_core(info, mine_ref, other_ref, write):
    shares = pl.num_programs(0) // 2
    upper = (pl.program_id(0) >= shares).astype(jnp.int32)

    @pl.when(upper == info[CORE])
    def _():
        write(mine_ref)

    @pl.when(upper != info[CORE])
    def _():
        write(other_ref)


def share_specs(shape):
    shares = shape[0]
    rest = (0,) * (len(shape) - 1)

    def index(core, i, info):
        step = i - core * shares
        return (jnp.clip(step, 0, shares - 1) ^ info[BATCH],) + rest

    block = (1,) + tuple(shape[1:])
    return [
        pl.BlockSpec(block, lambda i, info: index(info[CORE], i, info)),
        pl.BlockSpec(block, lambda i, info: index(1 - info[CORE], i, info)),
    ]


def divided_kernel(chips, info, mine_ref, other_ref, *out_refs):
    out_width, rest = out_refs[0].shape[2], out_refs[-1].shape[2]
    width = (mine_ref.shape[2] - rest) // chips

    def write(ref):
        for q in range(chips):
            begin = pl.multiple_of((info[CHIP] ^ q) * width, LANES)
            share = ref[0, :, pl.ds(begin, width)].astype(F32)
            at = q * width
            while at < (q + 1) * width:
                out, column = divmod(at, out_width)
                size = min((q + 1) * width - at, out_width - column)
                begin = at - q * width
                out_refs[out][0, :, column : column + size] = share[:, begin : begin + size]
                at += size
        out_refs[-1][0] = ref[0, :, chips * width :].astype(F32)

    select_core(info, mine_ref, other_ref, write)


def divided_call(info, mine, other, chips, divided, count):
    shares, height, total = mine.shape
    widths = [divided // count] * count + [total - divided]
    out = row_kernel_call(
        functools.partial(divided_kernel, chips),
        "assemble_divided",
        2 * shares,
        share_specs(mine.shape),
        [pl.BlockSpec((1, height, w), lambda i, info: (i, 0, 0)) for w in widths],
        [shape_of((2 * shares, height, w), F32) for w in widths],
        cost=cost_of(8),
    )(info, mine, other)
    return [o.reshape(2 * shares * height, w) for o, w in zip(out, widths)]


def whole_kernel(info, mine_ref, other_ref, out_ref):
    def write(ref):
        out_ref[...] = ref[...].astype(F32)

    select_core(info, mine_ref, other_ref, write)


def whole_call(info, mine, other):
    shares, height, width = mine.shape
    out = row_kernel_call(
        whole_kernel,
        "assemble_whole",
        2 * shares,
        share_specs(mine.shape),
        pl.BlockSpec((1, height, width), lambda i, info: (i, 0, 0)),
        shape_of((2 * shares, height, width), F32),
        cost=cost_of(3),
    )(info, mine, other)
    return out.reshape(2 * shares * height, width)


def assemble_kernel(info, mine_ref, other_ref, query_ref, key_ref, value_ref, gain_ref, whole_ref):
    shares, height, _ = mine_ref.shape
    batch = info[BATCH]

    def write(half, ref):
        for j in range(shares):
            at = (half * shares + j) * height
            whole_ref[at : at + height, :] = ref[j ^ batch].astype(F32)

    @pl.when(info[CORE] == 0)
    def _():
        write(0, mine_ref)
        write(1, other_ref)

    @pl.when(info[CORE] == 1)
    def _():
        write(0, other_ref)
        write(1, mine_ref)

    query_ref[...] = whole_ref[:, :Q_WIDTH]
    rest = whole_ref[:, Q_WIDTH:].T
    key_ref[...] = rest[: KV_WIDTH // 2]
    value_ref[...] = rest[KV_WIDTH // 2 : KV_WIDTH]
    gain_ref[0:1, :] = rest[KV_WIDTH : KV_WIDTH + 1]
    gain_ref[1:2, :] = rest[KV_WIDTH + LANES // 2 : KV_WIDTH + LANES // 2 + 1]


def assemble_call(info, mine, other):
    shares, height, total = mine.shape
    width = 2 * shares * height
    shapes = [(width, Q_WIDTH), (KVH * HD, width), (KVH * HD, width), (2, width)]
    return row_kernel_call(
        assemble_kernel,
        "assemble",
        1,
        [whole_spec(mine.shape)] * 2,
        [whole_spec(shape) for shape in shapes],
        [shape_of(shape, F32) for shape in shapes],
        [pltpu.VMEM((width, total), F32)],
        cost=cost_of(5),
    )(info, mine, other)


def describe(lengths, start, place):
    rows = lengths.shape[0]
    index = jnp.arange(rows)
    ahead = (lengths[None, :] > lengths[:, None]) | (
        (lengths[None, :] == lengths[:, None]) & (index[None, :] < index[:, None])
    )
    rank = ahead.sum(axis=1)
    chosen = rank[None, :] == index[:, None]
    ordered = jnp.where(chosen, lengths[None, :], 0).sum(axis=1)
    slots = jnp.where(chosen, index[None, :], 0).sum(axis=1)
    return jnp.concatenate(
        [jnp.stack([start, place // 2, place % 2, lax.axis_index("batch")]), ordered, slots]
    ).astype(jnp.int32)


PLANS = ((4, 4, 4, 4, 3, 3, 2, 1), (4, 4, 4, 4, 4, 3, 3, 1), (4, 4, 4, 4, 4, 4, 4, 1))
CHUNK = 2


def plan_of(chips, quarters):
    reaches = [-(-chips * q // 4) - 1 for q in quarters]
    plan, counts = [], []
    for first in range(0, len(quarters), CHUNK):
        own = reaches[first : first + CHUNK]
        plan.append((first, CHUNK, own[0]))
        counts.append([sum(reach >= d for reach in own) for d in range(own[0] + 1)])
    return plan, counts


def plan_index(ordered, span):
    needed = -(-ordered * 4 // span)
    _, count = place_of("batch", 1)
    for other in [exchange(needed, "batch", k) for k in range(1, count)]:
        needed = jnp.maximum(needed, other)
    index = len(PLANS) - 1
    for i in reversed(range(len(PLANS) - 1)):
        index = jnp.where(jnp.all(needed <= jnp.array(PLANS[i], jnp.int32)), i, index)
    return index


def hops(low, high, way):
    return [(2 * c + k, 2 * (c + way) + k) for c in range(low, high + 1) for k in range(2)]


def layer(quarters, info, x, dy, tables, gain_columns, queries, keys, qkv_weights, mlp_weights):
    rows = x.shape[0]
    seq = lax.axis_size("seq")
    chips = seq // 2
    cos, sin = tables
    gain_column, gain_mlp_column = gain_columns
    plan, counts = plan_of(chips, quarters)

    moving = [keys[first : first + count] for first, count, _ in plan]
    moving = lax.optimization_barrier(moving)
    kv = [[own, exchange(own, "seq", 1)] for own in moving]

    def hop(i, d):
        if d <= plan[i][2]:
            moving[i] = lax.ppermute(
                moving[i][: counts[i][d]], "seq", hops(d - 1, plan[i][2] - 1, 1)
            )
            kv[i].append(moving[i])
            if (i, d) != (1, chips - 1):
                kv[i].append(exchange(moving[i], "seq", 1))

    for d in range(1, chips):
        hop(0, d)
        hop(1, d)
        if d == 1:
            moving[2:] = after(moving[2:], moving[1])
        hop(2, d)
        hop(3, d)
        if d == 2:
            moving[0] = after(moving[0], kv[2][:4], kv[3][:4])

    def forward(i, mixed, *others):
        q = after(queries, *others) if others else queries
        return forward_call(plan[i], rows, info, q, kv[i], mixed)

    lse = [None] * len(plan)
    mixed, lse[3] = forward(3, None)
    mixed, lse[0] = forward(0, mixed)
    moving[1] = after(moving[1], lse[0])
    kv[1][2 * chips - 2 :] = [moving[1], exchange(moving[1], "seq", 1)]
    mixed, lse[2] = forward(2, mixed)
    mixed, lse[1] = forward(1, mixed)

    layer_out, da, dmix, keep, send, grad_gain_mlp = mlp_call(
        info, x, mixed, dy, gain_mlp_column, mlp_weights
    )

    hidden_width = mlp_weights[1].shape[1]
    divided = 3 * hidden_width
    if divided % (chips * LANES):
        divided = 0
    sums = Sum(keep, send, divided)
    swaps, parts, flights, totals, dq = {}, {}, {}, {}, {}

    def backward(i, *others):
        l = after(lse[i], *others)
        dq[i], own, sibling = backward_call(plan[i], info, queries, dmix, mixed, l, cos, sin, kv[i])
        swaps[i] = (own, exchange(sibling, "seq", 1))
        return own

    def joined(i, *others):
        own, received = swaps.pop(i)
        parts[i] = add(after(own, *others), received)
        reach = plan[i][2]
        totals[i] = (reach, parts[i][reach][: counts[i][reach]])
        return parts[i]

    def send_back(i):
        d, total = totals[i]
        if d:
            flights[i] = lax.ppermute(total, "seq", hops(d, plan[i][2], -1))

    def received(i, *others):
        if i in flights:
            d, _ = totals[i]
            local = after(parts[i][d - 1][: counts[i][d - 1]], *others)
            more = counts[i][d - 1] - counts[i][d]
            total = add(local, jnp.pad(flights.pop(i), ((0, more), (0, 0), (0, 0))))
            totals[i] = (d - 1, total)
            return total
        return totals[i][1]

    sums.begin()
    now = backward(0)
    now = sums.end(now)
    sums.begin()
    now = backward(1, now)
    now = joined(0, now)
    send_back(0)
    now = sums.end(now)
    sums.begin()
    now = backward(2, now)
    now = joined(1, now)
    now = received(0, now)
    send_back(0)
    send_back(1)
    now = sums.end(now)
    if divided:
        sums.begin()
    now = backward(3, now)
    now = received(0, now)
    now = received(1, now)
    send_back(0)
    send_back(1)
    now = joined(2, now)
    now = joined(3, now)
    if divided:
        now = sums.end(now)
    sums.begin()
    send_back(2)
    send_back(3)
    while any(d for d, _ in totals.values()):
        for i in range(len(plan)):
            now = received(i, now)
            send_back(i)
    late_dq = jnp.concatenate([dq[i] for i in range(len(plan))], axis=0)
    late_dkv = jnp.concatenate([totals[i][1] for i in range(len(plan))], axis=0)
    now = sums.end(late_dkv)
    sums.begin()
    late_dkv = after(late_dkv, now)
    dx, keep, send = qkv_back_call(
        info, x, da, late_dq, late_dkv, gain_column, qkv_weights, cos, sin, grad_gain_mlp
    )
    late = Sum(keep, send, 0)
    late.begin()
    now = late.end()
    pair = sums.end(now)
    late.begin()
    if divided:
        grads = divided_call(info, *pair, chips, divided, 3)
    else:
        ends = [hidden_width, 2 * hidden_width, 3 * hidden_width]
        grads = jnp.split(whole_call(info, *pair), ends, axis=1)
    late.end(*grads)
    late.begin()
    late.end()
    late.begin()
    late.end()
    late.begin()
    grad_gate, grad_up, grad_down, grad_out = grads
    grad_query, grad_key, grad_value, gains = assemble_call(info, *late.end())

    return (
        layer_out,
        dx,
        gains[0],
        grad_query,
        grad_key.T,
        grad_value.T,
        grad_out,
        gains[1],
        grad_gate,
        grad_up,
        grad_down.T,
    )


def body(
    tokens,
    lengths,
    gain_attn,
    w_query,
    w_key,
    w_value,
    w_out,
    gain_mlp,
    w_gate,
    w_up,
    w_down,
    cotangent,
):
    rows, local_len, _ = tokens.shape
    seq = lax.axis_size("seq")
    place = lax.axis_index("seq")
    start = place * local_len
    tables = rope_tables((start + jnp.arange(local_len, dtype=jnp.int32)).astype(F32))
    info = describe(lengths, start, place)
    qkv_weights = [w_query, w_key.T, w_value.T]
    x = jnp.swapaxes(tokens, 1, 2)
    dy = jnp.swapaxes(cotangent, 1, 2)
    gains = gain_attn[:, None], gain_mlp[:, None]
    index = plan_index(info[LENGTHS : LENGTHS + rows], seq * local_len)
    queries, keys = qkv_call(info, x, gains[0], qkv_weights, *tables)
    layer_out, dx, *grads = lax.switch(
        index,
        [functools.partial(layer, plan) for plan in PLANS],
        info,
        x,
        dy,
        tables,
        gains,
        queries,
        keys,
        qkv_weights,
        [w_out, w_gate, w_up, w_down.T],
    )
    return jnp.swapaxes(layer_out, 1, 2), jnp.swapaxes(dx, 1, 2), *grads


def solution(mesh):
    split, copied = P("batch", "seq", None), P()
    in_specs = (split, P("batch")) + (copied,) * 9 + (split,)
    out_specs = (split, split) + (copied,) * 9
    return jax.shard_map(body, mesh=mesh, in_specs=in_specs, out_specs=out_specs, check_vma=False)
```

```python
import functools

import jax
import jax.numpy as jnp
from jax import lax
from jax.experimental import pallas as pl
from jax.experimental.pallas import tpu as pltpu
from jax.sharding import PartitionSpec as P

H = 9
KVH = 3
HD = 64
GROUP = H // KVH
Q_WIDTH = H * HD
KV_WIDTH = 2 * KVH * HD

EPSILON = 1e-05
ROPE_BASE = 10000.0
MASKED_SCORE = -1e30
BF16 = jnp.bfloat16
F32 = jnp.float32
VMEM_LIMIT = 56 * 1024 * 1024
LANES = 128

START, CHIP, CORE, BATCH, LENGTHS = 0, 1, 2, 3, 4


def dot(a, b, a_dim=1, b_dim=0):
    return lax.dot_general(a, b, (((a_dim,), (b_dim,)), ((), ())), preferred_element_type=F32)


def rope_tables(positions):
    freqs = ROPE_BASE ** (-(jnp.arange(HD // 2, dtype=F32) * 2.0) / HD)
    phases = freqs[:, None] * positions[None, :]
    return jnp.cos(phases), jnp.sin(phases)


def rope(block, cos, sin):
    u1, u2 = block[: HD // 2], block[HD // 2 :]
    return jnp.concatenate([u1 * cos - u2 * sin, u2 * cos + u1 * sin], axis=0)


def rope_back(block, cos, sin):
    u1, u2 = block[: HD // 2], block[HD // 2 :]
    return jnp.concatenate([u1 * cos + u2 * sin, u2 * cos - u1 * sin], axis=0)


def rms_scale(vectors):
    return lax.rsqrt(jnp.mean(vectors * vectors, axis=0, keepdims=True) + EPSILON)


def norm_back(grad_normed, normed, inv_scale):
    return inv_scale * (
        grad_normed - normed * jnp.mean(grad_normed * normed, axis=0, keepdims=True)
    )


def clear(ref):
    ref[...] = jnp.zeros_like(ref)


def row_spec(shape, first=0):
    return pl.BlockSpec((1,) + shape, lambda r, info: (first + r, 0, 0))


def kv_spec(array):
    return pl.BlockSpec(
        (1,) + array.shape[1:], lambda r, info: (jnp.minimum(r, array.shape[0] - 1), 0, 0)
    )


def slot_spec(shape, rows, first=0):
    return pl.BlockSpec((1,) + shape, lambda r, info: (info[LENGTHS + rows + first + r], 0, 0))


def whole_spec(shape):
    return pl.BlockSpec(
        shape, lambda r, info: (0,) * len(shape), pipeline_mode=pl.Buffered(buffer_count=1)
    )


def shape_of(shape, dtype=BF16):
    return jax.ShapeDtypeStruct(shape, dtype)


def cost_of(microseconds):
    return pl.CostEstimate(
        flops=int(microseconds * 8e8), bytes_accessed=int(microseconds * 1e6), transcendentals=0
    )


def row_kernel_call(
    kernel, name, rows, in_specs, out_specs, out_shape, scratch=(), cost=None, aliases=None
):
    return pl.pallas_call(
        kernel,
        grid_spec=pltpu.PrefetchScalarGridSpec(
            num_scalar_prefetch=1,
            grid=(rows,),
            in_specs=in_specs,
            out_specs=out_specs,
            scratch_shapes=scratch,
        ),
        out_shape=out_shape,
        compiler_params=pltpu.CompilerParams(vmem_limit_bytes=VMEM_LIMIT),
        cost_estimate=cost,
        input_output_aliases=aliases or {},
        name=name,
    )


def row_used(info, first=0):
    length = info[LENGTHS + first + pl.program_id(0)]
    return length, info[START] < length


def qkv_kernel(first, info, x_ref, gain_ref, w_query_ref, w_key_t_ref, w_value_t_ref, cos_ref, sin_ref, q_ref, kv_ref):
    _, used = row_used(info, first)

    @pl.when(used)
    def _():
        x = x_ref[0].astype(F32)
        normed = (x * rms_scale(x) * gain_ref[...]).astype(BF16)
        out = dot(w_query_ref[...], normed, 0, 0)
        cos, sin = cos_ref[...], sin_ref[...]
        for h in range(H):
            rotated = rope(out[h * HD : (h + 1) * HD], cos, sin)
            q_ref[0, h * HD : (h + 1) * HD, :] = (rotated * HD**-0.5).astype(BF16)
        out_key, out_value = dot(w_key_t_ref[...], normed), dot(w_value_t_ref[...], normed)
        for k in range(KVH):
            head, at = slice(k * HD, (k + 1) * HD), 2 * HD * k
            kv_ref[0, at : at + HD, :] = rope(out_key[head], cos, sin).astype(BF16)
            kv_ref[0, at + HD : at + 2 * HD, :] = out_value[head].astype(BF16)

    @pl.when(jnp.logical_not(used))
    def _():
        clear(q_ref)
        clear(kv_ref)


def qkv_call(info, tokens, gain, weights, cos, sin, first=0, count=None):
    rows, width, length = tokens.shape
    count = count or rows
    return row_kernel_call(
        functools.partial(qkv_kernel, first),
        "qkv",
        count,
        [
            slot_spec((width, length), rows, first),
            whole_spec(gain.shape),
        ]
        + [whole_spec(a.shape) for a in (*weights, cos, sin)],
        [row_spec((Q_WIDTH, length)), row_spec((KV_WIDTH, length))],
        [shape_of((count, Q_WIDTH, length)), shape_of((count, KV_WIDTH, length))],
        cost=cost_of(1.2 * count),
    )(info, tokens, gain, *weights, cos, sin)


def heads_of(ref, k):
    return jnp.concatenate(
        [ref[0, (k * GROUP + g) * HD : (k * GROUP + g + 1) * HD, :] for g in range(GROUP)], axis=1
    )


def key_value(kv_refs, block, k):
    ref, at = kv_refs[block], 2 * HD * k
    return ref[0, at : at + HD, :], ref[0, at + HD : at + 2 * HD, :]


def stack_spec(reach, length):
    return pl.BlockSpec((reach + 1, 1, KV_WIDTH, length), lambda r, info: (0, r, 0, 0))


def mask_diagonal(scores, start, length):
    size = scores.shape[0]
    key = lax.broadcasted_iota(jnp.int32, scores.shape, 0)
    query = lax.broadcasted_iota(jnp.int32, scores.shape, 1) % size
    allowed = jnp.logical_and(key <= query, start + key < length)
    return jnp.where(allowed, scores, MASKED_SCORE)


def visit_blocks(info, chips, visit):
    chip, core = info[CHIP], info[CORE]

    @pl.when(core == 0)
    def _():
        visit([(0, True)], True)

    @pl.when(core == 1)
    def _():
        visit([(0, True), (1, False)], True)

    for d in range(1, chips, 2):
        near = [(2 * d, False), (2 * d + 1, False)]

        if d + 1 < chips:

            @pl.when(chip > d)
            def _():
                visit(near + [(2 * d + 2, False), (2 * d + 3, False)], False)

        @pl.when((chip == d) if d + 1 < chips else (chip >= d))
        def _():
            visit(near, False)


def forward_kernel(chunk, info, q_ref, *refs):
    first_row, _, reach = chunk
    kv_refs = refs[: 2 * reach + 2]
    mixed_ref, lse_ref, peak_ref, total_ref, acc_ref = refs[-5:]
    length, used = row_used(info, first_row)
    start = info[START]

    def visit(blocks, first):
        def scores_of(k):
            queries = heads_of(q_ref, k)
            scores = []
            for b, diagonal in blocks:
                s = dot(key_value(kv_refs, b, k)[0], queries, 0, 0)
                scores.append(mask_diagonal(s, start, length) if diagonal else s)
            return scores

        ahead = [scores_of(k) for k in range(1)]
        for k in range(KVH):
            scores = ahead.pop(0)
            if k + 1 < KVH:
                ahead.append(scores_of(k + 1))
            peak = scores[0].max(axis=0, keepdims=True)
            for s in scores[1:]:
                peak = jnp.maximum(peak, s.max(axis=0, keepdims=True))
            if not first:
                old = peak_ref[k]
                peak = jnp.maximum(peak, old)
                shrink = jnp.exp(old - peak)
            total, acc = 0.0, 0.0
            for (b, _), s in zip(blocks, scores):
                weights = jnp.exp(s - peak)
                total = total + weights.sum(axis=0, keepdims=True)
                acc = acc + dot(key_value(kv_refs, b, k)[1], weights.astype(BF16))
            if not first:
                total = total + total_ref[k] * shrink
                acc = acc + acc_ref[k] * shrink
            peak_ref[k], total_ref[k], acc_ref[k] = peak, total, acc

    @pl.when(used)
    def _():
        visit_blocks(info, reach + 1, visit)
        size = q_ref.shape[2]
        for k in range(KVH):
            total = total_ref[k]
            out = (acc_ref[k] / total).astype(BF16)
            lse = peak_ref[k] + jnp.log(total)
            for g in range(GROUP):
                h = k * GROUP + g
                lse_ref[0, h : h + 1, :] = lse[:, g * size : (g + 1) * size]
                mixed_ref[0, h * HD : (h + 1) * HD, :] = out[:, g * size : (g + 1) * size]

    @pl.when(jnp.logical_not(used))
    def _():
        clear(mixed_ref)
        clear(lse_ref)


def forward_call(chunk, rows, info, queries, kv, mixed):
    first, count, reach = chunk
    length = queries.shape[2]
    earlier = [] if mixed is None else [mixed]
    return row_kernel_call(
        functools.partial(forward_kernel, chunk),
        "attention_forward",
        count,
        [row_spec((Q_WIDTH, length), first)]
        + [kv_spec(a) for a in kv]
        + [pl.BlockSpec(memory_space=pl.ANY)] * len(earlier),
        [row_spec((Q_WIDTH, length), first), row_spec((H, length))],
        [shape_of((rows, Q_WIDTH, length)), shape_of((count, H, length), F32)],
        [
            pltpu.VMEM((KVH, 1, GROUP * length), F32),
            pltpu.VMEM((KVH, 1, GROUP * length), F32),
            pltpu.VMEM((KVH, HD, GROUP * length), F32),
        ],
        aliases={2 + len(kv): 0} if earlier else None,
        cost=cost_of(2.5 * count),
    )(info, queries, *kv, *earlier)


def backward_kernel(chunk, info, q_ref, dmix_ref, mixed_ref, lse_ref, cos_ref, sin_ref, *refs):
    first_row, _, reach = chunk
    kv_refs = refs[: 2 * reach + 2]
    dq_ref, *dkv_refs = refs[-5:-2]
    inner_ref, dq_acc_ref = refs[-2:]
    length, used = row_used(info, first_row)
    start, chip, core = info[START], info[CHIP], info[CORE]
    size = q_ref.shape[2]

    def visit(blocks, first):
        def products(k, b, diagonal):
            keys, values = key_value(kv_refs, b, k)
            s = dot(keys, heads_of(q_ref, k), 0, 0)
            if diagonal:
                s = mask_diagonal(s, start, length)
            return s, dot(values, heads_of(dmix_ref, k), 0, 0)

        work = [(k, b, diagonal) for k in range(KVH) for b, diagonal in blocks]
        ahead = products(*work[0])
        for n, (k, b, _) in enumerate(work):
            (s, dprobs), ahead = ahead, products(*work[n + 1]) if n + 1 < len(work) else None
            queries, dmix = heads_of(q_ref, k), heads_of(dmix_ref, k)
            lse = jnp.concatenate(
                [lse_ref[0, k * GROUP + g : k * GROUP + g + 1, :] for g in range(GROUP)], axis=1
            )
            probs = jnp.exp(s - lse)
            dscores = (probs * (dprobs - inner_ref[k])).astype(BF16)
            dq = dot(key_value(kv_refs, b, k)[0], dscores)
            if first and b == blocks[0][0]:
                dq_acc_ref[k] = dq
            else:
                dq_acc_ref[k] += dq
            at, out = 2 * HD * k, dkv_refs[b % 2]
            out[b // 2, 0, at : at + HD, :] = dot(queries, dscores, 1, 1).astype(BF16)
            out[b // 2, 0, at + HD : at + 2 * HD, :] = dot(dmix, probs.astype(BF16), 1, 1).astype(
                BF16
            )

    @pl.when(used)
    def _():
        for k in range(KVH):
            parts = []
            for g in range(GROUP):
                at = slice((k * GROUP + g) * HD, (k * GROUP + g + 1) * HD)
                product = dmix_ref[0, at, :].astype(F32) * mixed_ref[0, at, :].astype(F32)
                parts.append(product.sum(axis=0, keepdims=True))
            inner_ref[k] = jnp.concatenate(parts, axis=1)
        visit_blocks(info, reach + 1, visit)
        cos, sin = cos_ref[...], sin_ref[...]
        for k in range(KVH):
            dq = dq_acc_ref[k] * HD**-0.5
            for g in range(GROUP):
                h = k * GROUP + g
                dq_ref[0, h * HD : (h + 1) * HD, :] = rope_back(
                    dq[:, g * size : (g + 1) * size], cos, sin
                ).astype(BF16)

    unused = jnp.logical_not(used)

    def clear_block(b):
        dkv_refs[b % 2][b // 2] = jnp.zeros(dkv_refs[b % 2].shape[1:], BF16)

    @pl.when(unused)
    def _():
        clear(dq_ref)
        clear_block(0)

    @pl.when(jnp.logical_or(unused, core == 0))
    def _():
        clear_block(1)

    for d in range(1, reach + 1):

        @pl.when(jnp.logical_or(unused, chip < d))
        def _():
            clear_block(2 * d)
            clear_block(2 * d + 1)


def backward_call(chunk, info, queries, dmix, mixed, lse, cos, sin, kv):
    first, count, reach = chunk
    length = dmix.shape[2]
    return row_kernel_call(
        functools.partial(backward_kernel, chunk),
        "attention_backward",
        count,
        [
            row_spec((Q_WIDTH, length), first),
            row_spec((Q_WIDTH, length), first),
            row_spec((Q_WIDTH, length), first),
            row_spec((H, length)),
            whole_spec(cos.shape),
            whole_spec(sin.shape),
        ]
        + [kv_spec(a) for a in kv],
        [row_spec((Q_WIDTH, length))] + [stack_spec(reach, length)] * 2,
        [shape_of((count, Q_WIDTH, length))]
        + [shape_of((reach + 1, count, KV_WIDTH, length))] * 2,
        [
            pltpu.VMEM((KVH, 1, GROUP * length), F32),
            pltpu.VMEM((KVH, HD, GROUP * length), F32),
        ],
        cost=cost_of(4 * count),
    )(info, queries, dmix, mixed, lse, cos, sin, *kv)


def write_halves(info, acc_refs, keep_ref, send_ref):
    at = 0
    for acc_ref in acc_refs:
        half, width = acc_ref.shape[0] // 2, acc_ref.shape[1]
        mine = pl.multiple_of(info[CORE] * half, 8)
        other = pl.multiple_of((1 - info[CORE]) * half, 8)
        keep_ref[:, at : at + width] = acc_ref[pl.ds(mine, half), :].astype(BF16)
        send_ref[:, at : at + width] = acc_ref[pl.ds(other, half), :].astype(BF16)
        at += width


def mlp_kernel(
    info,
    x_ref,
    mixed_ref,
    dy_ref,
    gain_ref,
    w_out_ref,
    w_gate_ref,
    w_up_ref,
    w_down_t_ref,
    out_ref,
    da_ref,
    dmix_ref,
    keep_ref,
    send_ref,
    grad_gain_ref,
    acc_ref,
    acc_out_ref,
    acc_gain_ref,
):
    length, used = row_used(info)
    row = pl.program_id(0)
    width, size = x_ref.shape[1:]
    hidden_width = w_gate_ref.shape[1]
    step = hidden_width // 2 if hidden_width % (2 * LANES) == 0 else hidden_width

    @pl.when(row == 0)
    def _():
        clear(acc_ref)
        clear(acc_out_ref)
        clear(acc_gain_ref)

    @pl.when(used)
    def _():
        mixed = mixed_ref[0]
        resid = x_ref[0].astype(F32) + dot(w_out_ref[...], mixed, 0, 0)
        scale = rms_scale(resid)
        normed = resid * scale
        mlp_in = (normed * gain_ref[...]).astype(BF16)
        position = info[START] + lax.broadcasted_iota(jnp.int32, (1, size), 1)
        valid = (position < length).astype(F32)
        dy_wide = dy_ref[0].astype(F32) * valid
        dy = dy_wide.astype(BF16)
        def products(at):
            part = slice(at, at + step)
            return (
                dot(w_gate_ref[:, part], mlp_in, 0, 0),
                dot(w_up_ref[:, part], mlp_in, 0, 0),
                dot(w_down_t_ref[:, part], dy, 0, 0),
            )

        out, grad_in = resid, None
        ahead = products(0)
        for at in range(0, hidden_width, step):
            part = slice(at, at + step)
            (gate, up, dhidden), ahead = ahead, None
            if at + step < hidden_width:
                ahead = products(at + step)
            sigmoid = 0.5 + 0.5 * jnp.tanh(0.5 * gate)
            activated = gate * sigmoid
            hidden = (activated * up).astype(BF16)
            dgate = (dhidden * up * (sigmoid + activated * (1.0 - sigmoid))).astype(BF16)
            dup = (dhidden * activated).astype(BF16)
            out = out + dot(w_down_t_ref[:, part], hidden)
            piece = dot(w_gate_ref[:, part], dgate) + dot(w_up_ref[:, part], dup)
            grad_in = piece if grad_in is None else grad_in + piece
            acc_ref[:, at : at + step] += dot(mlp_in, dgate, 1, 1)
            acc_ref[:, hidden_width + at : hidden_width + at + step] += dot(mlp_in, dup, 1, 1)
            acc_ref[:, 2 * hidden_width + at : 2 * hidden_width + at + step] += dot(
                dy, hidden, 1, 1
            )
        out_ref[0] = (out * valid).astype(BF16)
        acc_gain_ref[...] += grad_in * normed
        dresid = dy_wide + norm_back(grad_in * gain_ref[...], normed, scale)
        da = dresid.astype(BF16)
        da_ref[0] = da
        dmix_ref[0] = dot(w_out_ref[...], da).astype(BF16)
        acc_out_ref[...] += dot(mixed, da, 1, 1)

    @pl.when(jnp.logical_not(used))
    def _():
        clear(out_ref)
        clear(da_ref)
        clear(dmix_ref)

    @pl.when(row == pl.num_programs(0) - 1)
    def _():
        write_halves(info, [acc_ref, acc_out_ref], keep_ref, send_ref)
        grad_gain_ref[...] = jnp.broadcast_to(
            acc_gain_ref[...].sum(axis=1, keepdims=True), grad_gain_ref.shape
        )


def mlp_call(info, tokens, mixed, cotangent, gain, weights):
    rows, width, length = tokens.shape
    total = 3 * weights[1].shape[1]
    return row_kernel_call(
        mlp_kernel,
        "feed_forward",
        rows,
        [
            slot_spec((width, length), rows),
            row_spec((Q_WIDTH, length)),
            slot_spec((width, length), rows),
            whole_spec(gain.shape),
        ]
        + [whole_spec(w.shape) for w in weights],
        [
            slot_spec((width, length), rows),
            row_spec((width, length)),
            row_spec((Q_WIDTH, length)),
            whole_spec((width // 2, total + width)),
            whole_spec((width // 2, total + width)),
            whole_spec((width, LANES)),
        ],
        [
            shape_of((rows, width, length)),
            shape_of((rows, width, length)),
            shape_of((rows, Q_WIDTH, length)),
            shape_of((width // 2, total + width)),
            shape_of((width // 2, total + width)),
            shape_of((width, LANES), F32),
        ],
        [
            pltpu.VMEM((width, total), F32),
            pltpu.VMEM((Q_WIDTH, width), F32),
            pltpu.VMEM((width, length), F32),
        ],
        cost=cost_of(60),
    )(info, tokens, mixed, cotangent, gain, *weights)


def qkv_back_kernel(
    info,
    x_ref,
    da_ref,
    dq_ref,
    dkv_ref,
    gain_ref,
    w_query_ref,
    w_key_t_ref,
    w_value_t_ref,
    cos_ref,
    sin_ref,
    grad_gain_mlp_ref,
    dx_ref,
    keep_ref,
    send_ref,
    acc_ref,
    acc_gain_ref,
):
    _, used = row_used(info)
    row = pl.program_id(0)
    width = x_ref.shape[1]
    inner = Q_WIDTH + KV_WIDTH

    @pl.when(row == 0)
    def _():
        clear(acc_ref)
        clear(acc_gain_ref)

    @pl.when(used)
    def _():
        x = x_ref[0].astype(F32)
        scale = rms_scale(x)
        normed = x * scale
        attn_in = (normed * gain_ref[...]).astype(BF16)
        cos, sin = cos_ref[...], sin_ref[...]
        dq, dk, dv = dq_ref[0], [], []
        for k in range(KVH):
            at = 2 * HD * k
            dk.append(rope_back(dkv_ref[0, at : at + HD, :].astype(F32), cos, sin).astype(BF16))
            dv.append(dkv_ref[0, at + HD : at + 2 * HD, :])
        dk, dv = jnp.concatenate(dk, axis=0), jnp.concatenate(dv, axis=0)
        dn = dot(w_query_ref[...], dq)
        dn += dot(w_key_t_ref[...], dk, 0, 0) + dot(w_value_t_ref[...], dv, 0, 0)
        acc_ref[:, :Q_WIDTH] += dot(attn_in, dq, 1, 1)
        acc_ref[:, Q_WIDTH:inner] += dot(attn_in, jnp.concatenate([dk, dv], axis=0), 1, 1)
        acc_gain_ref[...] += dn * normed
        dx_ref[0] = (
            da_ref[0].astype(F32) + norm_back(dn * gain_ref[...], normed, scale)
        ).astype(BF16)

    @pl.when(jnp.logical_not(used))
    def _():
        clear(dx_ref)

    @pl.when(row == pl.num_programs(0) - 1)
    def _():
        lane = lax.broadcasted_iota(jnp.int32, (width, LANES), 1)
        acc_ref[:, inner:] = jnp.where(
            lane < LANES // 2,
            acc_gain_ref[...].sum(axis=1, keepdims=True),
            grad_gain_mlp_ref[...],
        )
        write_halves(info, [acc_ref], keep_ref, send_ref)


def qkv_back_call(info, tokens, da, dq, dkv, gain, weights, cos, sin, grad_gain_mlp):
    rows, width, length = tokens.shape
    total = Q_WIDTH + KV_WIDTH + LANES
    return row_kernel_call(
        qkv_back_kernel,
        "qkv_backward",
        rows,
        [
            slot_spec((width, length), rows),
            row_spec((width, length)),
            row_spec((Q_WIDTH, length)),
            row_spec((KV_WIDTH, length)),
        ]
        + [whole_spec(a.shape) for a in (gain, *weights, cos, sin, grad_gain_mlp)],
        [
            slot_spec((width, length), rows),
            whole_spec((width // 2, total)),
            whole_spec((width // 2, total)),
        ],
        [
            shape_of((rows, width, length)),
            shape_of((width // 2, total)),
            shape_of((width // 2, total)),
        ],
        [pltpu.VMEM((width, total), F32), pltpu.VMEM((width, length), F32)],
        cost=cost_of(14),
    )(info, tokens, da, dq, dkv, gain, *weights, cos, sin, grad_gain_mlp)


def exchange(array, axis, bits, low=1):
    size = lax.axis_size(axis)
    return lax.ppermute(array, axis, [(i, i ^ (bits * low)) for i in range(size)])


def add(*arrays):
    total = arrays[0].astype(F32)
    for array in arrays[1:]:
        total = total + array.astype(F32)
    return total.astype(BF16)


def place_of(axis, low):
    return lax.axis_index(axis) // low, lax.axis_size(axis) // low


def after(value, *others):
    return lax.optimization_barrier((value, others))[0]


class Sum:
    def __init__(self, keep, send, divided):
        self.keep, self.send, self.divided = keep, send, divided
        self.share = divided // (lax.axis_size("seq") // 2)
        self.steps = iter(
            [self.halve, self.over_batch, self.over_chips]
            + ([self.back_chips] if divided else [])
            + [self.back_batch, self.back_halves]
        )

    def begin(self):
        next(self.steps)()

    def end(self, *others):
        self.local = after(self.local, *others)
        self.array = self.finish(self.local, self.received)
        return self.array

    def arrived(self, number, *others):
        return after(self.received[number], *others)

    def added(self, local, received):
        return add(local, *received)

    def halve(self):
        self.local, self.received = self.keep, [exchange(self.send, "seq", 1)]
        self.finish = self.added

    def over_batch(self):
        me, count = place_of("batch", 1)
        share = self.array.shape[0] // count

        def part(index):
            return lax.dynamic_slice_in_dim(self.array, index * share, share, 0)

        self.received = [exchange(part(me ^ k), "batch", k) for k in range(1, count)]
        self.local, self.finish = part(me), self.added

    def over_chips(self):
        me, count = place_of("seq", 2)

        def part(index):
            if not self.divided:
                return self.array
            left = lax.dynamic_slice_in_dim(self.array, index * self.share, self.share, 1)
            return jnp.concatenate([left, self.array[:, self.divided :]], axis=1)

        self.received = [exchange(part(me ^ k), "seq", k, 2) for k in range(1, count)]
        self.local, self.finish = part(me), self.added

    def back_chips(self):
        _, count = place_of("seq", 2)
        left, right = self.array[:, : self.share], self.array[:, self.share :]
        self.received = [exchange(left, "seq", k, 2) for k in range(1, count)]
        self.local = left
        self.finish = lambda local, received: jnp.concatenate([local, *received, right], axis=1)

    def back_batch(self):
        _, count = place_of("batch", 1)
        self.received = [exchange(self.array, "batch", k) for k in range(1, count)]
        self.local = self.array
        self.finish = lambda local, received: jnp.stack([local, *received])

    def back_halves(self):
        self.local, self.received = self.array, exchange(self.array, "seq", 1)
        self.finish = lambda local, received: (local, received)


def select_core(info, mine_ref, other_ref, write):
    shares = pl.num_programs(0) // 2
    upper = (pl.program_id(0) >= shares).astype(jnp.int32)

    @pl.when(upper == info[CORE])
    def _():
        write(mine_ref)

    @pl.when(upper != info[CORE])
    def _():
        write(other_ref)


def share_specs(shape):
    shares = shape[0]
    rest = (0,) * (len(shape) - 1)

    def index(core, i, info):
        step = i - core * shares
        return (jnp.clip(step, 0, shares - 1) ^ info[BATCH],) + rest

    block = (1,) + tuple(shape[1:])
    return [
        pl.BlockSpec(block, lambda i, info: index(info[CORE], i, info)),
        pl.BlockSpec(block, lambda i, info: index(1 - info[CORE], i, info)),
    ]


def divided_kernel(chips, info, mine_ref, other_ref, *out_refs):
    out_width, rest = out_refs[0].shape[2], out_refs[-1].shape[2]
    width = (mine_ref.shape[2] - rest) // chips

    def write(ref):
        for q in range(chips):
            begin = pl.multiple_of((info[CHIP] ^ q) * width, LANES)
            share = ref[0, :, pl.ds(begin, width)].astype(F32)
            at = q * width
            while at < (q + 1) * width:
                out, column = divmod(at, out_width)
                size = min((q + 1) * width - at, out_width - column)
                begin = at - q * width
                out_refs[out][0, :, column : column + size] = share[:, begin : begin + size]
                at += size
        out_refs[-1][0] = ref[0, :, chips * width :].astype(F32)

    select_core(info, mine_ref, other_ref, write)


def divided_call(info, mine, other, chips, divided, count):
    shares, height, total = mine.shape
    widths = [divided // count] * count + [total - divided]
    out = row_kernel_call(
        functools.partial(divided_kernel, chips),
        "assemble_divided",
        2 * shares,
        share_specs(mine.shape),
        [pl.BlockSpec((1, height, w), lambda i, info: (i, 0, 0)) for w in widths],
        [shape_of((2 * shares, height, w), F32) for w in widths],
        cost=cost_of(8),
    )(info, mine, other)
    return [o.reshape(2 * shares * height, w) for o, w in zip(out, widths)]


def whole_kernel(info, mine_ref, other_ref, out_ref):
    def write(ref):
        out_ref[...] = ref[...].astype(F32)

    select_core(info, mine_ref, other_ref, write)


def whole_call(info, mine, other):
    shares, height, width = mine.shape
    out = row_kernel_call(
        whole_kernel,
        "assemble_whole",
        2 * shares,
        share_specs(mine.shape),
        pl.BlockSpec((1, height, width), lambda i, info: (i, 0, 0)),
        shape_of((2 * shares, height, width), F32),
        cost=cost_of(3),
    )(info, mine, other)
    return out.reshape(2 * shares * height, width)


def assemble_kernel(info, mine_ref, other_ref, query_ref, key_ref, value_ref, gain_ref, whole_ref):
    shares, height, _ = mine_ref.shape
    batch = info[BATCH]

    def write(half, ref):
        for j in range(shares):
            at = (half * shares + j) * height
            whole_ref[at : at + height, :] = ref[j ^ batch].astype(F32)

    @pl.when(info[CORE] == 0)
    def _():
        write(0, mine_ref)
        write(1, other_ref)

    @pl.when(info[CORE] == 1)
    def _():
        write(0, other_ref)
        write(1, mine_ref)

    query_ref[...] = whole_ref[:, :Q_WIDTH]
    rest = whole_ref[:, Q_WIDTH:].T
    key_ref[...] = rest[: KV_WIDTH // 2]
    value_ref[...] = rest[KV_WIDTH // 2 : KV_WIDTH]
    gain_ref[0:1, :] = rest[KV_WIDTH : KV_WIDTH + 1]
    gain_ref[1:2, :] = rest[KV_WIDTH + LANES // 2 : KV_WIDTH + LANES // 2 + 1]


def assemble_call(info, mine, other):
    shares, height, total = mine.shape
    width = 2 * shares * height
    shapes = [(width, Q_WIDTH), (KVH * HD, width), (KVH * HD, width), (2, width)]
    return row_kernel_call(
        assemble_kernel,
        "assemble",
        1,
        [whole_spec(mine.shape)] * 2,
        [whole_spec(shape) for shape in shapes],
        [shape_of(shape, F32) for shape in shapes],
        [pltpu.VMEM((width, total), F32)],
        cost=cost_of(5),
    )(info, mine, other)


def describe(lengths, start, place):
    rows = lengths.shape[0]
    index = jnp.arange(rows)
    ahead = (lengths[None, :] > lengths[:, None]) | (
        (lengths[None, :] == lengths[:, None]) & (index[None, :] < index[:, None])
    )
    rank = ahead.sum(axis=1)
    chosen = rank[None, :] == index[:, None]
    ordered = jnp.where(chosen, lengths[None, :], 0).sum(axis=1)
    slots = jnp.where(chosen, index[None, :], 0).sum(axis=1)
    return jnp.concatenate(
        [jnp.stack([start, place // 2, place % 2, lax.axis_index("batch")]), ordered, slots]
    ).astype(jnp.int32)


PLANS = ((4, 4, 4, 4, 3, 3, 2, 1), (4, 4, 4, 4, 4, 3, 3, 1), (4, 4, 4, 4, 4, 4, 4, 1))
CHUNK = 2


def plan_of(chips, quarters):
    reaches = [-(-chips * q // 4) - 1 for q in quarters]
    plan, counts = [], []
    for first in range(0, len(quarters), CHUNK):
        own = reaches[first : first + CHUNK]
        plan.append((first, CHUNK, own[0]))
        counts.append([sum(reach >= d for reach in own) for d in range(own[0] + 1)])
    return plan, counts


def plan_index(ordered, span):
    needed = -(-ordered * 4 // span)
    _, count = place_of("batch", 1)
    for other in [exchange(needed, "batch", k) for k in range(1, count)]:
        needed = jnp.maximum(needed, other)
    index = len(PLANS) - 1
    for i in reversed(range(len(PLANS) - 1)):
        index = jnp.where(jnp.all(needed <= jnp.array(PLANS[i], jnp.int32)), i, index)
    return index


def hops(low, high, way):
    return [(2 * c + k, 2 * (c + way) + k) for c in range(low, high + 1) for k in range(2)]


def layer(quarters, info, x, dy, tables, gain_columns, queries, keys, qkv_weights, mlp_weights):
    rows = x.shape[0]
    seq = lax.axis_size("seq")
    chips = seq // 2
    cos, sin = tables
    gain_column, gain_mlp_column = gain_columns
    plan, counts = plan_of(chips, quarters)

    moving = [keys[first : first + count] for first, count, _ in plan]
    moving = lax.optimization_barrier(moving)
    kv = [[own, exchange(own, "seq", 1)] for own in moving]

    def hop(i, d):
        if d <= plan[i][2]:
            moving[i] = lax.ppermute(
                moving[i][: counts[i][d]], "seq", hops(d - 1, plan[i][2] - 1, 1)
            )
            kv[i].append(moving[i])
            if (i, d) != (1, chips - 1):
                kv[i].append(exchange(moving[i], "seq", 1))

    for d in range(1, chips):
        hop(0, d)
        hop(1, d)
        if d == 1:
            moving[2:] = after(moving[2:], moving[1])
        hop(2, d)
        hop(3, d)
        if d == 2:
            moving[0] = after(moving[0], kv[2][:4], kv[3][:4])

    def forward(i, mixed, *others):
        q = after(queries, *others) if others else queries
        return forward_call(plan[i], rows, info, q, kv[i], mixed)

    lse = [None] * len(plan)
    mixed, lse[3] = forward(3, None)
    mixed, lse[0] = forward(0, mixed)
    moving[1] = after(moving[1], lse[0])
    kv[1][2 * chips - 2 :] = [moving[1], exchange(moving[1], "seq", 1)]
    mixed, lse[2] = forward(2, mixed)
    mixed, lse[1] = forward(1, mixed)

    layer_out, da, dmix, keep, send, grad_gain_mlp = mlp_call(
        info, x, mixed, dy, gain_mlp_column, mlp_weights
    )

    hidden_width = mlp_weights[1].shape[1]
    divided = 3 * hidden_width
    if divided % (chips * LANES):
        divided = 0
    sums = Sum(keep, send, divided)
    swaps, parts, flights, totals, dq = {}, {}, {}, {}, {}

    def backward(i, *others):
        l = after(lse[i], *others)
        dq[i], own, sibling = backward_call(plan[i], info, queries, dmix, mixed, l, cos, sin, kv[i])
        swaps[i] = (own, exchange(sibling, "seq", 1))
        return own

    def joined(i, *others):
        own, received = swaps.pop(i)
        parts[i] = add(after(own, *others), received)
        reach = plan[i][2]
        totals[i] = (reach, parts[i][reach][: counts[i][reach]])
        return parts[i]

    def send_back(i):
        d, total = totals[i]
        if d:
            flights[i] = lax.ppermute(total, "seq", hops(d, plan[i][2], -1))

    def received(i, *others):
        if i in flights:
            d, _ = totals[i]
            local = after(parts[i][d - 1][: counts[i][d - 1]], *others)
            more = counts[i][d - 1] - counts[i][d]
            total = add(local, jnp.pad(flights.pop(i), ((0, more), (0, 0), (0, 0))))
            totals[i] = (d - 1, total)
            return total
        return totals[i][1]

    sums.begin()
    now = backward(0)
    now = sums.end(now)
    sums.begin()
    now = backward(1, now)
    now = joined(0, now)
    send_back(0)
    now = sums.end(now)
    sums.begin()
    now = backward(2, now)
    now = joined(1, now)
    now = received(0, now)
    send_back(0)
    send_back(1)
    now = sums.end(now)
    if divided:
        sums.begin()
    now = backward(3, now)
    now = received(0, now)
    now = received(1, now)
    send_back(0)
    send_back(1)
    now = joined(2, now)
    now = joined(3, now)
    if divided:
        now = sums.end(now)
    sums.begin()
    send_back(2)
    send_back(3)
    while any(d for d, _ in totals.values()):
        for i in range(len(plan)):
            now = received(i, now)
            send_back(i)
    late_dq = jnp.concatenate([dq[i] for i in range(len(plan))], axis=0)
    late_dkv = jnp.concatenate([totals[i][1] for i in range(len(plan))], axis=0)
    now = sums.end(late_dkv)
    sums.begin()
    late_dkv = after(late_dkv, now)
    dx, keep, send = qkv_back_call(
        info, x, da, late_dq, late_dkv, gain_column, qkv_weights, cos, sin, grad_gain_mlp
    )
    late = Sum(keep, send, 0)
    late.begin()
    now = late.end()
    pair = sums.end(now)
    late.begin()
    now = late.end(now)
    late.begin()
    pair = after(pair, now)
    if divided:
        grads = divided_call(info, *pair, chips, divided, 3)
    else:
        ends = [hidden_width, 2 * hidden_width, 3 * hidden_width]
        grads = jnp.split(whole_call(info, *pair), ends, axis=1)
    late.end(*grads)
    late.begin()
    late.end()
    late.begin()
    grad_gate, grad_up, grad_down, grad_out = grads
    grad_query, grad_key, grad_value, gains = assemble_call(info, *late.end())

    return (
        layer_out,
        dx,
        gains[0],
        grad_query,
        grad_key.T,
        grad_value.T,
        grad_out,
        gains[1],
        grad_gate,
        grad_up,
        grad_down.T,
    )


def body(
    tokens,
    lengths,
    gain_attn,
    w_query,
    w_key,
    w_value,
    w_out,
    gain_mlp,
    w_gate,
    w_up,
    w_down,
    cotangent,
):
    rows, local_len, _ = tokens.shape
    seq = lax.axis_size("seq")
    place = lax.axis_index("seq")
    start = place * local_len
    tables = rope_tables((start + jnp.arange(local_len, dtype=jnp.int32)).astype(F32))
    info = describe(lengths, start, place)
    qkv_weights = [w_query, w_key.T, w_value.T]
    x = jnp.swapaxes(tokens, 1, 2)
    dy = jnp.swapaxes(cotangent, 1, 2)
    gains = gain_attn[:, None], gain_mlp[:, None]
    index = plan_index(info[LENGTHS : LENGTHS + rows], seq * local_len)
    queries, keys = qkv_call(info, x, gains[0], qkv_weights, *tables)
    layer_out, dx, *grads = lax.switch(
        index,
        [functools.partial(layer, plan) for plan in PLANS],
        info,
        x,
        dy,
        tables,
        gains,
        queries,
        keys,
        qkv_weights,
        [w_out, w_gate, w_up, w_down.T],
    )
    return jnp.swapaxes(layer_out, 1, 2), jnp.swapaxes(dx, 1, 2), *grads


def solution(mesh):
    split, copied = P("batch", "seq", None), P()
    in_specs = (split, P("batch")) + (copied,) * 9 + (split,)
    out_specs = (split, split) + (copied,) * 9
    return jax.shard_map(body, mesh=mesh, in_specs=in_specs, out_specs=out_specs, check_vma=False)
```

```python
import functools

import jax
import jax.numpy as jnp
from jax import lax
from jax.experimental import pallas as pl
from jax.experimental.pallas import tpu as pltpu
from jax.sharding import PartitionSpec as P

H = 9
KVH = 3
HD = 64
GROUP = H // KVH
Q_WIDTH = H * HD
KV_WIDTH = 2 * KVH * HD

EPSILON = 1e-05
ROPE_BASE = 10000.0
MASKED_SCORE = -1e30
BF16 = jnp.bfloat16
F32 = jnp.float32
VMEM_LIMIT = 56 * 1024 * 1024
LANES = 128

START, CHIP, CORE, BATCH, LENGTHS = 0, 1, 2, 3, 4


def dot(a, b, a_dim=1, b_dim=0):
    return lax.dot_general(a, b, (((a_dim,), (b_dim,)), ((), ())), preferred_element_type=F32)


def rope_tables(positions):
    freqs = ROPE_BASE ** (-(jnp.arange(HD // 2, dtype=F32) * 2.0) / HD)
    phases = freqs[:, None] * positions[None, :]
    return jnp.cos(phases), jnp.sin(phases)


def rope(block, cos, sin):
    u1, u2 = block[: HD // 2], block[HD // 2 :]
    return jnp.concatenate([u1 * cos - u2 * sin, u2 * cos + u1 * sin], axis=0)


def rope_back(block, cos, sin):
    u1, u2 = block[: HD // 2], block[HD // 2 :]
    return jnp.concatenate([u1 * cos + u2 * sin, u2 * cos - u1 * sin], axis=0)


def rms_scale(vectors):
    return lax.rsqrt(jnp.mean(vectors * vectors, axis=0, keepdims=True) + EPSILON)


def norm_back(grad_normed, normed, inv_scale):
    return inv_scale * (
        grad_normed - normed * jnp.mean(grad_normed * normed, axis=0, keepdims=True)
    )


def clear(ref):
    ref[...] = jnp.zeros_like(ref)


def row_spec(shape, first=0):
    return pl.BlockSpec((1,) + shape, lambda r, info: (first + r, 0, 0))


def kv_spec(array):
    return pl.BlockSpec(
        (1,) + array.shape[1:], lambda r, info: (jnp.minimum(r, array.shape[0] - 1), 0, 0)
    )


def slot_spec(shape, rows, first=0):
    return pl.BlockSpec((1,) + shape, lambda r, info: (info[LENGTHS + rows + first + r], 0, 0))


def whole_spec(shape):
    return pl.BlockSpec(
        shape, lambda r, info: (0,) * len(shape), pipeline_mode=pl.Buffered(buffer_count=1)
    )


def shape_of(shape, dtype=BF16):
    return jax.ShapeDtypeStruct(shape, dtype)


def cost_of(microseconds):
    return pl.CostEstimate(
        flops=int(microseconds * 8e8), bytes_accessed=int(microseconds * 1e6), transcendentals=0
    )


def row_kernel_call(
    kernel, name, rows, in_specs, out_specs, out_shape, scratch=(), cost=None, aliases=None
):
    return pl.pallas_call(
        kernel,
        grid_spec=pltpu.PrefetchScalarGridSpec(
            num_scalar_prefetch=1,
            grid=(rows,),
            in_specs=in_specs,
            out_specs=out_specs,
            scratch_shapes=scratch,
        ),
        out_shape=out_shape,
        compiler_params=pltpu.CompilerParams(vmem_limit_bytes=VMEM_LIMIT),
        cost_estimate=cost,
        input_output_aliases=aliases or {},
        name=name,
    )


def row_used(info, first=0):
    length = info[LENGTHS + first + pl.program_id(0)]
    return length, info[START] < length


def qkv_kernel(info, x0_ref, x1_ref, gain_ref, w_query_ref, w_key_t_ref, w_value_t_ref, *refs):
    cos_ref, sin_ref, q_ref, *kv_refs = refs
    step = pl.program_id(0)
    used = info[START] < info[LENGTHS + CHUNK * step]
    size = x0_ref.shape[2]

    @pl.when(used)
    def _():
        x = jnp.concatenate([x0_ref[0].astype(F32), x1_ref[0].astype(F32)], axis=1)
        normed = (x * rms_scale(x) * gain_ref[...]).astype(BF16)
        cos = jnp.concatenate([cos_ref[...]] * 2, axis=1)
        sin = jnp.concatenate([sin_ref[...]] * 2, axis=1)
        out = dot(w_query_ref[...], normed, 0, 0)
        for h in range(H):
            at = slice(h * HD, (h + 1) * HD)
            block = (rope(out[at], cos, sin) * HD**-0.5).astype(BF16)
            q_ref[0, at, :] = block[:, :size]
            q_ref[1, at, :] = block[:, size:]
        out_key, out_value = dot(w_key_t_ref[...], normed), dot(w_value_t_ref[...], normed)
        parts = []
        for k in range(KVH):
            head = slice(k * HD, (k + 1) * HD)
            parts += [rope(out_key[head], cos, sin), out_value[head]]
        kv = jnp.concatenate(parts, axis=0).astype(BF16)
        for i, kv_ref in enumerate(kv_refs):

            @pl.when(step == i)
            def _():
                kv_ref[0] = kv[:, :size]
                kv_ref[1] = kv[:, size:]

    @pl.when(jnp.logical_not(used))
    def _():
        clear(q_ref)
        for i, kv_ref in enumerate(kv_refs):

            @pl.when(step == i)
            def _():
                clear(kv_ref)


def qkv_call(info, tokens, gain, weights, cos, sin):
    rows, width, length = tokens.shape
    chunks = rows // CHUNK

    def row_of_chunk(k):
        return pl.BlockSpec(
            (1, width, length), lambda r, info: (info[LENGTHS + rows + CHUNK * r + k], 0, 0)
        )

    queries, *kv = row_kernel_call(
        qkv_kernel,
        "qkv",
        chunks,
        [row_of_chunk(0), row_of_chunk(1)]
        + [whole_spec(a.shape) for a in (gain, *weights, cos, sin)],
        [pl.BlockSpec((CHUNK, Q_WIDTH, length), lambda r, info: (r, 0, 0))]
        + [whole_spec((CHUNK, KV_WIDTH, length))] * chunks,
        [shape_of((rows, Q_WIDTH, length))] + [shape_of((CHUNK, KV_WIDTH, length))] * chunks,
        cost=cost_of(1.2 * rows),
    )(info, tokens, tokens, gain, *weights, cos, sin)
    return queries, kv


def heads_of(ref, k):
    return jnp.concatenate(
        [ref[0, (k * GROUP + g) * HD : (k * GROUP + g + 1) * HD, :] for g in range(GROUP)], axis=1
    )


def key_value(kv_refs, block, k):
    ref, at = kv_refs[block], 2 * HD * k
    return ref[0, at : at + HD, :], ref[0, at + HD : at + 2 * HD, :]


def stack_spec(reach, length):
    return pl.BlockSpec((reach + 1, 1, KV_WIDTH, length), lambda r, info: (0, r, 0, 0))


def mask_diagonal(scores, start, length):
    size = scores.shape[0]
    key = lax.broadcasted_iota(jnp.int32, scores.shape, 0)
    query = lax.broadcasted_iota(jnp.int32, scores.shape, 1) % size
    allowed = jnp.logical_and(key <= query, start + key < length)
    return jnp.where(allowed, scores, MASKED_SCORE)


def visit_blocks(info, chips, visit):
    chip, core = info[CHIP], info[CORE]

    @pl.when(core == 0)
    def _():
        visit([(0, True)], True)

    @pl.when(core == 1)
    def _():
        visit([(0, True), (1, False)], True)

    for d in range(1, chips, 2):
        near = [(2 * d, False), (2 * d + 1, False)]

        if d + 1 < chips:

            @pl.when(chip > d)
            def _():
                visit(near + [(2 * d + 2, False), (2 * d + 3, False)], False)

        @pl.when((chip == d) if d + 1 < chips else (chip >= d))
        def _():
            visit(near, False)


def forward_kernel(chunk, info, q_ref, *refs):
    first_row, _, reach = chunk
    kv_refs = refs[: 2 * reach + 2]
    mixed_ref, lse_ref, peak_ref, total_ref, acc_ref = refs[-5:]
    length, used = row_used(info, first_row)
    start = info[START]

    def visit(blocks, first):
        def scores_of(k):
            queries = heads_of(q_ref, k)
            scores = []
            for b, diagonal in blocks:
                s = dot(key_value(kv_refs, b, k)[0], queries, 0, 0)
                scores.append(mask_diagonal(s, start, length) if diagonal else s)
            return scores

        ahead = [scores_of(k) for k in range(1)]
        for k in range(KVH):
            scores = ahead.pop(0)
            if k + 1 < KVH:
                ahead.append(scores_of(k + 1))
            peak = scores[0].max(axis=0, keepdims=True)
            for s in scores[1:]:
                peak = jnp.maximum(peak, s.max(axis=0, keepdims=True))
            if not first:
                old = peak_ref[k]
                peak = jnp.maximum(peak, old)
                shrink = jnp.exp(old - peak)
            total, acc = 0.0, 0.0
            for (b, _), s in zip(blocks, scores):
                weights = jnp.exp(s - peak)
                total = total + weights.sum(axis=0, keepdims=True)
                acc = acc + dot(key_value(kv_refs, b, k)[1], weights.astype(BF16))
            if not first:
                total = total + total_ref[k] * shrink
                acc = acc + acc_ref[k] * shrink
            peak_ref[k], total_ref[k], acc_ref[k] = peak, total, acc

    @pl.when(used)
    def _():
        visit_blocks(info, reach + 1, visit)
        size = q_ref.shape[2]
        for k in range(KVH):
            total = total_ref[k]
            out = (acc_ref[k] / total).astype(BF16)
            lse = peak_ref[k] + jnp.log(total)
            for g in range(GROUP):
                h = k * GROUP + g
                lse_ref[0, h : h + 1, :] = lse[:, g * size : (g + 1) * size]
                mixed_ref[0, h * HD : (h + 1) * HD, :] = out[:, g * size : (g + 1) * size]

    @pl.when(jnp.logical_not(used))
    def _():
        clear(mixed_ref)
        clear(lse_ref)


def forward_call(chunk, rows, info, queries, kv, mixed):
    first, count, reach = chunk
    length = queries.shape[2]
    earlier = [] if mixed is None else [mixed]
    return row_kernel_call(
        functools.partial(forward_kernel, chunk),
        "attention_forward",
        count,
        [row_spec((Q_WIDTH, length), first)]
        + [kv_spec(a) for a in kv]
        + [pl.BlockSpec(memory_space=pl.ANY)] * len(earlier),
        [row_spec((Q_WIDTH, length), first), row_spec((H, length))],
        [shape_of((rows, Q_WIDTH, length)), shape_of((count, H, length), F32)],
        [
            pltpu.VMEM((KVH, 1, GROUP * length), F32),
            pltpu.VMEM((KVH, 1, GROUP * length), F32),
            pltpu.VMEM((KVH, HD, GROUP * length), F32),
        ],
        aliases={2 + len(kv): 0} if earlier else None,
        cost=cost_of(2.5 * count),
    )(info, queries, *kv, *earlier)


def backward_kernel(chunk, info, q_ref, dmix_ref, mixed_ref, lse_ref, cos_ref, sin_ref, *refs):
    first_row, _, reach = chunk
    kv_refs = refs[: 2 * reach + 2]
    dq_ref, *dkv_refs = refs[-5:-2]
    inner_ref, dq_acc_ref = refs[-2:]
    length, used = row_used(info, first_row)
    start, chip, core = info[START], info[CHIP], info[CORE]
    size = q_ref.shape[2]

    def visit(blocks, first):
        def products(k, b, diagonal):
            keys, values = key_value(kv_refs, b, k)
            s = dot(keys, heads_of(q_ref, k), 0, 0)
            if diagonal:
                s = mask_diagonal(s, start, length)
            return s, dot(values, heads_of(dmix_ref, k), 0, 0)

        work = [(k, b, diagonal) for k in range(KVH) for b, diagonal in blocks]
        ahead = products(*work[0])
        for n, (k, b, _) in enumerate(work):
            (s, dprobs), ahead = ahead, products(*work[n + 1]) if n + 1 < len(work) else None
            queries, dmix = heads_of(q_ref, k), heads_of(dmix_ref, k)
            lse = jnp.concatenate(
                [lse_ref[0, k * GROUP + g : k * GROUP + g + 1, :] for g in range(GROUP)], axis=1
            )
            probs = jnp.exp(s - lse)
            dscores = (probs * (dprobs - inner_ref[k])).astype(BF16)
            dq = dot(key_value(kv_refs, b, k)[0], dscores)
            if first and b == blocks[0][0]:
                dq_acc_ref[k] = dq
            else:
                dq_acc_ref[k] += dq
            at, out = 2 * HD * k, dkv_refs[b % 2]
            out[b // 2, 0, at : at + HD, :] = dot(queries, dscores, 1, 1).astype(BF16)
            out[b // 2, 0, at + HD : at + 2 * HD, :] = dot(dmix, probs.astype(BF16), 1, 1).astype(
                BF16
            )

    @pl.when(used)
    def _():
        for k in range(KVH):
            parts = []
            for g in range(GROUP):
                at = slice((k * GROUP + g) * HD, (k * GROUP + g + 1) * HD)
                product = dmix_ref[0, at, :].astype(F32) * mixed_ref[0, at, :].astype(F32)
                parts.append(product.sum(axis=0, keepdims=True))
            inner_ref[k] = jnp.concatenate(parts, axis=1)
        visit_blocks(info, reach + 1, visit)
        cos, sin = cos_ref[...], sin_ref[...]
        for k in range(KVH):
            dq = dq_acc_ref[k] * HD**-0.5
            for g in range(GROUP):
                h = k * GROUP + g
                dq_ref[0, h * HD : (h + 1) * HD, :] = rope_back(
                    dq[:, g * size : (g + 1) * size], cos, sin
                ).astype(BF16)

    unused = jnp.logical_not(used)

    def clear_block(b):
        dkv_refs[b % 2][b // 2] = jnp.zeros(dkv_refs[b % 2].shape[1:], BF16)

    @pl.when(unused)
    def _():
        clear(dq_ref)
        clear_block(0)

    @pl.when(jnp.logical_or(unused, core == 0))
    def _():
        clear_block(1)

    for d in range(1, reach + 1):

        @pl.when(jnp.logical_or(unused, chip < d))
        def _():
            clear_block(2 * d)
            clear_block(2 * d + 1)


def backward_call(chunk, info, queries, dmix, mixed, lse, cos, sin, kv):
    first, count, reach = chunk
    length = dmix.shape[2]
    return row_kernel_call(
        functools.partial(backward_kernel, chunk),
        "attention_backward",
        count,
        [
            row_spec((Q_WIDTH, length), first),
            row_spec((Q_WIDTH, length), first),
            row_spec((Q_WIDTH, length), first),
            row_spec((H, length)),
            whole_spec(cos.shape),
            whole_spec(sin.shape),
        ]
        + [kv_spec(a) for a in kv],
        [row_spec((Q_WIDTH, length))] + [stack_spec(reach, length)] * 2,
        [shape_of((count, Q_WIDTH, length))]
        + [shape_of((reach + 1, count, KV_WIDTH, length))] * 2,
        [
            pltpu.VMEM((KVH, 1, GROUP * length), F32),
            pltpu.VMEM((KVH, HD, GROUP * length), F32),
        ],
        cost=cost_of(4 * count),
    )(info, queries, dmix, mixed, lse, cos, sin, *kv)


def write_halves(info, acc_refs, keep_ref, send_ref):
    at = 0
    for acc_ref in acc_refs:
        half, width = acc_ref.shape[0] // 2, acc_ref.shape[1]
        mine = pl.multiple_of(info[CORE] * half, 8)
        other = pl.multiple_of((1 - info[CORE]) * half, 8)
        keep_ref[:, at : at + width] = acc_ref[pl.ds(mine, half), :].astype(BF16)
        send_ref[:, at : at + width] = acc_ref[pl.ds(other, half), :].astype(BF16)
        at += width


def mlp_kernel(
    info,
    x_ref,
    mixed_ref,
    dy_ref,
    gain_ref,
    w_out_ref,
    w_gate_ref,
    w_up_ref,
    w_down_t_ref,
    out_ref,
    da_ref,
    dmix_ref,
    keep_ref,
    send_ref,
    grad_gain_ref,
    acc_ref,
    acc_out_ref,
    acc_gain_ref,
):
    length, used = row_used(info)
    row = pl.program_id(0)
    width, size = x_ref.shape[1:]
    hidden_width = w_gate_ref.shape[1]
    step = hidden_width // 2 if hidden_width % (2 * LANES) == 0 else hidden_width

    @pl.when(row == 0)
    def _():
        clear(acc_ref)
        clear(acc_out_ref)
        clear(acc_gain_ref)

    @pl.when(used)
    def _():
        mixed = mixed_ref[0]
        resid = x_ref[0].astype(F32) + dot(w_out_ref[...], mixed, 0, 0)
        scale = rms_scale(resid)
        normed = resid * scale
        mlp_in = (normed * gain_ref[...]).astype(BF16)
        position = info[START] + lax.broadcasted_iota(jnp.int32, (1, size), 1)
        valid = (position < length).astype(F32)
        dy_wide = dy_ref[0].astype(F32) * valid
        dy = dy_wide.astype(BF16)
        def products(at):
            part = slice(at, at + step)
            return (
                dot(w_gate_ref[:, part], mlp_in, 0, 0),
                dot(w_up_ref[:, part], mlp_in, 0, 0),
                dot(w_down_t_ref[:, part], dy, 0, 0),
            )

        out, grad_in = resid, None
        ahead = products(0)
        for at in range(0, hidden_width, step):
            part = slice(at, at + step)
            (gate, up, dhidden), ahead = ahead, None
            if at + step < hidden_width:
                ahead = products(at + step)
            sigmoid = 0.5 + 0.5 * jnp.tanh(0.5 * gate)
            activated = gate * sigmoid
            hidden = (activated * up).astype(BF16)
            dgate = (dhidden * up * (sigmoid + activated * (1.0 - sigmoid))).astype(BF16)
            dup = (dhidden * activated).astype(BF16)
            out = out + dot(w_down_t_ref[:, part], hidden)
            piece = dot(w_gate_ref[:, part], dgate) + dot(w_up_ref[:, part], dup)
            grad_in = piece if grad_in is None else grad_in + piece
            acc_ref[:, at : at + step] += dot(mlp_in, dgate, 1, 1)
            acc_ref[:, hidden_width + at : hidden_width + at + step] += dot(mlp_in, dup, 1, 1)
            acc_ref[:, 2 * hidden_width + at : 2 * hidden_width + at + step] += dot(
                dy, hidden, 1, 1
            )
        out_ref[0] = (out * valid).astype(BF16)
        acc_gain_ref[...] += grad_in * normed
        dresid = dy_wide + norm_back(grad_in * gain_ref[...], normed, scale)
        da = dresid.astype(BF16)
        da_ref[0] = da
        dmix_ref[0] = dot(w_out_ref[...], da).astype(BF16)
        acc_out_ref[...] += dot(mixed, da, 1, 1)

    @pl.when(jnp.logical_not(used))
    def _():
        clear(out_ref)
        clear(da_ref)
        clear(dmix_ref)

    @pl.when(row == pl.num_programs(0) - 1)
    def _():
        write_halves(info, [acc_ref, acc_out_ref], keep_ref, send_ref)
        grad_gain_ref[...] = jnp.broadcast_to(
            acc_gain_ref[...].sum(axis=1, keepdims=True), grad_gain_ref.shape
        )


def mlp_call(info, tokens, mixed, cotangent, gain, weights):
    rows, width, length = tokens.shape
    total = 3 * weights[1].shape[1]
    return row_kernel_call(
        mlp_kernel,
        "feed_forward",
        rows,
        [
            slot_spec((width, length), rows),
            row_spec((Q_WIDTH, length)),
            slot_spec((width, length), rows),
            whole_spec(gain.shape),
        ]
        + [whole_spec(w.shape) for w in weights],
        [
            slot_spec((width, length), rows),
            row_spec((width, length)),
            row_spec((Q_WIDTH, length)),
            whole_spec((width // 2, total + width)),
            whole_spec((width // 2, total + width)),
            whole_spec((width, LANES)),
        ],
        [
            shape_of((rows, width, length)),
            shape_of((rows, width, length)),
            shape_of((rows, Q_WIDTH, length)),
            shape_of((width // 2, total + width)),
            shape_of((width // 2, total + width)),
            shape_of((width, LANES), F32),
        ],
        [
            pltpu.VMEM((width, total), F32),
            pltpu.VMEM((Q_WIDTH, width), F32),
            pltpu.VMEM((width, length), F32),
        ],
        cost=cost_of(60),
    )(info, tokens, mixed, cotangent, gain, *weights)


def qkv_back_kernel(
    info,
    x_ref,
    da_ref,
    dq_ref,
    dkv_ref,
    gain_ref,
    w_query_ref,
    w_key_t_ref,
    w_value_t_ref,
    cos_ref,
    sin_ref,
    grad_gain_mlp_ref,
    dx_ref,
    keep_ref,
    send_ref,
    acc_ref,
    acc_gain_ref,
):
    _, used = row_used(info)
    row = pl.program_id(0)
    width = x_ref.shape[1]
    inner = Q_WIDTH + KV_WIDTH

    @pl.when(row == 0)
    def _():
        clear(acc_ref)
        clear(acc_gain_ref)

    @pl.when(used)
    def _():
        x = x_ref[0].astype(F32)
        scale = rms_scale(x)
        normed = x * scale
        attn_in = (normed * gain_ref[...]).astype(BF16)
        cos, sin = cos_ref[...], sin_ref[...]
        dq, dk, dv = dq_ref[0], [], []
        for k in range(KVH):
            at = 2 * HD * k
            dk.append(rope_back(dkv_ref[0, at : at + HD, :].astype(F32), cos, sin).astype(BF16))
            dv.append(dkv_ref[0, at + HD : at + 2 * HD, :])
        dk, dv = jnp.concatenate(dk, axis=0), jnp.concatenate(dv, axis=0)
        dn = dot(w_query_ref[...], dq)
        dn += dot(w_key_t_ref[...], dk, 0, 0) + dot(w_value_t_ref[...], dv, 0, 0)
        acc_ref[:, :Q_WIDTH] += dot(attn_in, dq, 1, 1)
        acc_ref[:, Q_WIDTH:inner] += dot(attn_in, jnp.concatenate([dk, dv], axis=0), 1, 1)
        acc_gain_ref[...] += dn * normed
        dx_ref[0] = (
            da_ref[0].astype(F32) + norm_back(dn * gain_ref[...], normed, scale)
        ).astype(BF16)

    @pl.when(jnp.logical_not(used))
    def _():
        clear(dx_ref)

    @pl.when(row == pl.num_programs(0) - 1)
    def _():
        lane = lax.broadcasted_iota(jnp.int32, (width, LANES), 1)
        acc_ref[:, inner:] = jnp.where(
            lane < LANES // 2,
            acc_gain_ref[...].sum(axis=1, keepdims=True),
            grad_gain_mlp_ref[...],
        )
        write_halves(info, [acc_ref], keep_ref, send_ref)


def qkv_back_call(info, tokens, da, dq, dkv, gain, weights, cos, sin, grad_gain_mlp):
    rows, width, length = tokens.shape
    total = Q_WIDTH + KV_WIDTH + LANES
    return row_kernel_call(
        qkv_back_kernel,
        "qkv_backward",
        rows,
        [
            slot_spec((width, length), rows),
            row_spec((width, length)),
            row_spec((Q_WIDTH, length)),
            row_spec((KV_WIDTH, length)),
        ]
        + [whole_spec(a.shape) for a in (gain, *weights, cos, sin, grad_gain_mlp)],
        [
            slot_spec((width, length), rows),
            whole_spec((width // 2, total)),
            whole_spec((width // 2, total)),
        ],
        [
            shape_of((rows, width, length)),
            shape_of((width // 2, total)),
            shape_of((width // 2, total)),
        ],
        [pltpu.VMEM((width, total), F32), pltpu.VMEM((width, length), F32)],
        cost=cost_of(14),
    )(info, tokens, da, dq, dkv, gain, *weights, cos, sin, grad_gain_mlp)


def exchange(array, axis, bits, low=1):
    size = lax.axis_size(axis)
    return lax.ppermute(array, axis, [(i, i ^ (bits * low)) for i in range(size)])


def add(*arrays):
    total = arrays[0].astype(F32)
    for array in arrays[1:]:
        total = total + array.astype(F32)
    return total.astype(BF16)


def place_of(axis, low):
    return lax.axis_index(axis) // low, lax.axis_size(axis) // low


def after(value, *others):
    return lax.optimization_barrier((value, others))[0]


class Sum:
    def __init__(self, keep, send, divided):
        self.keep, self.send, self.divided = keep, send, divided
        self.share = divided // (lax.axis_size("seq") // 2)
        self.steps = iter(
            [self.halve, self.over_batch, self.over_chips]
            + ([self.back_chips] if divided else [])
            + [self.back_batch, self.back_halves]
        )

    def begin(self):
        next(self.steps)()

    def end(self, *others):
        self.local = after(self.local, *others)
        self.array = self.finish(self.local, self.received)
        return self.array

    def arrived(self, number, *others):
        return after(self.received[number], *others)

    def added(self, local, received):
        return add(local, *received)

    def halve(self):
        self.local, self.received = self.keep, [exchange(self.send, "seq", 1)]
        self.finish = self.added

    def over_batch(self):
        me, count = place_of("batch", 1)
        share = self.array.shape[0] // count

        def part(index):
            return lax.dynamic_slice_in_dim(self.array, index * share, share, 0)

        self.received = [exchange(part(me ^ k), "batch", k) for k in range(1, count)]
        self.local, self.finish = part(me), self.added

    def over_chips(self):
        me, count = place_of("seq", 2)

        def part(index):
            if not self.divided:
                return self.array
            left = lax.dynamic_slice_in_dim(self.array, index * self.share, self.share, 1)
            return jnp.concatenate([left, self.array[:, self.divided :]], axis=1)

        self.received = [exchange(part(me ^ k), "seq", k, 2) for k in range(1, count)]
        self.local, self.finish = part(me), self.added

    def back_chips(self):
        _, count = place_of("seq", 2)
        left, right = self.array[:, : self.share], self.array[:, self.share :]
        self.received = [exchange(left, "seq", k, 2) for k in range(1, count)]
        self.local = left
        self.finish = lambda local, received: jnp.concatenate([local, *received, right], axis=1)

    def back_batch(self):
        _, count = place_of("batch", 1)
        self.received = [exchange(self.array, "batch", k) for k in range(1, count)]
        self.local = self.array
        self.finish = lambda local, received: jnp.stack([local, *received])

    def back_halves(self):
        self.local, self.received = self.array, exchange(self.array, "seq", 1)
        self.finish = lambda local, received: (local, received)


def select_core(info, mine_ref, other_ref, write):
    shares = pl.num_programs(0) // 2
    upper = (pl.program_id(0) >= shares).astype(jnp.int32)

    @pl.when(upper == info[CORE])
    def _():
        write(mine_ref)

    @pl.when(upper != info[CORE])
    def _():
        write(other_ref)


def share_specs(shape):
    shares = shape[0]
    rest = (0,) * (len(shape) - 1)

    def index(core, i, info):
        step = i - core * shares
        return (jnp.clip(step, 0, shares - 1) ^ info[BATCH],) + rest

    block = (1,) + tuple(shape[1:])
    return [
        pl.BlockSpec(block, lambda i, info: index(info[CORE], i, info)),
        pl.BlockSpec(block, lambda i, info: index(1 - info[CORE], i, info)),
    ]


def divided_kernel(chips, info, mine_ref, other_ref, *out_refs):
    out_width, rest = out_refs[0].shape[2], out_refs[-1].shape[2]
    width = (mine_ref.shape[2] - rest) // chips

    def write(ref):
        for q in range(chips):
            begin = pl.multiple_of((info[CHIP] ^ q) * width, LANES)
            share = ref[0, :, pl.ds(begin, width)].astype(F32)
            at = q * width
            while at < (q + 1) * width:
                out, column = divmod(at, out_width)
                size = min((q + 1) * width - at, out_width - column)
                begin = at - q * width
                out_refs[out][0, :, column : column + size] = share[:, begin : begin + size]
                at += size
        out_refs[-1][0] = ref[0, :, chips * width :].astype(F32)

    select_core(info, mine_ref, other_ref, write)


def divided_call(info, mine, other, chips, divided, count):
    shares, height, total = mine.shape
    widths = [divided // count] * count + [total - divided]
    out = row_kernel_call(
        functools.partial(divided_kernel, chips),
        "assemble_divided",
        2 * shares,
        share_specs(mine.shape),
        [pl.BlockSpec((1, height, w), lambda i, info: (i, 0, 0)) for w in widths],
        [shape_of((2 * shares, height, w), F32) for w in widths],
        cost=cost_of(8),
    )(info, mine, other)
    return [o.reshape(2 * shares * height, w) for o, w in zip(out, widths)]


def whole_kernel(info, mine_ref, other_ref, out_ref):
    def write(ref):
        out_ref[...] = ref[...].astype(F32)

    select_core(info, mine_ref, other_ref, write)


def whole_call(info, mine, other):
    shares, height, width = mine.shape
    out = row_kernel_call(
        whole_kernel,
        "assemble_whole",
        2 * shares,
        share_specs(mine.shape),
        pl.BlockSpec((1, height, width), lambda i, info: (i, 0, 0)),
        shape_of((2 * shares, height, width), F32),
        cost=cost_of(3),
    )(info, mine, other)
    return out.reshape(2 * shares * height, width)


def assemble_kernel(info, mine_ref, other_ref, query_ref, key_ref, value_ref, gain_ref, whole_ref):
    shares, height, _ = mine_ref.shape
    batch = info[BATCH]

    def write(half, ref):
        for j in range(shares):
            at = (half * shares + j) * height
            whole_ref[at : at + height, :] = ref[j ^ batch].astype(F32)

    @pl.when(info[CORE] == 0)
    def _():
        write(0, mine_ref)
        write(1, other_ref)

    @pl.when(info[CORE] == 1)
    def _():
        write(0, other_ref)
        write(1, mine_ref)

    query_ref[...] = whole_ref[:, :Q_WIDTH]
    rest = whole_ref[:, Q_WIDTH:].T
    key_ref[...] = rest[: KV_WIDTH // 2]
    value_ref[...] = rest[KV_WIDTH // 2 : KV_WIDTH]
    gain_ref[0:1, :] = rest[KV_WIDTH : KV_WIDTH + 1]
    gain_ref[1:2, :] = rest[KV_WIDTH + LANES // 2 : KV_WIDTH + LANES // 2 + 1]


def assemble_call(info, mine, other):
    shares, height, total = mine.shape
    width = 2 * shares * height
    shapes = [(width, Q_WIDTH), (KVH * HD, width), (KVH * HD, width), (2, width)]
    return row_kernel_call(
        assemble_kernel,
        "assemble",
        1,
        [whole_spec(mine.shape)] * 2,
        [whole_spec(shape) for shape in shapes],
        [shape_of(shape, F32) for shape in shapes],
        [pltpu.VMEM((width, total), F32)],
        cost=cost_of(5),
    )(info, mine, other)


def describe(lengths, start, place):
    rows = lengths.shape[0]
    index = jnp.arange(rows)
    ahead = (lengths[None, :] > lengths[:, None]) | (
        (lengths[None, :] == lengths[:, None]) & (index[None, :] < index[:, None])
    )
    rank = ahead.sum(axis=1)
    chosen = rank[None, :] == index[:, None]
    ordered = jnp.where(chosen, lengths[None, :], 0).sum(axis=1)
    slots = jnp.where(chosen, index[None, :], 0).sum(axis=1)
    return jnp.concatenate(
        [jnp.stack([start, place // 2, place % 2, lax.axis_index("batch")]), ordered, slots]
    ).astype(jnp.int32)


PLANS = ((4, 4, 4, 4, 3, 3, 2, 1), (4, 4, 4, 4, 4, 3, 3, 1), (4, 4, 4, 4, 4, 4, 4, 1))
CHUNK = 2


def plan_of(chips, quarters):
    reaches = [-(-chips * q // 4) - 1 for q in quarters]
    plan, counts = [], []
    for first in range(0, len(quarters), CHUNK):
        own = reaches[first : first + CHUNK]
        plan.append((first, CHUNK, own[0]))
        counts.append([sum(reach >= d for reach in own) for d in range(own[0] + 1)])
    return plan, counts


def plan_index(ordered, span):
    needed = -(-ordered * 4 // span)
    _, count = place_of("batch", 1)
    for other in [exchange(needed, "batch", k) for k in range(1, count)]:
        needed = jnp.maximum(needed, other)
    index = len(PLANS) - 1
    for i in reversed(range(len(PLANS) - 1)):
        index = jnp.where(jnp.all(needed <= jnp.array(PLANS[i], jnp.int32)), i, index)
    return index


def hops(low, high, way):
    return [(2 * c + k, 2 * (c + way) + k) for c in range(low, high + 1) for k in range(2)]


def layer(quarters, info, x, dy, tables, gain_columns, queries, keys, qkv_weights, mlp_weights):
    rows = x.shape[0]
    seq = lax.axis_size("seq")
    chips = seq // 2
    cos, sin = tables
    gain_column, gain_mlp_column = gain_columns
    plan, counts = plan_of(chips, quarters)

    moving = list(keys)
    moving = lax.optimization_barrier(moving)
    kv = [[own, exchange(own, "seq", 1)] for own in moving]

    def hop(i, d):
        if d <= plan[i][2]:
            moving[i] = lax.ppermute(
                moving[i][: counts[i][d]], "seq", hops(d - 1, plan[i][2] - 1, 1)
            )
            kv[i].append(moving[i])
            if (i, d) != (1, chips - 1):
                kv[i].append(exchange(moving[i], "seq", 1))

    for d in range(1, chips):
        hop(0, d)
        hop(1, d)
        if d == 1:
            moving[2:] = after(moving[2:], moving[1])
        hop(2, d)
        hop(3, d)
        if d == 2:
            moving[0] = after(moving[0], kv[2][:4], kv[3][:4])

    def forward(i, mixed, *others):
        q = after(queries, *others) if others else queries
        return forward_call(plan[i], rows, info, q, kv[i], mixed)

    lse = [None] * len(plan)
    mixed, lse[3] = forward(3, None)
    mixed, lse[0] = forward(0, mixed)
    moving[1] = after(moving[1], lse[0])
    kv[1][2 * chips - 2 :] = [moving[1], exchange(moving[1], "seq", 1)]
    mixed, lse[2] = forward(2, mixed)
    mixed, lse[1] = forward(1, mixed)

    layer_out, da, dmix, keep, send, grad_gain_mlp = mlp_call(
        info, x, mixed, dy, gain_mlp_column, mlp_weights
    )

    hidden_width = mlp_weights[1].shape[1]
    divided = 3 * hidden_width
    if divided % (chips * LANES):
        divided = 0
    sums = Sum(keep, send, divided)
    swaps, parts, flights, totals, dq = {}, {}, {}, {}, {}

    def backward(i, *others):
        l = after(lse[i], *others)
        dq[i], own, sibling = backward_call(plan[i], info, queries, dmix, mixed, l, cos, sin, kv[i])
        swaps[i] = (own, exchange(sibling, "seq", 1))
        return own

    def joined(i, *others):
        own, received = swaps.pop(i)
        parts[i] = add(after(own, *others), received)
        reach = plan[i][2]
        totals[i] = (reach, parts[i][reach][: counts[i][reach]])
        return parts[i]

    def send_back(i):
        d, total = totals[i]
        if d:
            flights[i] = lax.ppermute(total, "seq", hops(d, plan[i][2], -1))

    def received(i, *others):
        if i in flights:
            d, _ = totals[i]
            local = after(parts[i][d - 1][: counts[i][d - 1]], *others)
            more = counts[i][d - 1] - counts[i][d]
            total = add(local, jnp.pad(flights.pop(i), ((0, more), (0, 0), (0, 0))))
            totals[i] = (d - 1, total)
            return total
        return totals[i][1]

    sums.begin()
    now = backward(0)
    now = sums.end(now)
    sums.begin()
    now = backward(1, now)
    now = joined(0, now)
    send_back(0)
    now = sums.end(now)
    sums.begin()
    now = backward(2, now)
    now = joined(1, now)
    now = received(0, now)
    send_back(0)
    send_back(1)
    now = sums.end(now)
    if divided:
        sums.begin()
    now = backward(3, now)
    now = received(0, now)
    now = received(1, now)
    send_back(0)
    send_back(1)
    now = joined(2, now)
    now = joined(3, now)
    if divided:
        now = sums.end(now)
    sums.begin()
    send_back(2)
    send_back(3)
    while any(d for d, _ in totals.values()):
        for i in range(len(plan)):
            now = received(i, now)
            send_back(i)
    late_dq = jnp.concatenate([dq[i] for i in range(len(plan))], axis=0)
    late_dkv = jnp.concatenate([totals[i][1] for i in range(len(plan))], axis=0)
    now = sums.end(late_dkv)
    sums.begin()
    late_dkv = after(late_dkv, now)
    dx, keep, send = qkv_back_call(
        info, x, da, late_dq, late_dkv, gain_column, qkv_weights, cos, sin, grad_gain_mlp
    )
    late = Sum(keep, send, 0)
    late.begin()
    now = late.end()
    pair = sums.end(now)
    late.begin()
    now = late.end(now)
    late.begin()
    pair = after(pair, now)
    if divided:
        grads = divided_call(info, *pair, chips, divided, 3)
    else:
        ends = [hidden_width, 2 * hidden_width, 3 * hidden_width]
        grads = jnp.split(whole_call(info, *pair), ends, axis=1)
    late.end(*grads)
    late.begin()
    late.end()
    late.begin()
    grad_gate, grad_up, grad_down, grad_out = grads
    grad_query, grad_key, grad_value, gains = assemble_call(info, *late.end())

    return (
        layer_out,
        dx,
        gains[0],
        grad_query,
        grad_key.T,
        grad_value.T,
        grad_out,
        gains[1],
        grad_gate,
        grad_up,
        grad_down.T,
    )


def body(
    tokens,
    lengths,
    gain_attn,
    w_query,
    w_key,
    w_value,
    w_out,
    gain_mlp,
    w_gate,
    w_up,
    w_down,
    cotangent,
):
    rows, local_len, _ = tokens.shape
    seq = lax.axis_size("seq")
    place = lax.axis_index("seq")
    start = place * local_len
    tables = rope_tables((start + jnp.arange(local_len, dtype=jnp.int32)).astype(F32))
    info = describe(lengths, start, place)
    qkv_weights = [w_query, w_key.T, w_value.T]
    x = jnp.swapaxes(tokens, 1, 2)
    dy = jnp.swapaxes(cotangent, 1, 2)
    gains = gain_attn[:, None], gain_mlp[:, None]
    index = plan_index(info[LENGTHS : LENGTHS + rows], seq * local_len)
    queries, keys = qkv_call(info, x, gains[0], qkv_weights, *tables)
    layer_out, dx, *grads = lax.switch(
        index,
        [functools.partial(layer, plan) for plan in PLANS],
        info,
        x,
        dy,
        tables,
        gains,
        queries,
        keys,
        qkv_weights,
        [w_out, w_gate, w_up, w_down.T],
    )
    return jnp.swapaxes(layer_out, 1, 2), jnp.swapaxes(dx, 1, 2), *grads


def solution(mesh):
    split, copied = P("batch", "seq", None), P()
    in_specs = (split, P("batch")) + (copied,) * 9 + (split,)
    out_specs = (split, split) + (copied,) * 9
    return jax.shard_map(body, mesh=mesh, in_specs=in_specs, out_specs=out_specs, check_vma=False)
```
